256 devices in a mesh: ens: 8 (over z_hi, x), space: 32 (over y, z_lo, core).
Axes of the slice: x: 4, y: 4, z: 8 (z_hi: 2, z_lo: 4; z = z_hi * 4 + z_lo), core: 2. Of those that a mesh axis runs over, the one named last changes fastest.
Arguments:
- mesh_feats: bfloat16 [8, 2048, 1024], P('ens', 'space'), may hold values from -6 to 6
- grid_embed: bfloat16 [16384, 1024], P('space'), may hold values from -6 to 6
- w_src: bfloat16 [1024, 1024], replicated, may hold values from -0.1875 to 0.1875
- w_dst: bfloat16 [1024, 1024], replicated, may hold values from -0.1875 to 0.1875
- w_out: bfloat16 [1024, 32], replicated, may hold values from -0.1875 to 0.1875
- truth: float32 [16384, 32], P('space'), may hold values from -6 to 6
- area_weight: float32 [16384], P('space'), may hold values from 0.3 to 3
- var_weight: float32 [32], replicated, may hold values from 0.5 to 2
- neighbour: int32 [16384, 16], P('space'), may hold values from 0 to 2047, as said below
- edge_mask: int32 [16384, 16], P('space'), may hold values from 0 to 1, as said below
Outputs:
- grad_mesh: bfloat16 [8, 2048, 1024], P('ens', 'space')
- grad_w_src: float32 [1024, 1024], P(('ens', 'space'))
- grad_w_dst: float32 [1024, 1024], P(('ens', 'space'))
- grad_w_out: float32 [1024, 32], P(('ens', 'space'))
The draws below stay inside these ranges and needn't reach their ends.
Inputs may be any that keep to these rules, and one draw needn't show every extreme that they name: `neighbour`: A grid point g in block b = g // 512 names only mesh nodes of blocks b-1, b and b+1 of 64 nodes each, counted cyclically over the 2048 nodes. `edge_mask`: the first slot of every grid point is used.
All inputs are finite; a program needn't handle non-finite values.
Results may differ from the reference program's by a relative error of at most 0.008.
Values may be sent and summed in bfloat16 or wider, within the bound.
No kernel may reach another device: no remote copies, remote signals or barrier semaphores. Data moves between devices by JAX's collectives and lax.ppermute only.
A program may use at most 128 MiB of HBM per device.

```python
import math
import jax
import jax.numpy as jnp
from jax import lax

H = 1024
VARS = 32
DEG = 16
GRID_DEV = 512
MESH_DEV = 64
MEMBERS = 8
GRID = 16384
MESH = 2048
N_SPACE = 32


def draw_neighbour(key, part):
    key = jax.random.fold_in(key, 11)
    offsets = jax.random.randint(key, (GRID, DEG), 0, 3 * MESH_DEV)
    block = (jnp.arange(GRID, dtype=jnp.int32) // GRID_DEV)[:, None]
    return jnp.mod((block - 1) * MESH_DEV + offsets, MESH).astype(jnp.int32)


def draw_edge_mask(key, part):
    key = jax.random.fold_in(key, 12)
    levels = jax.random.randint(key, (GRID, DEG), 0, 4)
    column = jnp.arange(DEG, dtype=jnp.int32)[None, :]
    return jnp.where(column == 0, 1, jnp.where(levels > 0, 1, 0)).astype(jnp.int32)


def spiked(entries, stream_key, source, target, blocks, factor):
    owner, partner = [(jnp.arange(entries.shape[dim]) // (entries.shape[dim] // blocks)).reshape([-1 if axis == dim else 1 for axis in range(entries.ndim)]) for dim in (source, target)]
    chosen = jax.random.permutation(stream_key, blocks)[partner]
    strong = (owner == chosen) | (owner == (partner + blocks // 2) % blocks)
    return jnp.where(strong, factor * entries, entries)


def shard_levels(key, dims, shards, smallest, top_value):
    gain = 1.0
    for dim, blocks in shards:
        steps = jax.random.uniform(jax.random.fold_in(jax.random.fold_in(key, 6), dim), (blocks,), jnp.float32, smallest / len(shards), top_value / len(shards))
        gain = gain * jnp.repeat(jnp.exp(steps), dims[dim] // blocks).reshape((-1,) + (1,) * (len(dims) - 1 - dim))
    return gain


def scatter_about(rng, extent, width, most, shards=(), held_as=jnp.bfloat16):
    result = jax.random.normal(rng, extent, jnp.float32) * width
    if len(shards) > 0:
        result = shard_levels(rng, extent, shards, -0.22, 0.18) * result
    return jnp.clip(result, min=-most, max=most).astype(held_as)


def noise_with(own_key, extent, scale, reach, pieces, heavy, held_as=jnp.bfloat16):
    drawn = scale * jax.random.normal(own_key, extent, jnp.float32)
    if pieces:
        drawn = drawn * shard_levels(own_key, extent, pieces, -0.22, 0.18)
    return jnp.clip(spiked(drawn, jax.random.fold_in(own_key, 3), *heavy), -reach, reach).astype(held_as)


def setup_inputs(seed: int = 0) -> dict:
    splits = jax.random.split(jax.random.key(seed), 11)
    mesh_feats = noise_with(splits[0], (MEMBERS, MESH, H), 1.0, 6.0, ((0, 8), (1, 32)), (1, 2, 32, 2.75))
    grid_embed = noise_with(splits[1], (GRID, H), 1.0, 6.0, ((0, 32),), (0, 1, 32, 2.75))
    w_src = scatter_about(splits[2], (H, H), H ** -0.5, 0.1875)
    w_dst = scatter_about(splits[3], (H, H), H ** -0.5, 0.1875)
    w_out = scatter_about(splits[4], (H, VARS), H ** -0.5, 0.1875)
    truth = scatter_about(splits[5], (GRID, VARS), 1.0, 6.0, ((0, 32),), jnp.float32)
    area_weight = jnp.clip(jnp.exp(math.log(3.0) - 2.3025851 * jax.random.uniform(splits[6], (GRID,), jnp.float32) ** shard_levels(splits[6], (GRID,), ((0, 32),), -0.2, 0.2)), 0.3, 3.0)
    var_weight = jnp.clip(jnp.exp(jax.random.uniform(splits[7], (VARS,), jnp.float32, math.log(0.5), math.log(2.0))), 0.5, 2.0)
    neighbour = draw_neighbour(jax.random.fold_in(splits[10], 71), 0)
    edge_mask = draw_edge_mask(jax.random.fold_in(splits[10], 71), 0)
    return dict(mesh_feats=mesh_feats, grid_embed=grid_embed, w_src=w_src, w_dst=w_dst, w_out=w_out, truth=truth, area_weight=area_weight, var_weight=var_weight, neighbour=neighbour, edge_mask=edge_mask)


loss_scale = 8.0
smooth_sq = 0.01

def gelu(v):
    return 0.5 * v * (1.0 + jnp.tanh(0.7978845608 * (v + 0.044715 * v * v * v)))

def gelu_grad(v):
    inner = 0.7978845608 * (v + 0.044715 * v * v * v)
    tval = jnp.tanh(inner)
    return 0.5 * (1.0 + tval) + 0.5 * v * (1.0 - tval * tval) * 0.7978845608 * (1.0 + 3.0 * 0.044715 * v * v)

def smooth_grad(diff):
    return diff / jnp.sqrt(diff * diff + smooth_sq)

def reference(mesh_feats, grid_embed, w_src, w_dst, w_out, truth, area_weight, var_weight, neighbour, edge_mask):
    f32 = jnp.float32
    members = mesh_feats.shape[0]
    proj = jnp.einsum('emh,hk->emk', mesh_feats.astype(f32), w_src.astype(f32)).astype(jnp.bfloat16)
    dst = jnp.dot(grid_embed, w_dst, preferred_element_type=f32)
    blocks = N_SPACE
    items = (neighbour.reshape(blocks, GRID_DEV, DEG), edge_mask.reshape(blocks, GRID_DEV, DEG), dst.reshape(blocks, GRID_DEV, H), truth.reshape(blocks, GRID_DEV, VARS), area_weight.reshape(blocks, GRID_DEV))

    def step(carry, item):
        nbr, mask, dstb, truthb, areab = item
        pre = proj[:, nbr].astype(f32) + dstb[None, :, None, :]
        maskf = mask.astype(f32)
        deg = lax.optimization_barrier(jnp.sum(maskf, axis=1))
        wgt = maskf / deg[:, None]
        agg = lax.optimization_barrier(jnp.sum(gelu(pre) * wgt[None, :, :, None], axis=2)).astype(jnp.bfloat16)
        pred = jnp.einsum('ebh,hv->ebv', agg.astype(f32), w_out.astype(f32))
        pair = lax.optimization_barrier(jnp.sum(smooth_grad(pred[:, None] - pred[None, :]), axis=1))
        dpred = (loss_scale * areab[None, :, None] * var_weight[None, None, :] * (smooth_grad(pred - truthb[None]) / members - pair / (members * (members - 1)))).astype(jnp.bfloat16)
        dagg = jnp.einsum('ebv,hv->ebh', dpred.astype(f32), w_out.astype(f32))
        dpre = (gelu_grad(pre) * wgt[None, :, :, None] * dagg[:, :, None, :]).astype(jnp.bfloat16)
        ddst = lax.optimization_barrier(jnp.sum(dpre.astype(f32), axis=2)).astype(jnp.bfloat16)
        flat = nbr.reshape(-1).astype(jnp.int32)
        add = jax.vmap(lambda d: jax.ops.segment_sum(d.reshape(-1, H).astype(f32), flat, num_segments=MESH))(dpre)
        return (carry + add, (agg, dpred, ddst))
    dproj, (agg, dpred, ddst) = lax.scan(step, jnp.zeros((members, MESH, H), f32), items)
    agg = jnp.transpose(agg, (1, 0, 2, 3)).reshape(members, GRID, H)
    dpred = jnp.transpose(dpred, (1, 0, 2, 3)).reshape(members, GRID, VARS)
    ddst = jnp.transpose(ddst, (1, 0, 2, 3)).reshape(members, GRID, H)
    dproj_b = dproj.astype(jnp.bfloat16)
    grad_mesh = jnp.einsum('emk,hk->emh', dproj_b.astype(f32), w_src.astype(f32)).astype(jnp.bfloat16)
    grad_w_src = jnp.einsum('emh,emk->hk', mesh_feats.astype(f32), dproj_b.astype(f32))
    grad_w_dst = jnp.einsum('gh,egk->hk', grid_embed.astype(f32), ddst.astype(f32))
    grad_w_out = jnp.einsum('egh,egv->hv', agg.astype(f32), dpred.astype(f32))
    return (grad_mesh, grad_w_src, grad_w_dst, grad_w_out)
```

```python
import functools
import jax
import jax.numpy as jnp
from jax import lax
from jax.experimental import pallas as pl
from jax.experimental.pallas import tpu as pltpu
from jax.sharding import Mesh, PartitionSpec as P

loss_scale = 8.0
smooth_sq = 0.01
TILE = 64
LANES = 128
NCOL = 256
f32 = jnp.float32
bf16 = jnp.bfloat16
SPACE = ("y", "zl", "c")
ENS = ("zh", "x")
LATE = ("zh", "y", "zl")


def shifted(block, axes, distance):
    count = lax.axis_size(axes)
    return lax.ppermute(block, axes, [(i, (i + distance) % count) for i in range(count)])


def smooth_grad(diff):
    return diff / jnp.sqrt(diff * diff + smooth_sq)


def gelu_parts(v):
    c0 = 0.7978845608
    c1 = c0 * 0.044715
    sq = v * v
    inner = v * (c0 + c1 * sq)
    t = jnp.tanh(inner)
    u = 1.0 + t
    slope = v * (c0 + (3.0 * c1) * sq)
    return v * u, u * (1.0 + (1.0 - t) * slope)


def forward_kernel(slots, wide_ref, dst_ref, idx_ref, scale_ref, gp_ref, agg_ref, sum_ref, rhs, hot, pre):
    nodes = wide_ref.shape[0]
    tile = dst_ref.shape[0]
    width = dst_ref.shape[1]
    depth = rhs.shape[0]

    @pl.when(pl.program_id(0) == 0)
    def _():
        rhs[:nodes, :] = wide_ref[...]

    rhs[nodes:, :] = dst_ref[...]
    lane = lax.broadcasted_iota(jnp.int32, (tile, depth), 1)
    row = lax.broadcasted_iota(jnp.int32, (tile, depth), 0)
    eye = lane == row + nodes
    for k in range(slots):
        col = idx_ref[:, k : k + 1]
        hit = (lane == col) | (eye & (col >= 0))
        hot[k * tile : (k + 1) * tile, :] = jnp.where(hit, 1.0, 0.0).astype(bf16)
    scale = scale_ref[...]
    for n in range(width // NCOL):
        pre[n % 2] = jnp.dot(
            hot[...], rhs[:, n * NCOL : (n + 1) * NCOL], preferred_element_type=f32
        )
        for half in range(NCOL // LANES):
            here = slice(half * LANES, (half + 1) * LANES)
            cols = slice(n * NCOL + half * LANES, n * NCOL + (half + 1) * LANES)
            acc_g = jnp.zeros((tile, LANES), f32)
            acc_s = jnp.zeros((tile, LANES), f32)
            for k in range(slots):
                rows = slice(k * tile, (k + 1) * tile)
                value, grad = gelu_parts(pre[n % 2, rows, here])
                acc_g = acc_g + value
                acc_s = acc_s + jnp.where(idx_ref[:, k : k + 1] >= 0, grad, 0.0)
                gp_ref[rows, cols] = grad.astype(bf16)
            agg_ref[:, cols] = (acc_g * scale).astype(bf16)
            sum_ref[:, cols] = acc_s.astype(bf16)


def forward(wide, dst, idx, scale):
    grid_rows, width = dst.shape
    nodes = wide.shape[0]
    slots = idx.shape[1]
    tiles = grid_rows // TILE
    whole = lambda t: (0, 0)
    step = lambda t: (t, 0)
    return pl.pallas_call(
        functools.partial(forward_kernel, slots),
        grid=(tiles,),
        in_specs=[
            pl.BlockSpec((nodes, width), whole),
            pl.BlockSpec((TILE, width), step),
            pl.BlockSpec((TILE, slots), step),
            pl.BlockSpec((TILE, 1), step),
        ],
        out_specs=[
            pl.BlockSpec((TILE * slots, width), step),
            pl.BlockSpec((TILE, width), step),
            pl.BlockSpec((TILE, width), step),
        ],
        out_shape=[
            jax.ShapeDtypeStruct((grid_rows * slots, width), bf16),
            jax.ShapeDtypeStruct((grid_rows, width), bf16),
            jax.ShapeDtypeStruct((grid_rows, width), bf16),
        ],
        scratch_shapes=[
            pltpu.VMEM((nodes + TILE, width), bf16),
            pltpu.VMEM((TILE * slots, nodes + TILE), bf16),
            pltpu.VMEM((2, TILE * slots, NCOL), f32),
        ],
        compiler_params=pltpu.CompilerParams(vmem_limit_bytes=40 * 1024 * 1024),
        cost_estimate=pl.CostEstimate(
            flops=2 * grid_rows * slots * 256 * width,
            bytes_accessed=2 * grid_rows * slots * width,
            transcendentals=grid_rows * slots * width,
        ),
    )(wide, dst, idx, scale)


def backward_kernel(slots, gp_ref, sum_ref, dpred_ref, wout_ref, scale_ref, idx_ref, out_ref, lead, prod, acc):
    step = pl.program_id(0)
    nodes = acc.shape[0]
    tile = gp_ref.shape[0] // slots
    width = gp_ref.shape[1]

    @pl.when(step == 0)
    def _():
        for n in range(width // NCOL):
            cols = slice(n * NCOL, (n + 1) * NCOL)
            dagg = lax.dot_general(
                dpred_ref[...], wout_ref[:, cols], (((0,), (0,)), ((), ())), preferred_element_type=f32
            )
            dagg = dagg * scale_ref[...]
            lead[:, cols] = dagg.astype(bf16)
            out_ref[nodes:, cols] = (dagg * sum_ref[:, cols].astype(f32)).astype(bf16)
        acc[...] = jnp.zeros_like(acc)

    node = lax.broadcasted_iota(jnp.int32, (nodes, tile * slots), 0)
    hot = jnp.where(node == idx_ref[0], 1.0, 0.0).astype(bf16)
    here = pl.ds(pl.multiple_of(step * tile, tile), tile)
    for k in range(slots):
        rows = slice(k * tile, (k + 1) * tile)
        prod[rows, :] = gp_ref[rows, :] * lead[here, :]
    for n in range(width // NCOL):
        cols = slice(n * NCOL, (n + 1) * NCOL)
        acc[:, cols] += jnp.dot(hot, prod[:, cols], preferred_element_type=f32)

    @pl.when(step == pl.num_programs(0) - 1)
    def _():
        out_ref[:nodes, :] = acc[...].astype(bf16)


def backward(gp, sums, dpred_t, wout_t, scale, idx_rows, nodes):
    grid_rows, width = sums.shape
    slots = gp.shape[0] // grid_rows
    tiles = grid_rows // TILE
    whole = lambda t: (0, 0)
    return pl.pallas_call(
        functools.partial(backward_kernel, slots),
        grid=(tiles,),
        in_specs=[
            pl.BlockSpec((TILE * slots, width), lambda t: (t, 0)),
            pl.BlockSpec((grid_rows, width), whole),
            pl.BlockSpec(dpred_t.shape, whole),
            pl.BlockSpec(wout_t.shape, whole),
            pl.BlockSpec((grid_rows, 1), whole),
            pl.BlockSpec((1, 1, TILE * slots), lambda t: (t, 0, 0)),
        ],
        out_specs=pl.BlockSpec((nodes + grid_rows, width), whole),
        out_shape=jax.ShapeDtypeStruct((nodes + grid_rows, width), bf16),
        scratch_shapes=[
            pltpu.VMEM((grid_rows, width), bf16),
            pltpu.VMEM((TILE * slots, width), bf16),
            pltpu.VMEM((nodes, width), f32),
        ],
        compiler_params=pltpu.CompilerParams(vmem_limit_bytes=40 * 1024 * 1024),
        cost_estimate=pl.CostEstimate(
            flops=2 * grid_rows * slots * 256 * width,
            bytes_accessed=2 * grid_rows * slots * width,
            transcendentals=0,
        ),
    )(gp, sums, dpred_t, wout_t, scale, idx_rows)


def contract_first(left, right):
    return lax.dot_general(left, right, (((0,), (0,)), ((), ())), preferred_element_type=f32)


def body(
    mesh_feats,
    grid_embed,
    w_src,
    w_dst,
    w_out,
    truth,
    area_weight,
    var_weight,
    neighbour,
    edge_mask,
):
    own = mesh_feats[0]
    node_rows, width = own.shape
    grid_rows, slots = neighbour.shape
    nodes = 3 * node_rows
    tiles = grid_rows // TILE
    space_count = lax.axis_size(SPACE)
    block_id = lax.axis_index(SPACE)
    members = lax.axis_size(ENS)
    swap = [(0, 1), (1, 0)]
    core = lax.axis_index("c")

    below = shifted(own, SPACE, 1)
    above = shifted(own, SPACE, -1)
    feats = jnp.concatenate([below, own, above], axis=0)

    h = jnp.arange(width, dtype=jnp.int32)
    half = width // 2
    source = (h % half // 4) * 8 + (h // half) * 4 + h % 4
    order = (h[:, None] == source[None, :]).astype(bf16)

    dst = jnp.dot(grid_embed, w_dst, preferred_element_type=f32).astype(bf16)
    local = jnp.mod(neighbour - (block_id - 1) * node_rows, node_rows * space_count)
    idx = jnp.where(edge_mask > 0, local, -1)
    idx_rows = idx.reshape(tiles, TILE, slots).transpose(0, 2, 1).reshape(tiles, 1, slots * TILE)
    scale = 0.5 / jnp.sum(edge_mask.astype(f32), axis=1, keepdims=True)
    wide = jnp.dot(feats, w_src, preferred_element_type=f32).astype(bf16)

    left = jnp.concatenate([feats, grid_embed], axis=0)
    left = jnp.dot(left, order, preferred_element_type=f32).astype(bf16)
    left = left.reshape(left.shape[0], 2, half)
    left_own = lax.dynamic_index_in_dim(left, core, 1, keepdims=False)
    left_far = lax.ppermute(lax.dynamic_index_in_dim(left, 1 - core, 1, keepdims=False), "c", swap)

    gp, agg, sums = forward(wide, dst, idx, scale)

    pred = lax.dot_general(w_out, agg, (((0,), (1,)), ((), ())), preferred_element_type=f32)
    everyone = lax.all_to_all(
        jnp.broadcast_to(pred[None], (members,) + pred.shape), ENS, 0, 0, tiled=True
    )
    pair = jnp.sum(smooth_grad(pred[None] - everyone), axis=0)
    weighting = loss_scale * area_weight[None, :] * var_weight[:, None]
    dpred = (
        weighting * (smooth_grad(pred - truth.T) / members - pair / (members * (members - 1)))
    ).astype(bf16)

    right_own = backward(gp, sums, dpred, w_out.T, scale, idx_rows, nodes)
    right_far = lax.ppermute(right_own, "c", swap)

    from_above = shifted(right_own[:node_rows], SPACE, -1)
    from_below = shifted(right_own[2 * node_rows : nodes], SPACE, 1)
    dproj = (
        right_own[node_rows : 2 * node_rows].astype(f32)
        + from_above.astype(f32)
        + from_below.astype(f32)
    ).astype(bf16)
    grad_mesh = lax.dot_general(
        dproj, w_src, (((1,), (1,)), ((), ())), preferred_element_type=f32
    ).astype(bf16)

    out_part = jnp.dot(dpred, agg, preferred_element_type=f32).astype(bf16)
    out_part = jnp.dot(out_part, order, preferred_element_type=f32).T.reshape(2, half, -1)
    out_own = lax.dynamic_index_in_dim(out_part, core, 0, keepdims=False)
    out_far = lax.ppermute(
        lax.dynamic_index_in_dim(out_part, 1 - core, 0, keepdims=False).astype(bf16), "c", swap
    )
    total = jnp.concatenate(
        [
            contract_first(left_own[:nodes], right_own[:nodes])
            + contract_first(left_far[:nodes], right_far[:nodes]),
            contract_first(left_own[nodes:], right_own[nodes:])
            + contract_first(left_far[nodes:], right_far[nodes:]),
            out_own + out_far.astype(f32),
        ],
        axis=1,
    )
    columns = total.shape[1]
    total = total.reshape(2, lax.axis_size("x"), -1, columns)
    along = lax.axis_index("x")
    total_x = lax.dynamic_index_in_dim(total, along, 1, keepdims=False)
    count = lax.axis_size("x")
    for d in (1, 3, 2):
        piece = lax.dynamic_index_in_dim(total, (along + d) % count, 1, keepdims=False)
        total_x = total_x + shifted(piece.astype(bf16), "x", d).astype(f32)
    pieces = lax.all_to_all(total_x.reshape(-1, columns).astype(bf16), LATE, 0, 0, tiled=True)
    total = jnp.sum(pieces.reshape(lax.axis_size(LATE), -1, columns).astype(f32), axis=0)
    return (
        grad_mesh[None],
        total[:, :width],
        total[:, width : 2 * width],
        total[:, 2 * width :],
    )


def solution(mesh):
    fine = Mesh(mesh.devices.reshape(2, 4, 4, 4, 2), ("zh", "x", "y", "zl", "c"))
    everywhere = ENS + SPACE
    in_specs = (
        P(ENS, SPACE, None),
        P(SPACE, None),
        P(),
        P(),
        P(),
        P(SPACE, None),
        P(SPACE),
        P(),
        P(SPACE, None),
        P(SPACE, None),
    )
    out_specs = (
        P(ENS, SPACE, None),
        P(everywhere, None),
        P(everywhere, None),
        P(everywhere, None),
    )
    return jax.shard_map(body, mesh=fine, in_specs=in_specs, out_specs=out_specs, check_vma=False)
```

```python
import functools
import jax
import jax.numpy as jnp
from jax import lax
from jax.experimental import pallas as pl
from jax.experimental.pallas import tpu as pltpu
from jax.sharding import Mesh, PartitionSpec as P

loss_scale = 8.0
smooth_sq = 0.01
TILE = 64
NCOL = 256
ROWS = 32
GROUP = 4
VMEM_LIMIT = 56 * 1024 * 1024
f32 = jnp.float32
bf16 = jnp.bfloat16
SPACE = ("y", "zl", "c")
ENS = ("zh", "x")
LATE = ("zh", "y", "zl", "c")


def shifted(block, axes, distance):
    count = lax.axis_size(axes)
    return lax.ppermute(block, axes, [(i, (i + distance) % count) for i in range(count)])


def smooth_grad(diff):
    return diff / jnp.sqrt(diff * diff + smooth_sq)


def gelu_parts(v):
    c0 = 0.7978845608
    c1 = c0 * 0.044715
    sq = v * v
    t = jnp.tanh(v * (c0 + c1 * sq))
    u = 1.0 + t
    slope = v * (c0 + (3.0 * c1) * sq)
    return v * u, u * (1.0 + (1.0 - t) * slope)


def forward_kernel(
    slots, wide_ref, dst_ref, idx_ref, scale_ref, wout_ref, gp_ref, agg_ref, sum_ref, pred_ref, rhs, hot, pre
):
    step = pl.program_id(0)
    nodes = wide_ref.shape[0]
    tile, width = dst_ref.shape
    depth = rhs.shape[0]

    @pl.when(step == 0)
    def _():
        rhs[:nodes, :] = wide_ref[...]

    rhs[nodes:, :] = dst_ref[...]
    lane = lax.broadcasted_iota(jnp.int32, (tile, depth), 1)
    row = lax.broadcasted_iota(jnp.int32, (tile, depth), 0)
    eye = lane == row + nodes
    for k in range(slots):
        col = idx_ref[:, k : k + 1]
        hit = (lane == col) | (eye & (col >= 0))
        hot[k * tile : (k + 1) * tile, :] = jnp.where(hit, 1.0, 0.0).astype(bf16)
    for n in range(width // NCOL):
        cols = slice(n * NCOL, (n + 1) * NCOL)
        pre[n % 2] = jnp.dot(hot[...], rhs[:, cols], preferred_element_type=f32).astype(bf16)
        for r in range(0, tile, ROWS):
            acc_g = jnp.zeros((ROWS, NCOL), f32)
            acc_s = jnp.zeros((ROWS, NCOL), f32)
            for k in range(slots):
                rows = slice(k * tile + r, k * tile + r + ROWS)
                value, grad = gelu_parts(pre[n % 2, rows, :])
                gp_ref[rows, cols] = grad
                if k % GROUP == 0:
                    some_g, some_s = value, grad
                else:
                    some_g, some_s = some_g + value, some_s + grad
                if k % GROUP == GROUP - 1:
                    acc_g = acc_g + some_g.astype(f32)
                    acc_s = acc_s + some_s.astype(f32)
            scale = scale_ref[r : r + ROWS, :]
            here = pl.ds(pl.multiple_of(step * tile + r, ROWS), ROWS)
            agg_ref[here, cols] = (acc_g * scale).astype(bf16)
            sum_ref[r : r + ROWS, cols] = (acc_s - (slots - 0.5 / scale)).astype(bf16)

    @pl.when(step == pl.num_programs(0) - 1)
    def _():
        pred_ref[...] = lax.dot_general(
            wout_ref[...], agg_ref[...], (((1,), (1,)), ((), ())), preferred_element_type=f32
        )


def forward(wide, dst, idx, scale, wout_t):
    grid_rows, width = dst.shape
    nodes = wide.shape[0]
    slots = idx.shape[1]
    outs = wout_t.shape[0]
    whole = lambda t: (0, 0)
    step = lambda t: (t, 0)
    return pl.pallas_call(
        functools.partial(forward_kernel, slots),
        grid=(grid_rows // TILE,),
        in_specs=[
            pl.BlockSpec((nodes, width), whole),
            pl.BlockSpec((TILE, width), step),
            pl.BlockSpec((TILE, slots), step),
            pl.BlockSpec((TILE, 1), step),
            pl.BlockSpec((outs, width), whole),
        ],
        out_specs=[
            pl.BlockSpec((TILE * slots, width), step),
            pl.BlockSpec((grid_rows, width), whole),
            pl.BlockSpec((TILE, width), step),
            pl.BlockSpec((outs, grid_rows), whole),
        ],
        out_shape=[
            jax.ShapeDtypeStruct((grid_rows * slots, width), bf16),
            jax.ShapeDtypeStruct((grid_rows, width), bf16),
            jax.ShapeDtypeStruct((grid_rows, width), bf16),
            jax.ShapeDtypeStruct((outs, grid_rows), f32),
        ],
        scratch_shapes=[
            pltpu.VMEM((nodes + TILE, width), bf16),
            pltpu.VMEM((TILE * slots, nodes + TILE), bf16),
            pltpu.VMEM((2, TILE * slots, NCOL), bf16),
        ],
        compiler_params=pltpu.CompilerParams(vmem_limit_bytes=VMEM_LIMIT),
        cost_estimate=pl.CostEstimate(
            flops=2 * grid_rows * slots * 256 * width,
            bytes_accessed=2 * grid_rows * slots * width,
            transcendentals=grid_rows * slots * width,
        ),
        name="forward",
    )(wide, dst, idx, scale, wout_t)


def middle_kernel(
    core_ref,
    every_ref,
    pred_ref,
    truth_ref,
    area_ref,
    var_ref,
    wout_ref,
    scale_ref,
    sum_ref,
    agg_ref,
    grid_ref,
    lead_ref,
    own_ref,
    far_ref,
    dpred,
    ddst,
    part,
):
    width = sum_ref.shape[1]
    half = width // 2
    members = every_ref.shape[0]
    outs = pred_ref.shape[0]
    core = core_ref[0]

    @pl.when(pl.program_id(0) == 0)
    def _():
        pred = pred_ref[...]
        pair = jnp.zeros_like(pred)
        for e in range(members):
            pair = pair + smooth_grad(pred - every_ref[e])
        weighting = loss_scale * area_ref[...] * var_ref[...]
        dpred[...] = (
            weighting
            * (smooth_grad(pred - truth_ref[...]) / members - pair / (members * (members - 1)))
        ).astype(bf16)
        for n in range(width // NCOL):
            cols = slice(n * NCOL, (n + 1) * NCOL)
            dagg = lax.dot_general(
                dpred[...], wout_ref[:, cols], (((0,), (0,)), ((), ())), preferred_element_type=f32
            )
            dagg = dagg * scale_ref[...]
            lead_ref[:, cols] = dagg.astype(bf16)
            ddst[:, cols] = (dagg * sum_ref[:, cols].astype(f32)).astype(bf16)

    first = (((0,), (0,)), ((), ()))
    mine = pl.ds(pl.multiple_of(core * half, half), half)
    other = pl.ds(pl.multiple_of((1 - core) * half, half), half)
    part[...] = jnp.dot(dpred[...], agg_ref[...], preferred_element_type=f32)
    few = outs // 2
    rows = far_ref.shape[1] - few
    for chunk in range(far_ref.shape[0]):
        here = slice(chunk * rows, (chunk + 1) * rows)
        for ref, columns, which in ((far_ref, other, 1 - core), (own_ref, mine, core)):
            ref[chunk, :rows, :] = lax.dot_general(
                grid_ref[:, here], ddst[:, columns], first, preferred_element_type=f32
            ).astype(ref.dtype)
            ref[chunk, rows:, :] = jnp.zeros((few, half), ref.dtype)
            ref[chunk, rows:, :rows] = part[
                pl.ds(pl.multiple_of(which * few, few), few), here
            ].astype(ref.dtype)


def middle(core, everyone, pred, truth_t, area, var, wout_t, scale, sums, agg, grid_embed, chunks):
    grid_rows, width = sums.shape
    outs = pred.shape[0]
    block = (chunks, width // chunks + outs // 2, width // 2)
    per_step = NCOL * chunks // width
    whole = lambda t, c: (0, 0)
    return pl.pallas_call(
        middle_kernel,
        grid_spec=pltpu.PrefetchScalarGridSpec(
            num_scalar_prefetch=1,
            grid=(width // NCOL,),
            in_specs=[
                pl.BlockSpec(everyone.shape, lambda t, c: (0, 0, 0)),
                pl.BlockSpec(pred.shape, whole),
                pl.BlockSpec(truth_t.shape, whole),
                pl.BlockSpec(area.shape, whole),
                pl.BlockSpec(var.shape, whole),
                pl.BlockSpec(wout_t.shape, whole),
                pl.BlockSpec(scale.shape, whole),
                pl.BlockSpec(sums.shape, whole),
                pl.BlockSpec((grid_rows, NCOL), lambda t, c: (0, t)),
                pl.BlockSpec((grid_rows, NCOL), lambda t, c: (0, t)),
            ],
            out_specs=[
                pl.BlockSpec((grid_rows, width), whole),
                pl.BlockSpec((per_step,) + block[1:], lambda t, c: (t, 0, 0)),
                pl.BlockSpec((per_step,) + block[1:], lambda t, c: (t, 0, 0)),
            ],
            scratch_shapes=[
                pltpu.VMEM((outs, grid_rows), bf16),
                pltpu.VMEM((grid_rows, width), bf16),
                pltpu.VMEM((outs, NCOL), f32),
            ],
        ),
        out_shape=[
            jax.ShapeDtypeStruct((grid_rows, width), bf16),
            jax.ShapeDtypeStruct(block, f32),
            jax.ShapeDtypeStruct(block, bf16),
        ],
        compiler_params=pltpu.CompilerParams(vmem_limit_bytes=VMEM_LIMIT),
        cost_estimate=pl.CostEstimate(
            flops=2 * grid_rows * width * width, bytes_accessed=10 * grid_rows * width, transcendentals=0
        ),
        name="middle",
    )(core, everyone, pred, truth_t, area, var, wout_t, scale, sums, agg, grid_embed)


def backward_kernel(slots, col_ref, gp_ref, lead_ref, idx_ref, feats_ref, wide_ref, part_ref, prod, acc):
    step = pl.program_id(0)
    nodes, half = acc.shape
    tile = lead_ref.shape[0]

    @pl.when(step == 0)
    def _():
        acc[...] = jnp.zeros_like(acc)

    node = lax.broadcasted_iota(jnp.int32, (nodes, tile * slots), 0)
    hot = jnp.where(node == idx_ref[0], 1.0, 0.0).astype(bf16)
    for k in range(slots):
        rows = slice(k * tile, (k + 1) * tile)
        prod[rows, :] = gp_ref[rows, :] * lead_ref[...]
    for n in range(half // NCOL):
        cols = slice(n * NCOL, (n + 1) * NCOL)
        acc[:, cols] += jnp.dot(hot, prod[:, cols], preferred_element_type=f32)

    @pl.when(step == pl.num_programs(0) - 1)
    def _():
        wide_ref[...] = acc[...].astype(bf16)
        for n in range(part_ref.shape[0] // NCOL):
            rows = slice(n * NCOL, (n + 1) * NCOL)
            part_ref[rows, :] = lax.dot_general(
                feats_ref[:, rows], wide_ref[...], (((0,), (0,)), ((), ())), preferred_element_type=f32
            ).astype(part_ref.dtype)


def backward(col, gp, lead, idx_rows, feats, part_type):
    grid_rows, width = lead.shape
    slots = gp.shape[0] // grid_rows
    nodes = feats.shape[0]
    half = width // 2
    whole = lambda t, c: (0, 0)
    return pl.pallas_call(
        functools.partial(backward_kernel, slots),
        grid_spec=pltpu.PrefetchScalarGridSpec(
            num_scalar_prefetch=1,
            grid=(grid_rows // TILE,),
            in_specs=[
                pl.BlockSpec((TILE * slots, half), lambda t, c: (t, c[0])),
                pl.BlockSpec((TILE, half), lambda t, c: (t, c[0])),
                pl.BlockSpec((1, 1, TILE * slots), lambda t, c: (t, 0, 0)),
                pl.BlockSpec(feats.shape, whole),
            ],
            out_specs=[
                pl.BlockSpec((nodes, half), whole),
                pl.BlockSpec((width, half), whole),
            ],
            scratch_shapes=[
                pltpu.VMEM((TILE * slots, half), bf16),
                pltpu.VMEM((nodes, half), f32),
            ],
        ),
        out_shape=[
            jax.ShapeDtypeStruct((nodes, half), bf16),
            jax.ShapeDtypeStruct((width, half), part_type),
        ],
        compiler_params=pltpu.CompilerParams(vmem_limit_bytes=VMEM_LIMIT),
        cost_estimate=pl.CostEstimate(
            flops=grid_rows * slots * 256 * width,
            bytes_accessed=grid_rows * slots * width,
            transcendentals=0,
        ),
        name="backward",
    )(col, gp, lead, idx_rows, feats)


def x_pieces(total):
    count = lax.axis_size("x")
    here = lax.axis_index("x")
    total = total.reshape(lax.axis_size("zh"), count, -1, total.shape[-1])
    quarter = lambda d: lax.dynamic_index_in_dim(total, (here + d) % count, 1, keepdims=False)
    return quarter(0), [quarter(d).astype(bf16) for d in (2, 1, 3)]


def x_moved(pieces):
    return [shifted(piece, "x", d) for piece, d in zip(pieces, (2, 1, 3))]


def summed(kept, moved):
    for piece in moved:
        kept = kept + piece.astype(f32)
    return kept


def body(
    mesh_feats,
    grid_embed,
    w_src,
    w_dst,
    w_out,
    truth,
    area_weight,
    var_weight,
    neighbour,
    edge_mask,
):
    own = mesh_feats[0]
    node_rows, width = own.shape
    grid_rows, slots = neighbour.shape
    half = width // 2
    tiles = grid_rows // TILE
    space_count = lax.axis_size(SPACE)
    block_id = lax.axis_index(SPACE)
    members = lax.axis_size(ENS)
    swap = [(0, 1), (1, 0)]
    core = lax.axis_index("c")
    mine = jnp.full((1,), core, jnp.int32)

    below = shifted(own, SPACE, 1)
    above = shifted(own, SPACE, -1)
    feats = jnp.concatenate([below, own, above], axis=0)

    dst = jnp.dot(grid_embed, w_dst, preferred_element_type=f32).astype(bf16)
    local = jnp.mod(neighbour - (block_id - 1) * node_rows, node_rows * space_count)
    idx = jnp.where(edge_mask > 0, local, -1)
    idx_rows = idx.reshape(tiles, TILE, slots).transpose(0, 2, 1).reshape(tiles, 1, slots * TILE)
    scale = 0.5 / jnp.sum(edge_mask.astype(f32), axis=1, keepdims=True)
    wout_t = w_out.T
    truth_t = truth.T
    dst, idx, idx_rows, scale, wout_t, truth_t, below = lax.optimization_barrier(
        (dst, idx, idx_rows, scale, wout_t, truth_t, below)
    )
    feats = jnp.concatenate([below, own, above], axis=0)
    wide = jnp.dot(feats, w_src, preferred_element_type=f32).astype(bf16)

    gp, agg, sums, pred = forward(wide, dst, idx, scale, wout_t)
    everyone = lax.all_to_all(
        jnp.broadcast_to(pred[None], (members,) + pred.shape), ENS, 0, 0, tiled=True
    )
    lead, dst_own, dst_far = middle(
        mine,
        everyone,
        pred,
        truth_t,
        area_weight[None, :],
        var_weight[:, None],
        wout_t,
        scale,
        sums,
        agg,
        grid_embed,
        members,
    )
    dst_far = lax.ppermute(dst_far, "c", swap)
    wide_far, src_far = backward(1 - mine, gp, lead, idx_rows, feats, bf16)
    src_far = lax.ppermute(src_far, "c", swap)
    dst_kept, dst_pieces = x_pieces(dst_own + dst_far.astype(f32))
    lead, *dst_pieces = lax.optimization_barrier((lead, *dst_pieces))
    dst_moved = x_moved(dst_pieces)
    wide_own, src_own = backward(mine, gp, lead, idx_rows, feats, f32)
    src_own, src_far, *dst_moved = lax.optimization_barrier((src_own, src_far, *dst_moved))
    src_kept, src_pieces = x_pieces(src_own + src_far.astype(f32))
    src_moved = x_moved(src_pieces)

    lower = core == 0
    dwide = jnp.concatenate(
        [jnp.where(lower, wide_own, wide_far), jnp.where(lower, wide_far, wide_own)], axis=1
    )
    from_above = shifted(dwide[:node_rows], SPACE, -1)
    from_below = shifted(dwide[2 * node_rows :], SPACE, 1)

    dst_sum = summed(dst_kept, dst_moved)
    late_rows = width // lax.axis_size("x")
    per_chunk = width // members
    total = jnp.concatenate(
        [
            summed(src_kept, src_moved).reshape(late_rows, half),
            dst_sum[:, :per_chunk].reshape(late_rows, half),
            dst_sum[:, per_chunk:, :per_chunk].transpose(0, 2, 1).reshape(late_rows, -1),
        ],
        axis=1,
    )
    total, from_above, from_below = lax.optimization_barrier(
        (total.astype(bf16), from_above, from_below)
    )
    dproj = (
        dwide[node_rows : 2 * node_rows].astype(f32)
        + from_above.astype(f32)
        + from_below.astype(f32)
    ).astype(bf16)
    grad_mesh = lax.dot_general(
        dproj, w_src, (((1,), (1,)), ((), ())), preferred_element_type=f32
    ).astype(bf16)
    columns = total.shape[1]
    pieces = lax.all_to_all(total, LATE, 0, 0, tiled=True)
    pieces = pieces.reshape(-1, 2, pieces.shape[0] // lax.axis_size(LATE), columns)
    total = jnp.sum(pieces.astype(f32), axis=0)
    joined = lambda a, b: jnp.concatenate([total[0, :, a:b], total[1, :, a:b]], axis=1)
    return (
        grad_mesh[None],
        joined(0, half),
        joined(half, 2 * half),
        joined(2 * half, columns),
    )


def solution(mesh):
    fine = Mesh(mesh.devices.reshape(2, 4, 4, 4, 2), ("zh", "x", "y", "zl", "c"))
    everywhere = ENS + SPACE
    in_specs = (
        P(ENS, SPACE, None),
        P(SPACE, None),
        P(),
        P(),
        P(),
        P(SPACE, None),
        P(SPACE),
        P(),
        P(SPACE, None),
        P(SPACE, None),
    )
    out_specs = (
        P(ENS, SPACE, None),
        P(everywhere, None),
        P(everywhere, None),
        P(everywhere, None),
    )
    return jax.shard_map(body, mesh=fine, in_specs=in_specs, out_specs=out_specs, check_vma=False)
```

```python
import functools
import jax
import jax.numpy as jnp
from jax import lax
from jax.experimental import pallas as pl
from jax.experimental.pallas import tpu as pltpu
from jax.sharding import Mesh, PartitionSpec as P

loss_scale = 8.0
smooth_sq = 0.01
TILE = 64
NCOL = 256
ROWS = 32
GROUP = 4
VMEM_LIMIT = 12 * 1024 * 1024
BACK = 2
AHEAD = (2, 1, 3)
f32 = jnp.float32
bf16 = jnp.bfloat16
SPACE = ("y", "zl", "c")
ENS = ("zh", "x")
LATE = ("zh", "y", "zl", "c")


def shifted(block, axes, distance):
    count = lax.axis_size(axes)
    return lax.ppermute(block, axes, [(i, (i + distance) % count) for i in range(count)])


def smooth_grad(diff):
    return diff / jnp.sqrt(diff * diff + smooth_sq)


def gelu_parts(v):
    c0 = 0.7978845608
    c1 = c0 * 0.044715
    sq = v * v
    t = jnp.tanh(v * (c0 + c1 * sq))
    u = 1.0 + t
    slope = v * (c0 + (3.0 * c1) * sq)
    return v * u, u * (1.0 + (1.0 - t) * slope)


def resident(shape, dtype):
    return pltpu.VMEM(shape, dtype)


def in_vmem():
    return pl.BlockSpec(memory_space=pltpu.VMEM)


def params():
    return pltpu.CompilerParams(vmem_limit_bytes=VMEM_LIMIT)


def forward_kernel(
    slots,
    members,
    below_ref,
    here_ref,
    above_ref,
    wsrc_ref,
    dst_ref,
    idx_ref,
    scale_ref,
    wout_ref,
    gp_ref,
    agg_ref,
    sum_ref,
    pred_ref,
    sent_ref,
    feats,
    rhs,
    hot,
    pre,
):
    step = pl.program_id(0)
    nodes, width = feats.shape
    depth = rhs.shape[0]
    tile = depth - nodes
    block = below_ref.shape[0]

    @pl.when(step == 0)
    def _():
        for i, ref in enumerate((below_ref, here_ref, above_ref)):
            feats[i * block : (i + 1) * block, :] = ref[...]
        for n in range(width // NCOL):
            cols = slice(n * NCOL, (n + 1) * NCOL)
            rhs[:nodes, cols] = jnp.dot(
                feats[...], wsrc_ref[:, cols], preferred_element_type=f32
            ).astype(bf16)

    base = pl.multiple_of(step * tile, tile)
    rhs[nodes:, :] = dst_ref[pl.ds(base, tile), :]
    lane = lax.broadcasted_iota(jnp.int32, (tile, depth), 1)
    row = lax.broadcasted_iota(jnp.int32, (tile, depth), 0)
    eye = lane == row + nodes
    idx = idx_ref[pl.ds(base, tile), :]
    for k in range(slots):
        col = idx[:, k : k + 1]
        hit = (lane == col) | (eye & (col >= 0))
        hot[k * tile : (k + 1) * tile, :] = jnp.where(hit, 1.0, 0.0).astype(bf16)
    for n in range(width // NCOL):
        cols = slice(n * NCOL, (n + 1) * NCOL)
        pre[n % 2] = jnp.dot(hot[...], rhs[:, cols], preferred_element_type=f32).astype(bf16)
        for r in range(0, tile, ROWS):
            acc_g = jnp.zeros((ROWS, NCOL), f32)
            acc_s = jnp.zeros((ROWS, NCOL), f32)
            for k in range(slots):
                rows = k * tile + r
                value, grad = gelu_parts(pre[n % 2, rows : rows + ROWS, :])
                gp_ref[pl.ds(pl.multiple_of(step * tile * slots + rows, ROWS), ROWS), cols] = grad
                if k % GROUP == 0:
                    some_g, some_s = value, grad
                else:
                    some_g, some_s = some_g + value, some_s + grad
                if k % GROUP == GROUP - 1:
                    acc_g = acc_g + some_g.astype(f32)
                    acc_s = acc_s + some_s.astype(f32)
            at = pl.ds(pl.multiple_of(base + r, ROWS), ROWS)
            scale = scale_ref[at, :]
            agg_ref[at, cols] = (acc_g * scale).astype(bf16)
            sum_ref[at, cols] = (acc_s - (slots - 0.5 / scale)).astype(bf16)

    @pl.when(step == pl.num_programs(0) - 1)
    def _():
        pred = lax.dot_general(
            wout_ref[...], agg_ref[...], (((1,), (1,)), ((), ())), preferred_element_type=f32
        )
        pred_ref[...] = pred
        for e in range(members):
            sent_ref[e] = pred.astype(bf16)


def forward(below, here, above, w_src, dst, idx, scale, wout_t, members):
    grid_rows, width = dst.shape
    nodes = 3 * here.shape[0]
    slots = idx.shape[1]
    outs = wout_t.shape[0]
    return pl.pallas_call(
        functools.partial(forward_kernel, slots, members),
        grid=(grid_rows // TILE,),
        in_specs=[in_vmem() for _ in range(8)],
        out_specs=[in_vmem() for _ in range(5)],
        out_shape=[
            resident((grid_rows * slots, width), bf16),
            resident((grid_rows, width), bf16),
            resident((grid_rows, width), bf16),
            resident((outs, grid_rows), f32),
            resident((members, outs, grid_rows), bf16),
        ],
        scratch_shapes=[
            pltpu.VMEM((nodes, width), bf16),
            pltpu.VMEM((nodes + TILE, width), bf16),
            pltpu.VMEM((TILE * slots, nodes + TILE), bf16),
            pltpu.VMEM((2, TILE * slots, NCOL), bf16),
        ],
        compiler_params=params(),
        cost_estimate=pl.CostEstimate(
            flops=2 * grid_rows * slots * 256 * width,
            bytes_accessed=2 * grid_rows * slots * width,
            transcendentals=grid_rows * slots * width,
        ),
        name="forward",
    )(below, here, above, w_src, dst, idx, scale, wout_t)


def middle_kernel(
    core_ref,
    every_ref,
    pred_ref,
    truth_ref,
    area_ref,
    var_ref,
    wout_ref,
    scale_ref,
    sum_ref,
    agg_ref,
    grid_ref,
    lead_ref,
    own_ref,
    far_ref,
    ddst,
    part,
):
    width = sum_ref.shape[1]
    half = width // 2
    members = every_ref.shape[0]
    outs = pred_ref.shape[0]
    core = core_ref[0]

    pred = pred_ref[...]
    pair = -smooth_grad(pred - pred.astype(bf16).astype(f32))
    for e in range(members):
        pair = pair + smooth_grad(pred - every_ref[e].astype(f32))
    weighting = loss_scale * area_ref[...] * var_ref[...]
    dpred = (
        weighting
        * (smooth_grad(pred - truth_ref[...]) / members - pair / (members * (members - 1)))
    ).astype(bf16)
    for n in range(width // NCOL):
        cols = slice(n * NCOL, (n + 1) * NCOL)
        dagg = lax.dot_general(
            dpred, wout_ref[:, cols], (((0,), (0,)), ((), ())), preferred_element_type=f32
        )
        dagg = dagg * scale_ref[...]
        lead_ref[:, cols] = dagg.astype(bf16)
        ddst[:, cols] = (dagg * sum_ref[:, cols].astype(f32)).astype(bf16)

    mine = pl.ds(pl.multiple_of(core * half, half), half)
    other = pl.ds(pl.multiple_of((1 - core) * half, half), half)
    part[...] = jnp.dot(dpred, agg_ref[...], preferred_element_type=f32)
    few = outs // 2
    chunks = far_ref.shape[0]
    rows = far_ref.shape[1] - few
    for ref, columns, which in ((far_ref, other, 1 - core), (own_ref, mine, core)):
        ref[:, :rows, :] = (
            lax.dot_general(
                grid_ref[...], ddst[:, columns], (((0,), (0,)), ((), ())), preferred_element_type=f32
            )
            .reshape(chunks, rows, half)
            .astype(ref.dtype)
        )
        ref[:, rows:, :] = jnp.zeros((chunks, few, half), ref.dtype)
        for chunk in range(chunks):
            ref[chunk, rows:, :rows] = part[
                pl.ds(pl.multiple_of(which * few, few), few), chunk * rows : (chunk + 1) * rows
            ].astype(ref.dtype)


def prefetched(count, ins, outs, scratch):
    return pltpu.PrefetchScalarGridSpec(
        num_scalar_prefetch=1,
        grid=(count,),
        in_specs=[in_vmem() for _ in range(ins)],
        out_specs=[in_vmem() for _ in range(outs)],
        scratch_shapes=scratch,
    )


def middle(core, everyone, pred, truth_t, area, var, wout_t, scale, sums, agg, grid_embed):
    grid_rows, width = sums.shape
    outs = pred.shape[0]
    chunks = everyone.shape[0]
    block = (chunks, width // chunks + outs // 2, width // 2)
    return pl.pallas_call(
        middle_kernel,
        grid_spec=prefetched(
            1,
            10,
            3,
            [pltpu.VMEM((grid_rows, width), bf16), pltpu.VMEM((outs, width), f32)],
        ),
        out_shape=[
            resident((grid_rows, width), bf16),
            resident(block, f32),
            resident(block, bf16),
        ],
        compiler_params=params(),
        cost_estimate=pl.CostEstimate(
            flops=2 * grid_rows * width * width, bytes_accessed=10 * grid_rows * width, transcendentals=0
        ),
        name="middle",
    )(core, everyone, pred, truth_t, area, var, wout_t, scale, sums, agg, grid_embed)


def quarter(here, zh, d, count):
    return zh * count + (here + d) % count


def combine_kernel(place_ref, own_ref, far_ref, kept_ref, *piece_refs):
    count = own_ref.shape[0] // kept_ref.shape[0]
    for zh in range(kept_ref.shape[0]):
        for d, ref in zip((0,) + AHEAD, (kept_ref,) + piece_refs):
            at = quarter(place_ref[0], zh, d, count)
            ref[zh] = (own_ref[at] + far_ref[at].astype(f32)).astype(ref.dtype)


def combine(place, own, far, groups):
    block = (groups,) + own.shape[1:]
    return pl.pallas_call(
        combine_kernel,
        grid_spec=prefetched(1, 2, 1 + len(AHEAD), []),
        out_shape=[resident(block, f32)] + [resident(block, bf16) for _ in AHEAD],
        compiler_params=params(),
        cost_estimate=pl.CostEstimate(flops=own.size, bytes_accessed=12 * own.size, transcendentals=0),
        name="combine",
    )(place, own, far)


def scatter_step(slots, col, gp_ref, lead_ref, idx_ref, hot, prod, acc):
    step = pl.program_id(0)
    nodes, half = acc.shape
    wide = BACK * TILE

    @pl.when(step == 0)
    def _():
        acc[...] = jnp.zeros_like(acc)

    cols = pl.ds(pl.multiple_of(col * half, half), half)
    node = lax.broadcasted_iota(jnp.int32, (nodes, wide), 0)
    idx = idx_ref[:, pl.ds(pl.multiple_of(step * wide, wide), wide)]
    for k in range(slots):
        hot[:, k * wide : (k + 1) * wide] = jnp.where(node == idx[k : k + 1, :], 1.0, 0.0).astype(bf16)
    for part in range(BACK):
        lead = lead_ref[pl.ds(pl.multiple_of(step * wide + part * TILE, TILE), TILE), cols]
        for k in range(slots):
            start = (step * BACK + part) * slots * TILE + k * TILE
            to = k * wide + part * TILE
            prod[to : to + TILE, :] = gp_ref[pl.ds(pl.multiple_of(start, TILE), TILE), cols] * lead
    for n in range(half // NCOL):
        here = slice(n * NCOL, (n + 1) * NCOL)
        acc[:, here] += jnp.dot(hot[...], prod[:, here], preferred_element_type=f32)


def far_kernel(
    slots, core_ref, gp_ref, lead_ref, idx_ref, below_ref, here_ref, above_ref, wide_ref, part_ref, hot, prod, acc
):
    scatter_step(slots, 1 - core_ref[0], gp_ref, lead_ref, idx_ref, hot, prod, acc)

    @pl.when(pl.program_id(0) == pl.num_programs(0) - 1)
    def _():
        wide_ref[...] = acc[...].astype(bf16)
        feats = jnp.concatenate([below_ref[...], here_ref[...], above_ref[...]], axis=0)
        part_ref[...] = (
            lax.dot_general(feats, wide_ref[...], (((0,), (0,)), ((), ())), preferred_element_type=f32)
            .reshape(part_ref.shape)
            .astype(bf16)
        )


def own_kernel(
    slots,
    place_ref,
    gp_ref,
    lead_ref,
    idx_ref,
    below_ref,
    here_ref,
    above_ref,
    widefar_ref,
    far_ref,
    lower_ref,
    centre_ref,
    upper_ref,
    kept_ref,
    *rest,
):
    pieces, (hot, prod, acc, total) = rest[: len(AHEAD)], rest[len(AHEAD) :]
    core = place_ref[1]
    scatter_step(slots, core, gp_ref, lead_ref, idx_ref, hot, prod, acc)

    @pl.when(pl.program_id(0) == pl.num_programs(0) - 1)
    def _():
        half = acc.shape[1]
        block = lower_ref.shape[0]
        mine = pl.ds(pl.multiple_of(core * half, half), half)
        other = pl.ds(pl.multiple_of((1 - core) * half, half), half)
        wide = acc[...].astype(bf16)
        for i, ref in enumerate((lower_ref, centre_ref, upper_ref)):
            ref[:, mine] = wide[i * block : (i + 1) * block, :]
            ref[:, other] = widefar_ref[i * block : (i + 1) * block, :]
        feats = jnp.concatenate([below_ref[...], here_ref[...], above_ref[...]], axis=0)
        total[...] = lax.dot_general(
            feats, wide, (((0,), (0,)), ((), ())), preferred_element_type=f32
        ).reshape(total.shape)
        count = total.shape[0] // kept_ref.shape[0]
        for zh in range(kept_ref.shape[0]):
            for d, ref in zip((0,) + AHEAD, (kept_ref,) + pieces):
                at = quarter(place_ref[0], zh, d, count)
                ref[zh] = (total[at] + far_ref[at].astype(f32)).astype(ref.dtype)


def scatter_scratch(slots, nodes, half):
    wide = BACK * TILE * slots
    return [
        pltpu.VMEM((nodes, wide), bf16),
        pltpu.VMEM((wide, half), bf16),
        pltpu.VMEM((nodes, half), f32),
    ]


def scatter_cost(gp):
    return pl.CostEstimate(flops=gp.size * 256, bytes_accessed=gp.size, transcendentals=0)


def backward_far(core, gp, lead, idx_t, feats, chunks):
    grid_rows, width = lead.shape
    slots = idx_t.shape[0]
    nodes = 3 * feats[0].shape[0]
    half = width // 2
    return pl.pallas_call(
        functools.partial(far_kernel, slots),
        grid_spec=prefetched(
            grid_rows // (BACK * TILE), 6, 2, scatter_scratch(slots, nodes, half)
        ),
        out_shape=[
            resident((nodes, half), bf16),
            resident((chunks, width // chunks, half), bf16),
        ],
        compiler_params=params(),
        cost_estimate=scatter_cost(gp),
        name="backward_far",
    )(core, gp, lead, idx_t, *feats)


def backward_own(place, gp, lead, idx_t, feats, wide_far, far, groups):
    grid_rows, width = lead.shape
    slots = idx_t.shape[0]
    block = feats[0].shape[0]
    half = width // 2
    quarter_shape = (groups,) + far.shape[1:]
    return pl.pallas_call(
        functools.partial(own_kernel, slots),
        grid_spec=prefetched(
            grid_rows // (BACK * TILE),
            8,
            4 + len(AHEAD),
            scatter_scratch(slots, 3 * block, half) + [pltpu.VMEM(far.shape, f32)],
        ),
        out_shape=[resident((block, width), bf16) for _ in range(3)]
        + [resident(quarter_shape, f32)]
        + [resident(quarter_shape, bf16) for _ in AHEAD],
        compiler_params=params(),
        cost_estimate=scatter_cost(gp),
        name="backward_own",
    )(place, gp, lead, idx_t, *feats, wide_far, far)


def x_moved(pieces):
    return [shifted(piece, "x", d) for piece, d in zip(pieces, AHEAD)]


def summed(kept, moved):
    for piece in moved:
        kept = kept + piece.astype(f32)
    return kept


def body(
    mesh_feats,
    grid_embed,
    w_src,
    w_dst,
    w_out,
    truth,
    area_weight,
    var_weight,
    neighbour,
    edge_mask,
):
    own = mesh_feats[0]
    node_rows, width = own.shape
    grid_rows, slots = neighbour.shape
    half = width // 2
    space_count = lax.axis_size(SPACE)
    block_id = lax.axis_index(SPACE)
    members = lax.axis_size(ENS)
    swap = [(0, 1), (1, 0)]
    core = lax.axis_index("c")
    mine = jnp.full((1,), core, jnp.int32)

    groups = lax.axis_size("zh")
    place = jnp.stack([lax.axis_index("x"), core]).astype(jnp.int32)

    below = shifted(own, SPACE, 1)
    above = shifted(own, SPACE, -1)

    dst = jnp.dot(grid_embed, w_dst, preferred_element_type=f32).astype(bf16)
    local = jnp.mod(neighbour.T - (block_id - 1) * node_rows, node_rows * space_count)
    idx_t = jnp.where(edge_mask.T > 0, local, -1)
    idx = idx_t.T
    scale = 0.5 / jnp.sum(edge_mask.T.astype(f32), axis=0)[:, None]
    wout_t = w_out.T
    truth_t = truth.T
    var = var_weight[:, None]
    area = area_weight[None, :]
    dst, idx, idx_t, scale, wout_t, truth_t, var, area, below = lax.optimization_barrier(
        (dst, idx, idx_t, scale, wout_t, truth_t, var, area, below)
    )
    feats = (below, own, above)
    gp, agg, sums, pred, sent = forward(*feats, w_src, dst, idx, scale, wout_t, members)
    everyone = lax.all_to_all(sent, ENS, 0, 0, tiled=True)
    lead, dst_own, dst_far = middle(
        mine, everyone, pred, truth_t, area, var, wout_t, scale, sums, agg, grid_embed
    )
    dst_far = lax.ppermute(dst_far, "c", swap)
    wide_far, src_far = backward_far(mine, gp, lead, idx_t, feats, members)
    src_far = lax.ppermute(src_far, "c", swap)
    dst_kept, *dst_pieces = combine(place, dst_own, dst_far, groups)
    lead, *dst_pieces = lax.optimization_barrier((lead, *dst_pieces))
    dst_moved = x_moved(dst_pieces)
    lower, centre, upper, src_kept, *src_pieces = backward_own(
        place, gp, lead, idx_t, feats, wide_far, src_far, groups
    )
    dst_moved = lax.optimization_barrier(tuple(dst_moved) + tuple(src_pieces))
    src_pieces = dst_moved[len(AHEAD) :]
    dst_moved = dst_moved[: len(AHEAD)]
    src_moved = x_moved(src_pieces)
    from_above = shifted(lower, SPACE, -1)
    from_below = shifted(upper, SPACE, 1)

    dst_sum = summed(dst_kept, dst_moved)
    late_rows = width // lax.axis_size("x")
    per_chunk = width // members
    dst_total = jnp.concatenate(
        [
            dst_sum[:, :per_chunk].reshape(late_rows, half),
            dst_sum[:, per_chunk:, :per_chunk].transpose(0, 2, 1).reshape(late_rows, -1),
        ],
        axis=1,
    ).astype(bf16)
    dst_parts = lax.all_to_all(dst_total, LATE, 0, 0, tiled=True)

    src_total = summed(src_kept, src_moved).reshape(late_rows, half).astype(bf16)
    src_total, dst_parts, from_above, from_below = lax.optimization_barrier(
        (src_total, dst_parts, from_above, from_below)
    )
    src_parts = lax.all_to_all(src_total, LATE, 0, 0, tiled=True)
    dproj = (centre.astype(f32) + from_above.astype(f32) + from_below.astype(f32)).astype(bf16)
    grad_mesh = lax.dot_general(
        dproj, w_src, (((1,), (1,)), ((), ())), preferred_element_type=f32
    ).astype(bf16)

    def late_sum(parts):
        parts = parts.reshape(-1, 2, parts.shape[0] // lax.axis_size(LATE), parts.shape[1])
        return jnp.sum(parts.astype(f32), axis=0)

    def joined(total, a, b):
        return jnp.concatenate([total[0, :, a:b], total[1, :, a:b]], axis=1)

    dst_final = late_sum(dst_parts)
    return (
        grad_mesh[None],
        joined(late_sum(src_parts), 0, half),
        joined(dst_final, 0, half),
        joined(dst_final, half, dst_final.shape[-1]),
    )


def solution(mesh):
    fine = Mesh(mesh.devices.reshape(2, 4, 4, 4, 2), ("zh", "x", "y", "zl", "c"))
    everywhere = ENS + SPACE
    in_specs = (
        P(ENS, SPACE, None),
        P(SPACE, None),
        P(),
        P(),
        P(),
        P(SPACE, None),
        P(SPACE),
        P(),
        P(SPACE, None),
        P(SPACE, None),
    )
    out_specs = (
        P(ENS, SPACE, None),
        P(everywhere, None),
        P(everywhere, None),
        P(everywhere, None),
    )
    return jax.shard_map(body, mesh=fine, in_specs=in_specs, out_specs=out_specs, check_vma=False)
```

```python
import functools
import jax
import jax.numpy as jnp
from jax import lax
from jax.experimental import pallas as pl
from jax.experimental.pallas import tpu as pltpu
from jax.sharding import Mesh, PartitionSpec as P

loss_scale = 8.0
smooth_sq = 0.01
TILE = 64
NCOL = 256
ROWS = 32
GROUP = 4
VMEM_LIMIT = 56 * 1024 * 1024
BACK = 2
GROUPS = 2
f32 = jnp.float32
bf16 = jnp.bfloat16
SPACE = ("y", "zl", "c")
ENS = ("zh", "x")
FIRST = ("x", "y")
SECOND = ("zh", "zl", "c")


def shifted(block, axes, distance):
    count = lax.axis_size(axes)
    return lax.ppermute(block, axes, [(i, (i + distance) % count) for i in range(count)])


def smooth_grad(diff):
    return diff / jnp.sqrt(diff * diff + smooth_sq)


def gelu_parts(v):
    c0 = 0.7978845608
    c1 = c0 * 0.044715
    sq = v * v
    t = jnp.tanh(v * (c0 + c1 * sq))
    u = 1.0 + t
    slope = v * (c0 + (3.0 * c1) * sq)
    return v * u, u * (1.0 + (1.0 - t) * slope)


def whole(array):
    zeros = (0,) * len(array.shape)
    return pl.BlockSpec(array.shape, lambda *_: zeros)


def params():
    return pltpu.CompilerParams(vmem_limit_bytes=VMEM_LIMIT)


def forward_kernel(
    slots,
    members,
    below_ref,
    here_ref,
    above_ref,
    wsrc_ref,
    dst_ref,
    idx_ref,
    scale_ref,
    wout_ref,
    gp_ref,
    agg_ref,
    sum_ref,
    pred_ref,
    sent_ref,
    feats,
    rhs,
    hot,
    pre,
):
    step = pl.program_id(0)
    nodes, width = feats.shape
    depth = rhs.shape[0]
    tile = depth - nodes
    block = below_ref.shape[0]

    @pl.when(step == 0)
    def _():
        for i, ref in enumerate((below_ref, here_ref, above_ref)):
            feats[i * block : (i + 1) * block, :] = ref[...]
        for n in range(width // NCOL):
            cols = slice(n * NCOL, (n + 1) * NCOL)
            rhs[:nodes, cols] = jnp.dot(
                feats[...], wsrc_ref[:, cols], preferred_element_type=f32
            ).astype(bf16)

    base = pl.multiple_of(step * tile, tile)
    rhs[nodes:, :] = dst_ref[...]
    lane = lax.broadcasted_iota(jnp.int32, (tile, depth), 1)
    row = lax.broadcasted_iota(jnp.int32, (tile, depth), 0)
    eye = lane == row + nodes
    for k in range(slots):
        col = idx_ref[:, k : k + 1]
        hit = (lane == col) | (eye & (col >= 0))
        hot[k * tile : (k + 1) * tile, :] = jnp.where(hit, 1.0, 0.0).astype(bf16)
    for n in range(width // NCOL):
        cols = slice(n * NCOL, (n + 1) * NCOL)
        pre[n % 2] = jnp.dot(hot[...], rhs[:, cols], preferred_element_type=f32).astype(bf16)
        for r in range(0, tile, ROWS):
            acc_g = jnp.zeros((ROWS, NCOL), f32)
            acc_s = jnp.zeros((ROWS, NCOL), f32)
            for k in range(slots):
                rows = slice(k * tile + r, k * tile + r + ROWS)
                value, grad = gelu_parts(pre[n % 2, rows, :])
                gp_ref[rows, cols] = grad
                if k % GROUP == 0:
                    some_g, some_s = value, grad
                else:
                    some_g, some_s = some_g + value, some_s + grad
                if k % GROUP == GROUP - 1:
                    acc_g = acc_g + some_g.astype(f32)
                    acc_s = acc_s + some_s.astype(f32)
            scale = scale_ref[r : r + ROWS, :]
            agg_ref[pl.ds(pl.multiple_of(base + r, ROWS), ROWS), cols] = (acc_g * scale).astype(bf16)
            sum_ref[r : r + ROWS, cols] = (acc_s - (slots - 0.5 / scale)).astype(bf16)

    @pl.when(step == pl.num_programs(0) - 1)
    def _():
        pred = lax.dot_general(
            wout_ref[...], agg_ref[...], (((1,), (1,)), ((), ())), preferred_element_type=f32
        )
        pred_ref[...] = pred
        for e in range(members):
            sent_ref[e] = pred.astype(bf16)


def forward(below, here, above, w_src, dst, idx, scale, wout_t, members):
    grid_rows, width = dst.shape
    nodes = 3 * here.shape[0]
    slots = idx.shape[1]
    outs = wout_t.shape[0]
    step = lambda t: (t, 0)
    out_shape = [
        jax.ShapeDtypeStruct((grid_rows * slots, width), bf16),
        jax.ShapeDtypeStruct((grid_rows, width), bf16),
        jax.ShapeDtypeStruct((grid_rows, width), bf16),
        jax.ShapeDtypeStruct((outs, grid_rows), f32),
        jax.ShapeDtypeStruct((members, outs, grid_rows), bf16),
    ]
    return pl.pallas_call(
        functools.partial(forward_kernel, slots, members),
        grid=(grid_rows // TILE,),
        in_specs=[whole(below), whole(here), whole(above), whole(w_src)]
        + [
            pl.BlockSpec((TILE, width), step),
            pl.BlockSpec((TILE, slots), step),
            pl.BlockSpec((TILE, 1), step),
            whole(wout_t),
        ],
        out_specs=[
            pl.BlockSpec((TILE * slots, width), step),
            whole(out_shape[1]),
            pl.BlockSpec((TILE, width), step),
            whole(out_shape[3]),
            whole(out_shape[4]),
        ],
        out_shape=out_shape,
        scratch_shapes=[
            pltpu.VMEM((nodes, width), bf16),
            pltpu.VMEM((nodes + TILE, width), bf16),
            pltpu.VMEM((TILE * slots, nodes + TILE), bf16),
            pltpu.VMEM((2, TILE * slots, NCOL), bf16),
        ],
        compiler_params=params(),
        cost_estimate=pl.CostEstimate(
            flops=2 * grid_rows * slots * 256 * width,
            bytes_accessed=2 * grid_rows * slots * width,
            transcendentals=grid_rows * slots * width,
        ),
        name="forward",
    )(below, here, above, w_src, dst, idx, scale, wout_t)


def middle_kernel(
    core_ref,
    every_ref,
    pred_ref,
    truth_ref,
    area_ref,
    var_ref,
    wout_ref,
    scale_ref,
    sum_ref,
    agg_hbm,
    grid_hbm,
    lead_hbm,
    own_hbm,
    far_hbm,
    agg_ref,
    grid_ref,
    lead_ref,
    own_ref,
    far_ref,
    ddst,
    part,
    sems,
):
    loads = [
        pltpu.make_async_copy(agg_hbm, agg_ref, sems.at[0]),
        pltpu.make_async_copy(grid_hbm, grid_ref, sems.at[1]),
    ]
    stores = [
        pltpu.make_async_copy(lead_ref, lead_hbm, sems.at[2]),
        pltpu.make_async_copy(far_ref, far_hbm, sems.at[3]),
        pltpu.make_async_copy(own_ref, own_hbm, sems.at[4]),
    ]
    for copy in loads:
        copy.start()
    width = sum_ref.shape[1]
    half = width // 2
    members = every_ref.shape[0]
    outs = pred_ref.shape[0]
    core = core_ref[0]

    pred = pred_ref[...]
    pair = -smooth_grad(pred - pred.astype(bf16).astype(f32))
    for e in range(members):
        pair = pair + smooth_grad(pred - every_ref[e].astype(f32))
    weighting = loss_scale * area_ref[...] * var_ref[...]
    dpred = (
        weighting
        * (smooth_grad(pred - truth_ref[...]) / members - pair / (members * (members - 1)))
    ).astype(bf16)
    for n in range(width // NCOL):
        cols = slice(n * NCOL, (n + 1) * NCOL)
        dagg = lax.dot_general(
            dpred, wout_ref[:, cols], (((0,), (0,)), ((), ())), preferred_element_type=f32
        )
        dagg = dagg * scale_ref[...]
        lead_ref[:, cols] = dagg.astype(bf16)
        ddst[:, cols] = (dagg * sum_ref[:, cols].astype(f32)).astype(bf16)

    stores[0].start()
    for copy in loads:
        copy.wait()
    mine = pl.ds(pl.multiple_of(core * half, half), half)
    other = pl.ds(pl.multiple_of((1 - core) * half, half), half)
    part[...] = jnp.dot(dpred, agg_ref[...], preferred_element_type=f32)
    few = outs // 2
    for ref, columns, which, store in (
        (far_ref, other, 1 - core, stores[1]),
        (own_ref, mine, core, stores[2]),
    ):
        ref[:width, :] = lax.dot_general(
            grid_ref[...], ddst[:, columns], (((0,), (0,)), ((), ())), preferred_element_type=f32
        ).astype(bf16)
        at = pl.ds(pl.multiple_of(which * few, few), few)
        ref[width : width + few, :] = part[at, :half].astype(bf16)
        ref[width + few :, :] = part[at, half:].astype(bf16)
        store.start()
    for copy in stores:
        copy.wait()


def prefetched(count, ins, outs, scratch):
    return pltpu.PrefetchScalarGridSpec(
        num_scalar_prefetch=1, grid=(count,), in_specs=ins, out_specs=outs, scratch_shapes=scratch
    )


def middle(core, everyone, pred, truth_t, area, var, wout_t, scale, sums, agg, grid_embed):
    grid_rows, width = sums.shape
    outs = pred.shape[0]
    block = (width + outs, width // 2)
    anywhere = pl.BlockSpec(memory_space=pl.ANY)
    small = (everyone, pred, truth_t, area, var, wout_t, scale, sums)
    return pl.pallas_call(
        middle_kernel,
        grid_spec=prefetched(
            1,
            [whole(x) for x in small] + [anywhere] * 2,
            [anywhere] * 3,
            [
                pltpu.VMEM((grid_rows, width), bf16),
                pltpu.VMEM((grid_rows, width), bf16),
                pltpu.VMEM((grid_rows, width), bf16),
                pltpu.VMEM(block, bf16),
                pltpu.VMEM(block, bf16),
                pltpu.VMEM((grid_rows, width), bf16),
                pltpu.VMEM((outs, width), f32),
                pltpu.SemaphoreType.DMA((5,)),
            ],
        ),
        out_shape=[
            jax.ShapeDtypeStruct((grid_rows, width), bf16),
            jax.ShapeDtypeStruct(block, bf16),
            jax.ShapeDtypeStruct(block, bf16),
        ],
        compiler_params=params(),
        cost_estimate=pl.CostEstimate(
            flops=2 * grid_rows * width * width, bytes_accessed=10 * grid_rows * width, transcendentals=0
        ),
        name="middle",
    )(core, everyone, pred, truth_t, area, var, wout_t, scale, sums, agg, grid_embed)


def scatter_step(slots, gp_ref, lead_ref, idx_ref, hot, prod, acc):
    nodes, half = acc.shape
    wide = lead_ref.shape[0]

    @pl.when(pl.program_id(0) == 0)
    def _():
        acc[...] = jnp.zeros_like(acc)

    node = lax.broadcasted_iota(jnp.int32, (nodes, wide), 0)
    for k in range(slots):
        hot[:, k * wide : (k + 1) * wide] = jnp.where(node == idx_ref[k : k + 1, :], 1.0, 0.0).astype(bf16)
    for start in range(0, wide, TILE):
        lead = lead_ref[start : start + TILE, :]
        for k in range(slots):
            at = start * slots + k * TILE
            to = k * wide + start
            prod[to : to + TILE, :] = gp_ref[at : at + TILE, :] * lead
    for n in range(half // NCOL):
        here = slice(n * NCOL, (n + 1) * NCOL)
        acc[:, here] += jnp.dot(hot[...], prod[:, here], preferred_element_type=f32)


def far_kernel(
    slots, core_ref, gp_ref, lead_ref, idx_ref, below_ref, here_ref, above_ref, wide_ref, part_ref, hot, prod, acc
):
    scatter_step(slots, gp_ref, lead_ref, idx_ref, hot, prod, acc)

    @pl.when(pl.program_id(0) == pl.num_programs(0) - 1)
    def _():
        wide_ref[...] = acc[...].astype(bf16)
        feats = jnp.concatenate([below_ref[...], here_ref[...], above_ref[...]], axis=0)
        part_ref[...] = lax.dot_general(
            feats, wide_ref[...], (((0,), (0,)), ((), ())), preferred_element_type=f32
        ).astype(bf16)


def own_kernel(
    slots,
    place_ref,
    gp_ref,
    lead_ref,
    idx_ref,
    below_ref,
    here_ref,
    above_ref,
    widefar_ref,
    srcfar_ref,
    dstown_ref,
    dstfar_ref,
    lower_ref,
    centre_ref,
    upper_ref,
    total_ref,
    hot,
    prod,
    acc,
):
    core = place_ref[0]
    scatter_step(slots, gp_ref, lead_ref, idx_ref, hot, prod, acc)

    @pl.when(pl.program_id(0) == pl.num_programs(0) - 1)
    def _():
        half = acc.shape[1]
        block = lower_ref.shape[0]
        mine = pl.ds(pl.multiple_of(core * half, half), half)
        other = pl.ds(pl.multiple_of((1 - core) * half, half), half)
        wide = acc[...].astype(bf16)
        for i, ref in enumerate((lower_ref, centre_ref, upper_ref)):
            ref[:, mine] = wide[i * block : (i + 1) * block, :]
            ref[:, other] = widefar_ref[i * block : (i + 1) * block, :]
        feats = jnp.concatenate([below_ref[...], here_ref[...], above_ref[...]], axis=0)
        total = lax.dot_general(
            feats, wide, (((0,), (0,)), ((), ())), preferred_element_type=f32
        )
        width = total_ref.shape[0] * total_ref.shape[1]
        few = (dstown_ref.shape[0] - width) // 2

        def give(columns, values):
            chunks, rows = total_ref.shape[0], total_ref.shape[1] // GROUPS
            for zh in range(GROUPS):
                some = values[zh * chunks * rows : (zh + 1) * chunks * rows, :]
                total_ref[:, zh * rows : (zh + 1) * rows, columns] = some.astype(bf16).reshape(
                    chunks, rows, values.shape[1]
                )

        give(slice(0, half), total + srcfar_ref[...].astype(f32))
        give(
            slice(half, 2 * half),
            dstown_ref[:width, :].astype(f32) + dstfar_ref[:width, :].astype(f32),
        )
        out = dstown_ref[width:, :].astype(f32) + dstfar_ref[width:, :].astype(f32)
        out = jnp.concatenate([out[:few, :], out[few:, :]], axis=1)
        give(slice(2 * half, 2 * half + few), out.T)


def scatter_scratch(slots, nodes, half):
    wide = BACK * TILE * slots
    return [
        pltpu.VMEM((nodes, wide), bf16),
        pltpu.VMEM((wide, half), bf16),
        pltpu.VMEM((nodes, half), f32),
    ]


def scatter_cost(gp):
    return pl.CostEstimate(flops=gp.size * 256, bytes_accessed=gp.size, transcendentals=0)


def backward(kernel, name, column, mine, gp, lead, idx_t, feats, extra, out_shape):
    grid_rows, width = lead.shape
    slots = idx_t.shape[0]
    nodes = 3 * feats[0].shape[0]
    half = width // 2
    rows = BACK * TILE
    half_at = lambda t, core: (t, column(core[0]))
    others = list(feats) + extra
    return pl.pallas_call(
        functools.partial(kernel, slots),
        grid_spec=prefetched(
            grid_rows // rows,
            [
                pl.BlockSpec((rows * slots, half), half_at),
                pl.BlockSpec((rows, half), half_at),
                pl.BlockSpec((slots, rows), lambda t, core: (0, t)),
            ]
            + [whole(x) for x in others],
            [whole(x) for x in out_shape],
            scatter_scratch(slots, nodes, half),
        ),
        out_shape=out_shape,
        compiler_params=params(),
        cost_estimate=scatter_cost(gp),
        name=name,
    )(mine, gp, lead, idx_t, *others)


def backward_far(mine, gp, lead, idx_t, feats):
    half = lead.shape[1] // 2
    out_shape = [
        jax.ShapeDtypeStruct((3 * feats[0].shape[0], half), bf16),
        jax.ShapeDtypeStruct((lead.shape[1], half), bf16),
    ]
    column = lambda core: 1 - core
    return backward(far_kernel, "backward_far", column, mine, gp, lead, idx_t, feats, [], out_shape)


def backward_own(mine, gp, lead, idx_t, feats, wide_far, src_far, dst_own, dst_far, chunks):
    width = lead.shape[1]
    columns = width + (dst_own.shape[0] - width) // 2
    out_shape = [jax.ShapeDtypeStruct((feats[0].shape[0], width), bf16)] * 3 + [
        jax.ShapeDtypeStruct((chunks, width // chunks, columns), bf16)
    ]
    column = lambda core: core
    return backward(
        own_kernel,
        "backward_own",
        column,
        mine,
        gp,
        lead,
        idx_t,
        feats,
        [wide_far, src_far, dst_own, dst_far],
        out_shape,
    )


def body(
    mesh_feats,
    grid_embed,
    w_src,
    w_dst,
    w_out,
    truth,
    area_weight,
    var_weight,
    neighbour,
    edge_mask,
):
    own = mesh_feats[0]
    node_rows, width = own.shape
    grid_rows, slots = neighbour.shape
    half = width // 2
    space_count = lax.axis_size(SPACE)
    block_id = lax.axis_index(SPACE)
    members = lax.axis_size(ENS)
    swap = [(0, 1), (1, 0)]
    core = lax.axis_index("c")
    mine = jnp.full((1,), core, jnp.int32)

    below = shifted(own, SPACE, 1)
    above = shifted(own, SPACE, -1)

    dst = jnp.dot(grid_embed, w_dst, preferred_element_type=f32).astype(bf16)
    local = jnp.mod(neighbour.T - (block_id - 1) * node_rows, node_rows * space_count)
    idx_t = jnp.where(edge_mask.T > 0, local, -1)
    idx = idx_t.T
    scale = 0.5 / jnp.sum(edge_mask.T.astype(f32), axis=0)[:, None]
    wout_t = w_out.T
    truth_t = truth.T
    var = var_weight[:, None]
    area = area_weight[None, :]
    dst, idx, idx_t, scale, wout_t, truth_t, var, area, below = lax.optimization_barrier(
        (dst, idx, idx_t, scale, wout_t, truth_t, var, area, below)
    )
    feats = (below, own, above)
    gp, agg, sums, pred, sent = forward(*feats, w_src, dst, idx, scale, wout_t, members)
    everyone = lax.all_to_all(sent, ENS, 0, 0, tiled=True)
    lead, dst_own, dst_far = middle(
        mine, everyone, pred, truth_t, area, var, wout_t, scale, sums, agg, grid_embed
    )
    dst_far = lax.ppermute(dst_far, "c", swap)
    wide_far, src_far = backward_far(mine, gp, lead, idx_t, feats)
    src_far = lax.ppermute(src_far, "c", swap)
    lower, centre, upper, total = backward_own(
        mine, gp, lead, idx_t, feats, wide_far, src_far, dst_own, dst_far, lax.axis_size(FIRST)
    )
    from_above = shifted(lower, SPACE, -1)
    from_below = shifted(upper, SPACE, 1)

    parts = lax.all_to_all(total, FIRST, 0, 0, tiled=True)
    total = jnp.sum(parts.astype(f32), axis=0).astype(bf16)
    total, from_above, from_below = lax.optimization_barrier((total, from_above, from_below))
    parts = lax.all_to_all(total, SECOND, 0, 0, tiled=True)
    dproj = (centre.astype(f32) + from_above.astype(f32) + from_below.astype(f32)).astype(bf16)
    grad_mesh = lax.dot_general(
        dproj, w_src, (((1,), (1,)), ((), ())), preferred_element_type=f32
    ).astype(bf16)
    rows_out = width // lax.axis_size(ENS + SPACE)
    total = jnp.sum(parts.reshape(-1, 2, rows_out, parts.shape[1]).astype(f32), axis=0)
    joined = lambda a, b: jnp.concatenate([total[0, :, a:b], total[1, :, a:b]], axis=1)
    return (
        grad_mesh[None],
        joined(0, half),
        joined(half, 2 * half),
        joined(2 * half, total.shape[-1]),
    )


def solution(mesh):
    fine = Mesh(mesh.devices.reshape(2, 4, 4, 4, 2), ("zh", "x", "y", "zl", "c"))
    everywhere = ENS + SPACE
    in_specs = (
        P(ENS, SPACE, None),
        P(SPACE, None),
        P(),
        P(),
        P(),
        P(SPACE, None),
        P(SPACE),
        P(),
        P(SPACE, None),
        P(SPACE, None),
    )
    out_specs = (
        P(ENS, SPACE, None),
        P(everywhere, None),
        P(everywhere, None),
        P(everywhere, None),
    )
    return jax.shard_map(body, mesh=fine, in_specs=in_specs, out_specs=out_specs, check_vma=False)
```

```python
import functools
import jax
import jax.numpy as jnp
from jax import lax
from jax.experimental import pallas as pl
from jax.experimental.pallas import tpu as pltpu
from jax.sharding import Mesh, PartitionSpec as P

loss_scale = 8.0
smooth_sq = 0.01
TILE = 64
NCOL = 256
ROWS = 32
GROUP = 4
VMEM_LIMIT = 56 * 1024 * 1024
BACK = 2
GROUPS = 2
f32 = jnp.float32
bf16 = jnp.bfloat16
SPACE = ("y", "zl", "c")
ENS = ("zh", "x")
FIRST = ("x", "y")
SECOND = ("zh", "zl", "c")


def shifted(block, axes, distance):
    count = lax.axis_size(axes)
    return lax.ppermute(block, axes, [(i, (i + distance) % count) for i in range(count)])


def smooth_grad(diff):
    return diff / jnp.sqrt(diff * diff + smooth_sq)


def gelu_parts(v):
    c0 = 0.7978845608
    c1 = c0 * 0.044715
    sq = v * v
    t = jnp.tanh(v * (c0 + c1 * sq))
    u = 1.0 + t
    slope = v * (c0 + (3.0 * c1) * sq)
    return v * u, u * (1.0 + (1.0 - t) * slope)


def whole(array):
    zeros = (0,) * len(array.shape)
    return pl.BlockSpec(array.shape, lambda *_: zeros)


def params():
    return pltpu.CompilerParams(vmem_limit_bytes=VMEM_LIMIT)


def give(ref, columns, values):
    chunks, rows = ref.shape[0], ref.shape[1] // GROUPS
    for zh in range(GROUPS):
        some = values[zh * chunks * rows : (zh + 1) * chunks * rows, :].astype(ref.dtype)
        ref[:, zh * rows : (zh + 1) * rows, columns] = some.reshape(chunks, rows, some.shape[1])


def scale_column(idx_ref):
    used = jnp.sum(jnp.where(idx_ref[...] >= 0, 1.0, 0.0), axis=0, keepdims=True)
    return jnp.broadcast_to(0.5 / used, (8, used.shape[1])).T[:, :1]


def forward_kernel(
    slots,
    members,
    below_ref,
    here_ref,
    above_ref,
    wsrc_ref,
    dst_ref,
    idxt_ref,
    wout_ref,
    gp_ref,
    agg_ref,
    sum_ref,
    pred_ref,
    sent_ref,
    feats,
    rhs,
    hot,
    pre,
    idx_all,
    scale_all,
):
    step = pl.program_id(0)
    nodes, width = feats.shape
    depth = rhs.shape[0]
    tile = depth - nodes
    block = below_ref.shape[0]

    @pl.when(step == 0)
    def _():
        idx_all[...] = idxt_ref[...].astype(f32).T.astype(jnp.int32)
        scale_all[...] = scale_column(idxt_ref)
        for i, ref in enumerate((below_ref, here_ref, above_ref)):
            feats[i * block : (i + 1) * block, :] = ref[...]
        for n in range(width // NCOL):
            cols = slice(n * NCOL, (n + 1) * NCOL)
            rhs[:nodes, cols] = jnp.dot(
                feats[...], wsrc_ref[:, cols], preferred_element_type=f32
            ).astype(bf16)

    base = pl.multiple_of(step * tile, tile)
    rhs[nodes:, :] = dst_ref[...]
    lane = lax.broadcasted_iota(jnp.int32, (tile, depth), 1)
    row = lax.broadcasted_iota(jnp.int32, (tile, depth), 0)
    eye = lane == row + nodes
    idx = idx_all[pl.ds(base, tile), :]
    for k in range(slots):
        col = idx[:, k : k + 1]
        hit = (lane == col) | (eye & (col >= 0))
        hot[k * tile : (k + 1) * tile, :] = jnp.where(hit, 1.0, 0.0).astype(bf16)
    for n in range(width // NCOL):
        cols = slice(n * NCOL, (n + 1) * NCOL)
        pre[n % 2] = jnp.dot(hot[...], rhs[:, cols], preferred_element_type=f32).astype(bf16)
        for r in range(0, tile, ROWS):
            acc_g = jnp.zeros((ROWS, NCOL), f32)
            acc_s = jnp.zeros((ROWS, NCOL), f32)
            for k in range(slots):
                rows = slice(k * tile + r, k * tile + r + ROWS)
                value, grad = gelu_parts(pre[n % 2, rows, :])
                gp_ref[rows, cols] = grad
                if k % GROUP == 0:
                    some_g, some_s = value, grad
                else:
                    some_g, some_s = some_g + value, some_s + grad
                if k % GROUP == GROUP - 1:
                    acc_g = acc_g + some_g.astype(f32)
                    acc_s = acc_s + some_s.astype(f32)
            scale = scale_all[pl.ds(pl.multiple_of(base + r, ROWS), ROWS), :]
            agg_ref[pl.ds(pl.multiple_of(base + r, ROWS), ROWS), cols] = (acc_g * scale).astype(bf16)
            sum_ref[r : r + ROWS, cols] = (acc_s - (slots - 0.5 / scale)).astype(bf16)

    @pl.when(step == pl.num_programs(0) - 1)
    def _():
        pred = lax.dot_general(
            wout_ref[...], agg_ref[...], (((1,), (1,)), ((), ())), preferred_element_type=f32
        )
        pred_ref[...] = pred
        for e in range(members):
            sent_ref[e] = pred.astype(bf16)


def forward(below, here, above, w_src, dst, idx_t, wout_t, members):
    grid_rows, width = dst.shape
    nodes = 3 * here.shape[0]
    slots = idx_t.shape[0]
    outs = wout_t.shape[0]
    step = lambda t: (t, 0)
    out_shape = [
        jax.ShapeDtypeStruct((grid_rows * slots, width), bf16),
        jax.ShapeDtypeStruct((grid_rows, width), bf16),
        jax.ShapeDtypeStruct((grid_rows, width), bf16),
        jax.ShapeDtypeStruct((outs, grid_rows), f32),
        jax.ShapeDtypeStruct((members, outs, grid_rows), bf16),
    ]
    return pl.pallas_call(
        functools.partial(forward_kernel, slots, members),
        grid=(grid_rows // TILE,),
        in_specs=[whole(below), whole(here), whole(above), whole(w_src)]
        + [
            pl.BlockSpec((TILE, width), step),
            whole(idx_t),
            whole(wout_t),
        ],
        out_specs=[
            pl.BlockSpec((TILE * slots, width), step),
            whole(out_shape[1]),
            pl.BlockSpec((TILE, width), step),
            whole(out_shape[3]),
            whole(out_shape[4]),
        ],
        out_shape=out_shape,
        scratch_shapes=[
            pltpu.VMEM((nodes, width), bf16),
            pltpu.VMEM((nodes + TILE, width), bf16),
            pltpu.VMEM((TILE * slots, nodes + TILE), bf16),
            pltpu.VMEM((2, TILE * slots, NCOL), bf16),
            pltpu.VMEM((grid_rows, slots), jnp.int32),
            pltpu.VMEM((grid_rows, 1), f32),
        ],
        compiler_params=params(),
        cost_estimate=pl.CostEstimate(
            flops=2 * grid_rows * slots * 256 * width,
            bytes_accessed=2 * grid_rows * slots * width,
            transcendentals=grid_rows * slots * width,
        ),
        name="forward",
    )(below, here, above, w_src, dst, idx_t, wout_t)


def middle_kernel(
    core_ref,
    every_ref,
    pred_ref,
    truth_ref,
    area_ref,
    var_ref,
    wout_ref,
    idxt_ref,
    sum_ref,
    agg_hbm,
    grid_hbm,
    lead_hbm,
    own_hbm,
    far_hbm,
    agg_ref,
    grid_ref,
    lead_ref,
    own_ref,
    far_ref,
    ddst,
    part,
    sems,
):
    loads = [
        pltpu.make_async_copy(agg_hbm, agg_ref, sems.at[0]),
        pltpu.make_async_copy(grid_hbm, grid_ref, sems.at[1]),
    ]
    stores = [
        pltpu.make_async_copy(lead_ref, lead_hbm, sems.at[2]),
        pltpu.make_async_copy(far_ref, far_hbm, sems.at[3]),
        pltpu.make_async_copy(own_ref, own_hbm, sems.at[4]),
    ]
    for copy in loads:
        copy.start()
    width = sum_ref.shape[1]
    half = width // 2
    members = every_ref.shape[0]
    outs = pred_ref.shape[0]
    core = core_ref[0]

    pred = pred_ref[...]
    pair = -smooth_grad(pred - pred.astype(bf16).astype(f32))
    for e in range(members):
        pair = pair + smooth_grad(pred - every_ref[e].astype(f32))
    weighting = loss_scale * area_ref[...] * var_ref[...]
    dpred = (
        weighting
        * (smooth_grad(pred - truth_ref[...]) / members - pair / (members * (members - 1)))
    ).astype(bf16)
    scale = scale_column(idxt_ref)
    for n in range(width // NCOL):
        cols = slice(n * NCOL, (n + 1) * NCOL)
        dagg = lax.dot_general(
            dpred, wout_ref[:, cols], (((0,), (0,)), ((), ())), preferred_element_type=f32
        )
        dagg = dagg * scale
        lead_ref[:, cols] = dagg.astype(bf16)
        ddst[:, cols] = (dagg * sum_ref[:, cols].astype(f32)).astype(bf16)

    stores[0].start()
    for copy in loads:
        copy.wait()
    mine = pl.ds(pl.multiple_of(core * half, half), half)
    other = pl.ds(pl.multiple_of((1 - core) * half, half), half)
    part[...] = jnp.dot(dpred, agg_ref[...], preferred_element_type=f32)
    few = outs // 2
    for ref, columns, which, store in (
        (far_ref, other, 1 - core, stores[1]),
        (own_ref, mine, core, stores[2]),
    ):
        give(
            ref,
            slice(0, half),
            lax.dot_general(
                grid_ref[...], ddst[:, columns], (((0,), (0,)), ((), ())), preferred_element_type=f32
            ),
        )
        give(ref, slice(half, half + few), part[pl.ds(pl.multiple_of(which * few, few), few), :].T)
        store.start()
    for copy in stores:
        copy.wait()


def prefetched(count, ins, outs, scratch):
    return pltpu.PrefetchScalarGridSpec(
        num_scalar_prefetch=1, grid=(count,), in_specs=ins, out_specs=outs, scratch_shapes=scratch
    )


def middle(core, everyone, pred, truth_t, area, var, wout_t, idx_t, sums, agg, grid_embed, chunks):
    grid_rows, width = sums.shape
    outs = pred.shape[0]
    block = (chunks, width // chunks, (width + outs) // 2)
    anywhere = pl.BlockSpec(memory_space=pl.ANY)
    small = (everyone, pred, truth_t, area, var, wout_t, idx_t, sums)
    return pl.pallas_call(
        middle_kernel,
        grid_spec=prefetched(
            1,
            [whole(x) for x in small] + [anywhere] * 2,
            [anywhere] * 3,
            [
                pltpu.VMEM((grid_rows, width), bf16),
                pltpu.VMEM((grid_rows, width), bf16),
                pltpu.VMEM((grid_rows, width), bf16),
                pltpu.VMEM(block, bf16),
                pltpu.VMEM(block, bf16),
                pltpu.VMEM((grid_rows, width), bf16),
                pltpu.VMEM((outs, width), f32),
                pltpu.SemaphoreType.DMA((5,)),
            ],
        ),
        out_shape=[
            jax.ShapeDtypeStruct((grid_rows, width), bf16),
            jax.ShapeDtypeStruct(block, bf16),
            jax.ShapeDtypeStruct(block, bf16),
        ],
        compiler_params=params(),
        cost_estimate=pl.CostEstimate(
            flops=2 * grid_rows * width * width, bytes_accessed=10 * grid_rows * width, transcendentals=0
        ),
        name="middle",
    )(core, everyone, pred, truth_t, area, var, wout_t, idx_t, sums, agg, grid_embed)


def scatter_step(slots, gp_ref, lead_ref, idx_ref, hot, prod, acc):
    nodes, half = acc.shape
    wide = lead_ref.shape[0]

    @pl.when(pl.program_id(0) == 0)
    def _():
        acc[...] = jnp.zeros_like(acc)

    node = lax.broadcasted_iota(jnp.int32, (nodes, wide), 0)
    for k in range(slots):
        hot[:, k * wide : (k + 1) * wide] = jnp.where(node == idx_ref[k : k + 1, :], 1.0, 0.0).astype(bf16)
    for start in range(0, wide, TILE):
        lead = lead_ref[start : start + TILE, :]
        for k in range(slots):
            at = start * slots + k * TILE
            to = k * wide + start
            prod[to : to + TILE, :] = gp_ref[at : at + TILE, :] * lead
    for n in range(half // NCOL):
        here = slice(n * NCOL, (n + 1) * NCOL)
        acc[:, here] += jnp.dot(hot[...], prod[:, here], preferred_element_type=f32)


def far_kernel(
    slots, core_ref, gp_ref, lead_ref, idx_ref, below_ref, here_ref, above_ref, wide_ref, part_ref, hot, prod, acc
):
    scatter_step(slots, gp_ref, lead_ref, idx_ref, hot, prod, acc)

    @pl.when(pl.program_id(0) == pl.num_programs(0) - 1)
    def _():
        wide_ref[...] = acc[...].astype(bf16)
        feats = jnp.concatenate([below_ref[...], here_ref[...], above_ref[...]], axis=0)
        give(
            part_ref,
            slice(None),
            lax.dot_general(
                feats, wide_ref[...], (((0,), (0,)), ((), ())), preferred_element_type=f32
            ),
        )


def own_kernel(
    slots,
    place_ref,
    gp_ref,
    lead_ref,
    idx_ref,
    below_ref,
    here_ref,
    above_ref,
    widefar_ref,
    lower_ref,
    centre_ref,
    upper_ref,
    total_ref,
    hot,
    prod,
    acc,
):
    core = place_ref[0]
    scatter_step(slots, gp_ref, lead_ref, idx_ref, hot, prod, acc)

    @pl.when(pl.program_id(0) == pl.num_programs(0) - 1)
    def _():
        half = acc.shape[1]
        block = lower_ref.shape[0]
        mine = pl.ds(pl.multiple_of(core * half, half), half)
        other = pl.ds(pl.multiple_of((1 - core) * half, half), half)
        wide = acc[...].astype(bf16)
        for i, ref in enumerate((lower_ref, centre_ref, upper_ref)):
            ref[:, mine] = wide[i * block : (i + 1) * block, :]
            ref[:, other] = widefar_ref[i * block : (i + 1) * block, :]
        feats = jnp.concatenate([below_ref[...], here_ref[...], above_ref[...]], axis=0)
        give(
            total_ref,
            slice(None),
            lax.dot_general(feats, wide, (((0,), (0,)), ((), ())), preferred_element_type=f32),
        )


def scatter_scratch(slots, nodes, half):
    wide = BACK * TILE * slots
    return [
        pltpu.VMEM((nodes, wide), bf16),
        pltpu.VMEM((wide, half), bf16),
        pltpu.VMEM((nodes, half), f32),
    ]


def scatter_cost(gp):
    return pl.CostEstimate(flops=gp.size * 256, bytes_accessed=gp.size, transcendentals=0)


def backward(kernel, name, column, mine, gp, lead, idx_t, feats, extra, out_shape):
    grid_rows, width = lead.shape
    slots = idx_t.shape[0]
    nodes = 3 * feats[0].shape[0]
    half = width // 2
    rows = BACK * TILE
    half_at = lambda t, core: (t, column(core[0]))
    others = list(feats) + extra
    return pl.pallas_call(
        functools.partial(kernel, slots),
        grid_spec=prefetched(
            grid_rows // rows,
            [
                pl.BlockSpec((rows * slots, half), half_at),
                pl.BlockSpec((rows, half), half_at),
                pl.BlockSpec((slots, rows), lambda t, core: (0, t)),
            ]
            + [whole(x) for x in others],
            [whole(x) for x in out_shape],
            scatter_scratch(slots, nodes, half),
        ),
        out_shape=out_shape,
        compiler_params=params(),
        cost_estimate=scatter_cost(gp),
        name=name,
    )(mine, gp, lead, idx_t, *others)


def product_shape(lead, chunks):
    width = lead.shape[1]
    return jax.ShapeDtypeStruct((chunks, width // chunks, width // 2), bf16)


def backward_far(mine, gp, lead, idx_t, feats, chunks):
    half = lead.shape[1] // 2
    out_shape = [
        jax.ShapeDtypeStruct((3 * feats[0].shape[0], half), bf16),
        product_shape(lead, chunks),
    ]
    column = lambda core: 1 - core
    return backward(far_kernel, "backward_far", column, mine, gp, lead, idx_t, feats, [], out_shape)


def backward_own(mine, gp, lead, idx_t, feats, wide_far, chunks):
    out_shape = [jax.ShapeDtypeStruct((feats[0].shape[0], lead.shape[1]), bf16)] * 3 + [
        product_shape(lead, chunks)
    ]
    column = lambda core: core
    return backward(
        own_kernel, "backward_own", column, mine, gp, lead, idx_t, feats, [wide_far], out_shape
    )


def added(a, b):
    return (a.astype(f32) + b.astype(f32)).astype(bf16)


def summed(parts):
    return jnp.sum(parts.astype(f32), axis=0).astype(bf16)


def body(
    mesh_feats,
    grid_embed,
    w_src,
    w_dst,
    w_out,
    truth,
    area_weight,
    var_weight,
    neighbour,
    edge_mask,
):
    own = mesh_feats[0]
    node_rows, width = own.shape
    grid_rows, slots = neighbour.shape
    half = width // 2
    space_count = lax.axis_size(SPACE)
    block_id = lax.axis_index(SPACE)
    members = lax.axis_size(ENS)
    swap = [(0, 1), (1, 0)]
    core = lax.axis_index("c")
    mine = jnp.full((1,), core, jnp.int32)

    below = shifted(own, SPACE, 1)
    above = shifted(own, SPACE, -1)

    dst = jnp.dot(grid_embed, w_dst, preferred_element_type=f32).astype(bf16)
    local = jnp.mod(neighbour.T - (block_id - 1) * node_rows, node_rows * space_count)
    idx_t = jnp.where(edge_mask.T > 0, local, -1)
    wout_t = w_out.T
    truth_t = truth.T
    var = var_weight[:, None]
    area = area_weight[None, :]
    dst, idx_t, below = lax.optimization_barrier((dst, idx_t, below))
    feats = (below, own, above)
    chunks = lax.axis_size(FIRST)
    gp, agg, sums, pred, sent = forward(*feats, w_src, dst, idx_t, wout_t, members)
    everyone = lax.all_to_all(sent, ENS, 0, 0, tiled=True)
    lead, dst_own, dst_far = middle(
        mine, everyone, pred, truth_t, area, var, wout_t, idx_t, sums, agg, grid_embed, chunks
    )
    dst_far = lax.ppermute(dst_far, "c", swap)
    wide_far, src_far = backward_far(mine, gp, lead, idx_t, feats, chunks)
    src_far = lax.ppermute(src_far, "c", swap)

    dst_total = added(dst_own, dst_far)
    lead, dst_total = lax.optimization_barrier((lead, dst_total))
    dst_parts = lax.all_to_all(dst_total, FIRST, 0, 0, tiled=True)
    lower, centre, upper, src_own = backward_own(mine, gp, lead, idx_t, feats, wide_far, chunks)
    src_own, src_far, dst_parts = lax.optimization_barrier((src_own, src_far, dst_parts))
    src_parts = lax.all_to_all(added(src_own, src_far), FIRST, 0, 0, tiled=True)
    from_above = shifted(lower, SPACE, -1)
    from_below = shifted(upper, SPACE, 1)
    total = jnp.concatenate([summed(src_parts), summed(dst_parts)], axis=1)
    total, from_above, from_below = lax.optimization_barrier((total, from_above, from_below))
    parts = lax.all_to_all(total, SECOND, 0, 0, tiled=True)
    dproj = (centre.astype(f32) + from_above.astype(f32) + from_below.astype(f32)).astype(bf16)
    grad_mesh = lax.dot_general(
        dproj, w_src, (((1,), (1,)), ((), ())), preferred_element_type=f32
    ).astype(bf16)
    rows_out = width // lax.axis_size(ENS + SPACE)
    total = jnp.sum(parts.reshape(-1, 2, rows_out, parts.shape[1]).astype(f32), axis=0)
    joined = lambda a, b: jnp.concatenate([total[0, :, a:b], total[1, :, a:b]], axis=1)
    return (
        grad_mesh[None],
        joined(0, half),
        joined(half, 2 * half),
        joined(2 * half, total.shape[-1]),
    )


def solution(mesh):
    fine = Mesh(mesh.devices.reshape(2, 4, 4, 4, 2), ("zh", "x", "y", "zl", "c"))
    everywhere = ENS + SPACE
    in_specs = (
        P(ENS, SPACE, None),
        P(SPACE, None),
        P(),
        P(),
        P(),
        P(SPACE, None),
        P(SPACE),
        P(),
        P(SPACE, None),
        P(SPACE, None),
    )
    out_specs = (
        P(ENS, SPACE, None),
        P(everywhere, None),
        P(everywhere, None),
        P(everywhere, None),
    )
    return jax.shard_map(body, mesh=fine, in_specs=in_specs, out_specs=out_specs, check_vma=False)
```

```python
import functools
import jax
import jax.numpy as jnp
from jax import lax
from jax.experimental import pallas as pl
from jax.experimental.pallas import tpu as pltpu
from jax.sharding import Mesh, PartitionSpec as P

loss_scale = 8.0
smooth_sq = 0.01
TILE = 64
NCOL = 256
ROWS = 32
GROUP = 4
VMEM_LIMIT = 56 * 1024 * 1024
BACK = 2
GROUPS = 2
f32 = jnp.float32
bf16 = jnp.bfloat16
SPACE = ("y", "zl", "c")
ENS = ("zh", "x")
FIRST = ("x", "y")
SECOND = ("zh", "zl", "c")


def shifted(block, axes, distance):
    count = lax.axis_size(axes)
    return lax.ppermute(block, axes, [(i, (i + distance) % count) for i in range(count)])


def smooth_grad(diff):
    return diff / jnp.sqrt(diff * diff + smooth_sq)


def gelu_parts(v):
    c0 = 0.7978845608
    c1 = c0 * 0.044715
    sq = v * v
    t = jnp.tanh(v * (c0 + c1 * sq))
    u = 1.0 + t
    slope = v * (c0 + (3.0 * c1) * sq)
    return v * u, u * (1.0 + (1.0 - t) * slope)


def whole(array):
    zeros = (0,) * len(array.shape)
    return pl.BlockSpec(array.shape, lambda *_: zeros)


def params():
    return pltpu.CompilerParams(vmem_limit_bytes=VMEM_LIMIT)


def give(ref, columns, values):
    chunks, rows = ref.shape[0], ref.shape[1] // GROUPS
    for zh in range(GROUPS):
        some = values[zh * chunks * rows : (zh + 1) * chunks * rows, :].astype(ref.dtype)
        ref[:, zh * rows : (zh + 1) * rows, columns] = some.reshape(chunks, rows, some.shape[1])


def scale_column(idx_ref):
    used = jnp.sum(jnp.where(idx_ref[...] >= 0, 1.0, 0.0), axis=0, keepdims=True)
    return jnp.broadcast_to(0.5 / used, (8, used.shape[1])).T[:, :1]


def forward_kernel(
    slots,
    members,
    below_ref,
    here_ref,
    above_ref,
    wsrc_ref,
    dst_ref,
    idxt_ref,
    wout_ref,
    gp_ref,
    agg_ref,
    sum_ref,
    pred_ref,
    sent_ref,
    feats,
    rhs,
    hot,
    pre,
    idx_all,
    scale_all,
):
    step = pl.program_id(0)
    nodes, width = feats.shape
    depth = rhs.shape[0]
    tile = depth - nodes
    block = below_ref.shape[0]

    @pl.when(step == 0)
    def _():
        idx_all[...] = idxt_ref[...].astype(f32).T.astype(jnp.int32)
        scale_all[...] = scale_column(idxt_ref)
        for i, ref in enumerate((below_ref, here_ref, above_ref)):
            feats[i * block : (i + 1) * block, :] = ref[...]
        for n in range(width // NCOL):
            cols = slice(n * NCOL, (n + 1) * NCOL)
            rhs[:nodes, cols] = jnp.dot(
                feats[...], wsrc_ref[:, cols], preferred_element_type=f32
            ).astype(bf16)

    base = pl.multiple_of(step * tile, tile)
    rhs[nodes:, :] = dst_ref[...]
    lane = lax.broadcasted_iota(jnp.int32, (tile, depth), 1)
    row = lax.broadcasted_iota(jnp.int32, (tile, depth), 0)
    eye = lane == row + nodes
    idx = idx_all[pl.ds(base, tile), :]
    for k in range(slots):
        col = idx[:, k : k + 1]
        hit = (lane == col) | (eye & (col >= 0))
        hot[k * tile : (k + 1) * tile, :] = jnp.where(hit, 1.0, 0.0).astype(bf16)
    for n in range(width // NCOL):
        cols = slice(n * NCOL, (n + 1) * NCOL)
        pre[n % 2] = jnp.dot(hot[...], rhs[:, cols], preferred_element_type=f32).astype(bf16)
        for r in range(0, tile, ROWS):
            acc_g = jnp.zeros((ROWS, NCOL), f32)
            acc_s = jnp.zeros((ROWS, NCOL), f32)
            for k in range(slots):
                rows = slice(k * tile + r, k * tile + r + ROWS)
                value, grad = gelu_parts(pre[n % 2, rows, :])
                gp_ref[rows, cols] = grad
                if k % GROUP == 0:
                    some_g, some_s = value, grad
                else:
                    some_g, some_s = some_g + value, some_s + grad
                if k % GROUP == GROUP - 1:
                    acc_g = acc_g + some_g.astype(f32)
                    acc_s = acc_s + some_s.astype(f32)
            scale = scale_all[pl.ds(pl.multiple_of(base + r, ROWS), ROWS), :]
            agg_ref[pl.ds(pl.multiple_of(base + r, ROWS), ROWS), cols] = (acc_g * scale).astype(bf16)
            sum_ref[n, r : r + ROWS, :] = (acc_s - (slots - 0.5 / scale)).astype(bf16)

    @pl.when(step == pl.num_programs(0) - 1)
    def _():
        pred = lax.dot_general(
            wout_ref[...], agg_ref[...], (((1,), (1,)), ((), ())), preferred_element_type=f32
        )
        pred_ref[...] = pred
        for e in range(members):
            sent_ref[e] = pred.astype(bf16)


def forward(below, here, above, w_src, dst, idx_t, wout_t, members):
    grid_rows, width = dst.shape
    nodes = 3 * here.shape[0]
    slots = idx_t.shape[0]
    outs = wout_t.shape[0]
    step = lambda t: (t, 0)
    out_shape = [
        jax.ShapeDtypeStruct((grid_rows * slots, width), bf16),
        jax.ShapeDtypeStruct((grid_rows, width), bf16),
        jax.ShapeDtypeStruct((width // NCOL, grid_rows, NCOL), bf16),
        jax.ShapeDtypeStruct((outs, grid_rows), f32),
        jax.ShapeDtypeStruct((members, outs, grid_rows), bf16),
    ]
    return pl.pallas_call(
        functools.partial(forward_kernel, slots, members),
        grid=(grid_rows // TILE,),
        in_specs=[whole(below), whole(here), whole(above), whole(w_src)]
        + [
            pl.BlockSpec((TILE, width), step),
            whole(idx_t),
            whole(wout_t),
        ],
        out_specs=[
            pl.BlockSpec((TILE * slots, width), step),
            whole(out_shape[1]),
            pl.BlockSpec((width // NCOL, TILE, NCOL), lambda t: (0, t, 0)),
            whole(out_shape[3]),
            whole(out_shape[4]),
        ],
        out_shape=out_shape,
        scratch_shapes=[
            pltpu.VMEM((nodes, width), bf16),
            pltpu.VMEM((nodes + TILE, width), bf16),
            pltpu.VMEM((TILE * slots, nodes + TILE), bf16),
            pltpu.VMEM((2, TILE * slots, NCOL), bf16),
            pltpu.VMEM((grid_rows, slots), jnp.int32),
            pltpu.VMEM((grid_rows, 1), f32),
        ],
        compiler_params=params(),
        cost_estimate=pl.CostEstimate(
            flops=2 * grid_rows * slots * 256 * width,
            bytes_accessed=2 * grid_rows * slots * width,
            transcendentals=grid_rows * slots * width,
        ),
        name="forward",
    )(below, here, above, w_src, dst, idx_t, wout_t)


def middle_kernel(
    place_ref,
    every_ref,
    pred_ref,
    truth_ref,
    area_ref,
    var_ref,
    wout_ref,
    idxt_ref,
    sum_ref,
    agg_hbm,
    grid_hbm,
    lead_hbm,
    own_ref,
    far_ref,
    part_ref,
    agg_ref,
    grid_ref,
    lead_ref,
    ddst,
    sems,
):
    loads = [
        pltpu.make_async_copy(agg_hbm, agg_ref, sems.at[0]),
        pltpu.make_async_copy(grid_hbm, grid_ref, sems.at[1]),
    ]
    store = pltpu.make_async_copy(lead_ref, lead_hbm, sems.at[2])
    for copy in loads:
        copy.start()
    width = wout_ref.shape[1]
    members = every_ref.shape[0]
    near, columns = sum_ref.shape[0], sum_ref.shape[2]
    core, x, zh = place_ref[0], place_ref[1], place_ref[2]
    weighting = loss_scale * area_ref[...] * var_ref[...]

    def dpred_of(pred):
        pair = -smooth_grad(pred - pred.astype(bf16).astype(f32))
        for e in range(members):
            pair = pair + smooth_grad(pred - every_ref[e].astype(f32))
        against = smooth_grad(pred - truth_ref[...]) / members
        return (weighting * (against - pair / (members * (members - 1)))).astype(bf16)

    scale = scale_column(idxt_ref)
    first = (((0,), (0,)), ((), ()))
    dpred = dpred_of(pred_ref[...])
    for n in range(width // NCOL):
        cols = slice(n * NCOL, (n + 1) * NCOL)
        dagg = lax.dot_general(dpred, wout_ref[:, cols], first, preferred_element_type=f32)
        lead_ref[:, cols] = (dagg * scale).astype(bf16)
    store.start()

    quarter = wout_ref[:, pl.ds(pl.multiple_of(x * columns, columns), columns)]
    total = jnp.zeros((sum_ref.shape[1], columns), f32)
    for m in range(near):
        other = dpred_of(every_ref[zh * near + m].astype(f32))
        dagg = lax.dot_general(other, quarter, first, preferred_element_type=f32)
        total = total + dagg * sum_ref[m].astype(f32)
    ddst[...] = (total * scale).astype(bf16)

    for copy in loads:
        copy.wait()
    part_ref[...] = jnp.dot(dpred, agg_ref[...], preferred_element_type=f32)
    few = own_ref.shape[1]
    for ref, which in ((far_ref, 1 - core), (own_ref, core)):
        ref[...] = lax.dot_general(
            grid_ref[...],
            ddst[:, pl.ds(pl.multiple_of(which * few, few), few)],
            first,
            preferred_element_type=f32,
        ).astype(bf16)
    store.wait()


def prefetched(count, ins, outs, scratch):
    return pltpu.PrefetchScalarGridSpec(
        num_scalar_prefetch=1, grid=(count,), in_specs=ins, out_specs=outs, scratch_shapes=scratch
    )


def middle(place, everyone, pred, truth_t, area, var, wout_t, idx_t, sums, agg, grid_embed):
    grid_rows, width = agg.shape
    columns = sums.shape[2]
    anywhere = pl.BlockSpec(memory_space=pl.ANY)
    small = (everyone, pred, truth_t, area, var, wout_t, idx_t, sums)
    out_shape = [
        jax.ShapeDtypeStruct((grid_rows, width), bf16),
        jax.ShapeDtypeStruct((width, columns // 2), bf16),
        jax.ShapeDtypeStruct((width, columns // 2), bf16),
        jax.ShapeDtypeStruct(wout_t.shape, f32),
    ]
    return pl.pallas_call(
        middle_kernel,
        grid_spec=prefetched(
            1,
            [whole(x) for x in small] + [anywhere] * 2,
            [anywhere] + [whole(x) for x in out_shape[1:]],
            [
                pltpu.VMEM((grid_rows, width), bf16),
                pltpu.VMEM((grid_rows, width), bf16),
                pltpu.VMEM((grid_rows, width), bf16),
                pltpu.VMEM((grid_rows, columns), bf16),
                pltpu.SemaphoreType.DMA((3,)),
            ],
        ),
        out_shape=out_shape,
        compiler_params=params(),
        cost_estimate=pl.CostEstimate(
            flops=grid_rows * width * width, bytes_accessed=10 * grid_rows * width, transcendentals=0
        ),
        name="middle",
    )(place, everyone, pred, truth_t, area, var, wout_t, idx_t, sums, agg, grid_embed)


def scatter_step(slots, gp_ref, lead_ref, idx_ref, hot, prod, acc):
    nodes, half = acc.shape
    wide = lead_ref.shape[0]

    @pl.when(pl.program_id(0) == 0)
    def _():
        acc[...] = jnp.zeros_like(acc)

    node = lax.broadcasted_iota(jnp.int32, (nodes, wide), 0)
    for k in range(slots):
        hot[:, k * wide : (k + 1) * wide] = jnp.where(node == idx_ref[k : k + 1, :], 1.0, 0.0).astype(bf16)
    for start in range(0, wide, TILE):
        lead = lead_ref[start : start + TILE, :]
        for k in range(slots):
            at = start * slots + k * TILE
            to = k * wide + start
            prod[to : to + TILE, :] = gp_ref[at : at + TILE, :] * lead
    for n in range(half // NCOL):
        here = slice(n * NCOL, (n + 1) * NCOL)
        acc[:, here] += jnp.dot(hot[...], prod[:, here], preferred_element_type=f32)


def joined_feats(below_ref, here_ref, above_ref):
    return jnp.concatenate([below_ref[...], here_ref[...], above_ref[...]], axis=0)


def out_columns(part_ref, which):
    few = part_ref.shape[0] // 2
    return part_ref[pl.ds(pl.multiple_of(which * few, few), few), :].T


def far_kernel(
    slots,
    place_ref,
    gp_ref,
    lead_ref,
    idx_ref,
    below_ref,
    here_ref,
    above_ref,
    part_ref,
    wide_ref,
    far_ref,
    hot,
    prod,
    acc,
):
    scatter_step(slots, gp_ref, lead_ref, idx_ref, hot, prod, acc)

    @pl.when(pl.program_id(0) == pl.num_programs(0) - 1)
    def _():
        half = acc.shape[1]
        wide_ref[...] = acc[...].astype(bf16)
        feats = joined_feats(below_ref, here_ref, above_ref)
        product = lax.dot_general(
            feats, wide_ref[...], (((0,), (0,)), ((), ())), preferred_element_type=f32
        )
        give(far_ref, slice(0, half), product)
        give(far_ref, slice(half, far_ref.shape[2]), out_columns(part_ref, 1 - place_ref[0]))


def own_kernel(
    slots,
    place_ref,
    gp_ref,
    lead_ref,
    idx_ref,
    widefar_ref,
    lower_ref,
    centre_ref,
    upper_ref,
    wide_ref,
    hot,
    prod,
    acc,
):
    core = place_ref[0]
    scatter_step(slots, gp_ref, lead_ref, idx_ref, hot, prod, acc)

    @pl.when(pl.program_id(0) == pl.num_programs(0) - 1)
    def _():
        half = acc.shape[1]
        block = lower_ref.shape[0]
        mine = pl.ds(pl.multiple_of(core * half, half), half)
        other = pl.ds(pl.multiple_of((1 - core) * half, half), half)
        wide = acc[...].astype(bf16)
        wide_ref[...] = wide
        for i, ref in enumerate((lower_ref, centre_ref, upper_ref)):
            ref[:, mine] = wide[i * block : (i + 1) * block, :]
            ref[:, other] = widefar_ref[i * block : (i + 1) * block, :]


def pack_kernel(place_ref, below_ref, here_ref, above_ref, wide_ref, part_ref, far_ref, total_ref):
    half = wide_ref.shape[1]
    feats = joined_feats(below_ref, here_ref, above_ref)
    product = lax.dot_general(
        feats, wide_ref[...], (((0,), (0,)), ((), ())), preferred_element_type=f32
    )
    chunks, rows = total_ref.shape[0], total_ref.shape[1] // GROUPS
    columns = out_columns(part_ref, place_ref[0])
    for zh in range(GROUPS):
        here = slice(zh * rows, (zh + 1) * rows)
        for values, at in (
            (product, slice(0, half)),
            (columns, slice(half, total_ref.shape[2])),
        ):
            some = values[zh * chunks * rows : (zh + 1) * chunks * rows, :]
            some = some.reshape(chunks, rows, some.shape[1])
            total_ref[:, here, at] = (some + far_ref[:, here, at].astype(f32)).astype(bf16)


def pack(place, feats, wide, part, far):
    ins = list(feats) + [wide, part, far]
    return pl.pallas_call(
        pack_kernel,
        grid_spec=prefetched(1, [whole(x) for x in ins], whole(far), []),
        out_shape=jax.ShapeDtypeStruct(far.shape, bf16),
        compiler_params=params(),
        cost_estimate=pl.CostEstimate(
            flops=2 * far.size * wide.shape[0], bytes_accessed=4 * far.size, transcendentals=0
        ),
        name="pack",
    )(place, *ins)


def scatter_scratch(slots, nodes, half):
    wide = BACK * TILE * slots
    return [
        pltpu.VMEM((nodes, wide), bf16),
        pltpu.VMEM((wide, half), bf16),
        pltpu.VMEM((nodes, half), f32),
    ]


def scatter_cost(gp):
    return pl.CostEstimate(flops=gp.size * 256, bytes_accessed=gp.size, transcendentals=0)


def backward(kernel, name, column, place, gp, lead, idx_t, others, out_shape):
    grid_rows, width = lead.shape
    slots = idx_t.shape[0]
    half = width // 2
    nodes = out_shape[-1].shape[0] if kernel is own_kernel else out_shape[0].shape[0]
    rows = BACK * TILE
    half_at = lambda t, place: (t, column(place[0]))
    return pl.pallas_call(
        functools.partial(kernel, slots),
        grid_spec=prefetched(
            grid_rows // rows,
            [
                pl.BlockSpec((rows * slots, half), half_at),
                pl.BlockSpec((rows, half), half_at),
                pl.BlockSpec((slots, rows), lambda t, place: (0, t)),
            ]
            + [whole(x) for x in others],
            [whole(x) for x in out_shape],
            scatter_scratch(slots, nodes, half),
        ),
        out_shape=out_shape,
        compiler_params=params(),
        cost_estimate=scatter_cost(gp),
        name=name,
    )(place, gp, lead, idx_t, *others)


def backward_far(place, gp, lead, idx_t, feats, part, chunks):
    width = lead.shape[1]
    half = width // 2
    out_shape = [
        jax.ShapeDtypeStruct((3 * feats[0].shape[0], half), bf16),
        jax.ShapeDtypeStruct((chunks, width // chunks, half + part.shape[0] // 2), bf16),
    ]
    column = lambda core: 1 - core
    others = list(feats) + [part]
    return backward(far_kernel, "backward_far", column, place, gp, lead, idx_t, others, out_shape)


def backward_own(place, gp, lead, idx_t, wide_far):
    nodes, half = wide_far.shape
    out_shape = [jax.ShapeDtypeStruct((nodes // 3, 2 * half), bf16)] * 3 + [
        jax.ShapeDtypeStruct((nodes, half), bf16)
    ]
    column = lambda core: core
    return backward(own_kernel, "backward_own", column, place, gp, lead, idx_t, [wide_far], out_shape)


def added(a, b):
    return (a.astype(f32) + b.astype(f32)).astype(bf16)


def summed(parts):
    return jnp.sum(parts.astype(f32), axis=0).astype(bf16)


def body(
    mesh_feats,
    grid_embed,
    w_src,
    w_dst,
    w_out,
    truth,
    area_weight,
    var_weight,
    neighbour,
    edge_mask,
):
    own = mesh_feats[0]
    node_rows, width = own.shape
    grid_rows, slots = neighbour.shape
    half = width // 2
    space_count = lax.axis_size(SPACE)
    block_id = lax.axis_index(SPACE)
    members = lax.axis_size(ENS)
    swap = [(0, 1), (1, 0)]
    here = [lax.axis_index(name) for name in ("c", "x", "zh")]
    place = jnp.stack(here).astype(jnp.int32)

    below = shifted(own, SPACE, 1)
    above = shifted(own, SPACE, -1)

    dst = jnp.dot(grid_embed, w_dst, preferred_element_type=f32).astype(bf16)
    local = jnp.mod(neighbour.T - (block_id - 1) * node_rows, node_rows * space_count)
    idx_t = jnp.where(edge_mask.T > 0, local, -1)
    wout_t = w_out.T
    truth_t = truth.T
    var = var_weight[:, None]
    area = area_weight[None, :]
    dst, idx_t, below = lax.optimization_barrier((dst, idx_t, below))
    feats = (below, own, above)
    chunks = lax.axis_size(FIRST)
    gp, agg, sums, pred, sent = forward(*feats, w_src, dst, idx_t, wout_t, members)
    everyone = lax.all_to_all(sent, ENS, 0, 0, tiled=True)
    sums = lax.all_to_all(sums, "x", 0, 0, tiled=True)
    lead, dst_own, dst_far, part = middle(
        place, everyone, pred, truth_t, area, var, wout_t, idx_t, sums, agg, grid_embed
    )
    dst_far = lax.ppermute(dst_far, "c", swap)
    wide_far, src_far = backward_far(place, gp, lead, idx_t, feats, part, chunks)
    src_far = lax.ppermute(src_far, "c", swap)
    lower, centre, upper, wide_own = backward_own(place, gp, lead, idx_t, wide_far)
    from_above = shifted(lower, SPACE, -1)
    from_below = shifted(upper, SPACE, 1)

    src_total = pack(place, feats, wide_own, part, src_far)
    src_parts = lax.all_to_all(src_total, FIRST, 0, 0, tiled=True)
    src_total, dst_own, dst_far = lax.optimization_barrier((src_total, dst_own, dst_far))
    dst_parts = lax.all_to_all(added(dst_own, dst_far), ENS + SPACE, 0, 0, tiled=True)
    total = summed(src_parts)
    total, dst_parts, from_above, from_below = lax.optimization_barrier(
        (total, dst_parts, from_above, from_below)
    )
    parts = lax.all_to_all(total, SECOND, 0, 0, tiled=True)
    dproj = (centre.astype(f32) + from_above.astype(f32) + from_below.astype(f32)).astype(bf16)
    grad_mesh = lax.dot_general(
        dproj, w_src, (((1,), (1,)), ((), ())), preferred_element_type=f32
    ).astype(bf16)
    rows_out = width // lax.axis_size(ENS + SPACE)
    total = jnp.sum(parts.reshape(-1, 2, rows_out, parts.shape[1]).astype(f32), axis=0)
    joined = lambda a, b: jnp.concatenate([total[0, :, a:b], total[1, :, a:b]], axis=1)
    sizes = [lax.axis_size(name) for name in ENS + SPACE]
    dst_parts = dst_parts.reshape(*sizes, rows_out, dst_parts.shape[1])
    dst_final = jnp.sum(dst_parts.astype(f32), axis=(0, 2, 3))
    dst_final = dst_final.transpose(2, 0, 1, 3).reshape(rows_out, width)
    return (
        grad_mesh[None],
        joined(0, half),
        dst_final,
        joined(half, total.shape[-1]),
    )


def solution(mesh):
    fine = Mesh(mesh.devices.reshape(2, 4, 4, 4, 2), ("zh", "x", "y", "zl", "c"))
    everywhere = ENS + SPACE
    in_specs = (
        P(ENS, SPACE, None),
        P(SPACE, None),
        P(),
        P(),
        P(),
        P(SPACE, None),
        P(SPACE),
        P(),
        P(SPACE, None),
        P(SPACE, None),
    )
    out_specs = (
        P(ENS, SPACE, None),
        P(everywhere, None),
        P(everywhere, None),
        P(everywhere, None),
    )
    return jax.shard_map(body, mesh=fine, in_specs=in_specs, out_specs=out_specs, check_vma=False)
```

```python
import functools
import jax
import jax.numpy as jnp
from jax import lax
from jax.experimental import pallas as pl
from jax.experimental.pallas import tpu as pltpu
from jax.sharding import Mesh, PartitionSpec as P

loss_scale = 8.0
smooth_sq = 0.01
TILE = 64
NCOL = 256
ROWS = 32
GROUP = 4
VMEM_LIMIT = 56 * 1024 * 1024
BACK = 2
GROUPS = 2
QUARTERS = 4
f32 = jnp.float32
bf16 = jnp.bfloat16
SPACE = ("y", "zl", "c")
ENS = ("zh", "x")
FIRST = ("x", "y")
SECOND = ("zh", "zl", "c")


def shifted(block, axes, distance):
    count = lax.axis_size(axes)
    return lax.ppermute(block, axes, [(i, (i + distance) % count) for i in range(count)])


def smooth_grad(diff):
    return diff / jnp.sqrt(diff * diff + smooth_sq)


def gelu_parts(v):
    c0 = 0.7978845608
    c1 = c0 * 0.044715
    sq = v * v
    t = jnp.tanh(v * (c0 + c1 * sq))
    u = 1.0 + t
    slope = v * (c0 + (3.0 * c1) * sq)
    return v * u, u * (1.0 + (1.0 - t) * slope)


def whole(array):
    zeros = (0,) * len(array.shape)
    return pl.BlockSpec(array.shape, lambda *_: zeros)


def params():
    return pltpu.CompilerParams(vmem_limit_bytes=VMEM_LIMIT)


def give(ref, columns, values):
    chunks, rows = ref.shape[0], ref.shape[1] // GROUPS
    for zh in range(GROUPS):
        some = values[zh * chunks * rows : (zh + 1) * chunks * rows, :].astype(ref.dtype)
        ref[:, zh * rows : (zh + 1) * rows, columns] = some.reshape(chunks, rows, some.shape[1])


def scale_column(idx_ref):
    used = jnp.sum(jnp.where(idx_ref[...] >= 0, 1.0, 0.0), axis=0, keepdims=True)
    return jnp.broadcast_to(0.5 / used, (8, used.shape[1])).T[:, :1]


def forward_kernel(
    slots,
    members,
    place_ref,
    below_ref,
    here_ref,
    above_ref,
    wsrc_ref,
    dst_ref,
    idxt_ref,
    wout_ref,
    gp_ref,
    agg_ref,
    pred_ref,
    sent_ref,
    *rest,
):
    piece_refs = rest[:QUARTERS]
    forward_steps(
        slots,
        members,
        place_ref[1],
        (below_ref, here_ref, above_ref),
        wsrc_ref,
        dst_ref,
        idxt_ref,
        wout_ref,
        gp_ref,
        agg_ref,
        pred_ref,
        sent_ref,
        piece_refs,
        *rest[QUARTERS:],
    )


def forward_steps(
    slots,
    members,
    along,
    feat_refs,
    wsrc_ref,
    dst_ref,
    idxt_ref,
    wout_ref,
    gp_ref,
    agg_ref,
    pred_ref,
    sent_ref,
    piece_refs,
    feats,
    rhs,
    hot,
    pre,
    idx_all,
    scale_all,
    sums,
):
    step = pl.program_id(0)
    nodes, width = feats.shape
    depth = rhs.shape[0]
    tile = depth - nodes
    block = feat_refs[0].shape[0]

    @pl.when(step == 0)
    def _():
        idx_all[...] = idxt_ref[...].astype(f32).T.astype(jnp.int32)
        scale_all[...] = scale_column(idxt_ref)
        for i, ref in enumerate(feat_refs):
            feats[i * block : (i + 1) * block, :] = ref[...]
        for n in range(width // NCOL):
            cols = slice(n * NCOL, (n + 1) * NCOL)
            rhs[:nodes, cols] = jnp.dot(
                feats[...], wsrc_ref[:, cols], preferred_element_type=f32
            ).astype(bf16)

    base = pl.multiple_of(step * tile, tile)
    rhs[nodes:, :] = dst_ref[...]
    lane = lax.broadcasted_iota(jnp.int32, (tile, depth), 1)
    row = lax.broadcasted_iota(jnp.int32, (tile, depth), 0)
    eye = lane == row + nodes
    idx = idx_all[pl.ds(base, tile), :]
    for k in range(slots):
        col = idx[:, k : k + 1]
        hit = (lane == col) | (eye & (col >= 0))
        hot[k * tile : (k + 1) * tile, :] = jnp.where(hit, 1.0, 0.0).astype(bf16)
    for n in range(width // NCOL):
        cols = slice(n * NCOL, (n + 1) * NCOL)
        pre[n % 2] = jnp.dot(hot[...], rhs[:, cols], preferred_element_type=f32).astype(bf16)
        for r in range(0, tile, ROWS):
            acc_g = jnp.zeros((ROWS, NCOL), f32)
            acc_s = jnp.zeros((ROWS, NCOL), f32)
            for k in range(slots):
                rows = slice(k * tile + r, k * tile + r + ROWS)
                value, grad = gelu_parts(pre[n % 2, rows, :])
                gp_ref[rows, cols] = grad
                if k % GROUP == 0:
                    some_g, some_s = value, grad
                else:
                    some_g, some_s = some_g + value, some_s + grad
                if k % GROUP == GROUP - 1:
                    acc_g = acc_g + some_g.astype(f32)
                    acc_s = acc_s + some_s.astype(f32)
            scale = scale_all[pl.ds(pl.multiple_of(base + r, ROWS), ROWS), :]
            agg_ref[pl.ds(pl.multiple_of(base + r, ROWS), ROWS), cols] = (acc_g * scale).astype(bf16)
            sums[n, pl.ds(pl.multiple_of(base + r, ROWS), ROWS), :] = (
                acc_s - (slots - 0.5 / scale)
            ).astype(bf16)

    @pl.when(step == pl.num_programs(0) - 1)
    def _():
        pred = lax.dot_general(
            wout_ref[...], agg_ref[...], (((1,), (1,)), ((), ())), preferred_element_type=f32
        )
        pred_ref[...] = pred
        for e in range(members):
            sent_ref[e] = pred.astype(bf16)
        for d, ref in enumerate(piece_refs):
            ref[...] = sums[(along + d) % QUARTERS]


def forward(place, below, here, above, w_src, dst, idx_t, wout_t, members):
    grid_rows, width = dst.shape
    nodes = 3 * here.shape[0]
    slots = idx_t.shape[0]
    outs = wout_t.shape[0]
    step = lambda t, place: (t, 0)
    out_shape = [
        jax.ShapeDtypeStruct((grid_rows * slots, width), bf16),
        jax.ShapeDtypeStruct((grid_rows, width), bf16),
        jax.ShapeDtypeStruct((outs, grid_rows), f32),
        jax.ShapeDtypeStruct((members, outs, grid_rows), bf16),
    ] + [jax.ShapeDtypeStruct((grid_rows, NCOL), bf16)] * QUARTERS
    return pl.pallas_call(
        functools.partial(forward_kernel, slots, members),
        grid_spec=prefetched(
            grid_rows // TILE,
            [whole(below), whole(here), whole(above), whole(w_src)]
            + [pl.BlockSpec((TILE, width), step), whole(idx_t), whole(wout_t)],
            [pl.BlockSpec((TILE * slots, width), step)] + [whole(x) for x in out_shape[1:]],
            [
                pltpu.VMEM((nodes, width), bf16),
                pltpu.VMEM((nodes + TILE, width), bf16),
                pltpu.VMEM((TILE * slots, nodes + TILE), bf16),
                pltpu.VMEM((2, TILE * slots, NCOL), bf16),
                pltpu.VMEM((grid_rows, slots), jnp.int32),
                pltpu.VMEM((grid_rows, 1), f32),
                pltpu.VMEM((QUARTERS, grid_rows, NCOL), bf16),
            ],
        ),
        out_shape=out_shape,
        compiler_params=params(),
        cost_estimate=pl.CostEstimate(
            flops=2 * grid_rows * slots * 256 * width,
            bytes_accessed=2 * grid_rows * slots * width,
            transcendentals=grid_rows * slots * width,
        ),
        name="forward",
    )(place, below, here, above, w_src, dst, idx_t, wout_t)


def middle_kernel(
    place_ref,
    every_ref,
    pred_ref,
    truth_ref,
    area_ref,
    var_ref,
    wout_ref,
    idxt_ref,
    sum0_ref,
    sum1_ref,
    sum2_ref,
    sum3_ref,
    agg_hbm,
    grid_hbm,
    lead_hbm,
    own_ref,
    far_ref,
    part_ref,
    agg_ref,
    grid_ref,
    lead_ref,
    ddst,
    sems,
):
    loads = [
        pltpu.make_async_copy(agg_hbm, agg_ref, sems.at[0]),
        pltpu.make_async_copy(grid_hbm, grid_ref, sems.at[1]),
    ]
    store = pltpu.make_async_copy(lead_ref, lead_hbm, sems.at[2])
    for copy in loads:
        copy.start()
    width = wout_ref.shape[1]
    members = every_ref.shape[0]
    near, columns = QUARTERS, sum0_ref.shape[1]
    core, x, zh = place_ref[0], place_ref[1], place_ref[2]
    weighting = loss_scale * area_ref[...] * var_ref[...]

    def dpred_of(pred):
        pair = -smooth_grad(pred - pred.astype(bf16).astype(f32))
        for e in range(members):
            pair = pair + smooth_grad(pred - every_ref[e].astype(f32))
        against = smooth_grad(pred - truth_ref[...]) / members
        return (weighting * (against - pair / (members * (members - 1)))).astype(bf16)

    scale = scale_column(idxt_ref)
    first = (((0,), (0,)), ((), ()))
    dpred = dpred_of(pred_ref[...])
    for n in range(width // NCOL):
        cols = slice(n * NCOL, (n + 1) * NCOL)
        dagg = lax.dot_general(dpred, wout_ref[:, cols], first, preferred_element_type=f32)
        lead_ref[:, cols] = (dagg * scale).astype(bf16)
    store.start()

    quarter = wout_ref[:, pl.ds(pl.multiple_of(x * columns, columns), columns)]
    total = jnp.zeros(sum0_ref.shape, f32)
    for d, sum_ref in enumerate((sum0_ref, sum1_ref, sum2_ref, sum3_ref)):
        other = dpred_of(every_ref[zh * near + (x + near - d) % near].astype(f32))
        dagg = lax.dot_general(other, quarter, first, preferred_element_type=f32)
        total = total + dagg * sum_ref[...].astype(f32)
    ddst[...] = (total * scale).astype(bf16)

    for copy in loads:
        copy.wait()
    part_ref[...] = jnp.dot(dpred, agg_ref[...], preferred_element_type=f32)
    few = own_ref.shape[-1]
    for ref, which in ((far_ref, 1 - core), (own_ref, core)):
        product = lax.dot_general(
            grid_ref[...],
            ddst[:, pl.ds(pl.multiple_of(which * few, few), few)],
            first,
            preferred_element_type=f32,
        )
        ref[...] = product.astype(bf16).reshape(ref.shape)
    store.wait()


def prefetched(count, ins, outs, scratch):
    return pltpu.PrefetchScalarGridSpec(
        num_scalar_prefetch=1, grid=(count,), in_specs=ins, out_specs=outs, scratch_shapes=scratch
    )


def middle(place, everyone, pred, truth_t, area, var, wout_t, idx_t, sums, agg, grid_embed):
    grid_rows, width = agg.shape
    columns = sums[0].shape[1]
    along = lax.axis_size("y")
    product = (QUARTERS * GROUPS, along, width // (QUARTERS * GROUPS * along), columns // 2)
    anywhere = pl.BlockSpec(memory_space=pl.ANY)
    small = (everyone, pred, truth_t, area, var, wout_t, idx_t, *sums)
    out_shape = [
        jax.ShapeDtypeStruct((grid_rows, width), bf16),
        jax.ShapeDtypeStruct(product, bf16),
        jax.ShapeDtypeStruct(product, bf16),
        jax.ShapeDtypeStruct(wout_t.shape, f32),
    ]
    return pl.pallas_call(
        middle_kernel,
        grid_spec=prefetched(
            1,
            [whole(x) for x in small] + [anywhere] * 2,
            [anywhere] + [whole(x) for x in out_shape[1:]],
            [
                pltpu.VMEM((grid_rows, width), bf16),
                pltpu.VMEM((grid_rows, width), bf16),
                pltpu.VMEM((grid_rows, width), bf16),
                pltpu.VMEM((grid_rows, columns), bf16),
                pltpu.SemaphoreType.DMA((3,)),
            ],
        ),
        out_shape=out_shape,
        compiler_params=params(),
        cost_estimate=pl.CostEstimate(
            flops=grid_rows * width * width, bytes_accessed=10 * grid_rows * width, transcendentals=0
        ),
        name="middle",
    )(place, *small, agg, grid_embed)


def scatter_step(slots, gp_ref, lead_ref, idx_ref, hot, prod, acc):
    nodes, half = acc.shape
    wide = lead_ref.shape[0]

    @pl.when(pl.program_id(0) == 0)
    def _():
        acc[...] = jnp.zeros_like(acc)

    node = lax.broadcasted_iota(jnp.int32, (nodes, wide), 0)
    for k in range(slots):
        hot[:, k * wide : (k + 1) * wide] = jnp.where(node == idx_ref[k : k + 1, :], 1.0, 0.0).astype(bf16)
    for start in range(0, wide, TILE):
        lead = lead_ref[start : start + TILE, :]
        for k in range(slots):
            at = start * slots + k * TILE
            to = k * wide + start
            prod[to : to + TILE, :] = gp_ref[at : at + TILE, :] * lead
    for n in range(half // NCOL):
        here = slice(n * NCOL, (n + 1) * NCOL)
        acc[:, here] += jnp.dot(hot[...], prod[:, here], preferred_element_type=f32)


def joined_feats(below_ref, here_ref, above_ref):
    return jnp.concatenate([below_ref[...], here_ref[...], above_ref[...]], axis=0)


def out_columns(part_ref, which):
    few = part_ref.shape[0] // 2
    return part_ref[pl.ds(pl.multiple_of(which * few, few), few), :].T


def far_kernel(
    slots,
    place_ref,
    gp_ref,
    lead_ref,
    idx_ref,
    below_ref,
    here_ref,
    above_ref,
    part_ref,
    wide_ref,
    far_ref,
    hot,
    prod,
    acc,
):
    scatter_step(slots, gp_ref, lead_ref, idx_ref, hot, prod, acc)

    @pl.when(pl.program_id(0) == pl.num_programs(0) - 1)
    def _():
        half = acc.shape[1]
        wide_ref[...] = acc[...].astype(bf16)
        feats = joined_feats(below_ref, here_ref, above_ref)
        product = lax.dot_general(
            feats, wide_ref[...], (((0,), (0,)), ((), ())), preferred_element_type=f32
        )
        give(far_ref, slice(0, half), product)
        give(far_ref, slice(half, far_ref.shape[2]), out_columns(part_ref, 1 - place_ref[0]))


def own_kernel(
    slots,
    place_ref,
    gp_ref,
    lead_ref,
    idx_ref,
    widefar_ref,
    lower_ref,
    centre_ref,
    upper_ref,
    wide_ref,
    hot,
    prod,
    acc,
):
    core = place_ref[0]
    scatter_step(slots, gp_ref, lead_ref, idx_ref, hot, prod, acc)

    @pl.when(pl.program_id(0) == pl.num_programs(0) - 1)
    def _():
        half = acc.shape[1]
        block = lower_ref.shape[0]
        mine = pl.ds(pl.multiple_of(core * half, half), half)
        other = pl.ds(pl.multiple_of((1 - core) * half, half), half)
        wide = acc[...].astype(bf16)
        wide_ref[...] = wide
        for i, ref in enumerate((lower_ref, centre_ref, upper_ref)):
            ref[:, mine] = wide[i * block : (i + 1) * block, :]
            ref[:, other] = widefar_ref[i * block : (i + 1) * block, :]


def pack_kernel(place_ref, below_ref, here_ref, above_ref, wide_ref, part_ref, far_ref, total_ref):
    half = wide_ref.shape[1]
    feats = joined_feats(below_ref, here_ref, above_ref)
    product = lax.dot_general(
        feats, wide_ref[...], (((0,), (0,)), ((), ())), preferred_element_type=f32
    )
    chunks, rows = total_ref.shape[0], total_ref.shape[1] // GROUPS
    columns = out_columns(part_ref, place_ref[0])
    for zh in range(GROUPS):
        here = slice(zh * rows, (zh + 1) * rows)
        for values, at in (
            (product, slice(0, half)),
            (columns, slice(half, total_ref.shape[2])),
        ):
            some = values[zh * chunks * rows : (zh + 1) * chunks * rows, :]
            some = some.reshape(chunks, rows, some.shape[1])
            total_ref[:, here, at] = (some + far_ref[:, here, at].astype(f32)).astype(bf16)


def pack(place, feats, wide, part, far):
    ins = list(feats) + [wide, part, far]
    return pl.pallas_call(
        pack_kernel,
        grid_spec=prefetched(1, [whole(x) for x in ins], whole(far), []),
        out_shape=jax.ShapeDtypeStruct(far.shape, bf16),
        compiler_params=params(),
        cost_estimate=pl.CostEstimate(
            flops=2 * far.size * wide.shape[0], bytes_accessed=4 * far.size, transcendentals=0
        ),
        name="pack",
    )(place, *ins)


def scatter_scratch(slots, nodes, half):
    wide = BACK * TILE * slots
    return [
        pltpu.VMEM((nodes, wide), bf16),
        pltpu.VMEM((wide, half), bf16),
        pltpu.VMEM((nodes, half), f32),
    ]


def scatter_cost(gp):
    return pl.CostEstimate(flops=gp.size * 256, bytes_accessed=gp.size, transcendentals=0)


def backward(kernel, name, column, place, gp, lead, idx_t, others, out_shape):
    grid_rows, width = lead.shape
    slots = idx_t.shape[0]
    half = width // 2
    nodes = out_shape[-1].shape[0] if kernel is own_kernel else out_shape[0].shape[0]
    rows = BACK * TILE
    half_at = lambda t, place: (t, column(place[0]))
    return pl.pallas_call(
        functools.partial(kernel, slots),
        grid_spec=prefetched(
            grid_rows // rows,
            [
                pl.BlockSpec((rows * slots, half), half_at),
                pl.BlockSpec((rows, half), half_at),
                pl.BlockSpec((slots, rows), lambda t, place: (0, t)),
            ]
            + [whole(x) for x in others],
            [whole(x) for x in out_shape],
            scatter_scratch(slots, nodes, half),
        ),
        out_shape=out_shape,
        compiler_params=params(),
        cost_estimate=scatter_cost(gp),
        name=name,
    )(place, gp, lead, idx_t, *others)


def backward_far(place, gp, lead, idx_t, feats, part, chunks):
    width = lead.shape[1]
    half = width // 2
    out_shape = [
        jax.ShapeDtypeStruct((3 * feats[0].shape[0], half), bf16),
        jax.ShapeDtypeStruct((chunks, width // chunks, half + part.shape[0] // 2), bf16),
    ]
    column = lambda core: 1 - core
    others = list(feats) + [part]
    return backward(far_kernel, "backward_far", column, place, gp, lead, idx_t, others, out_shape)


def backward_own(place, gp, lead, idx_t, wide_far):
    nodes, half = wide_far.shape
    out_shape = [jax.ShapeDtypeStruct((nodes // 3, 2 * half), bf16)] * 3 + [
        jax.ShapeDtypeStruct((nodes, half), bf16)
    ]
    column = lambda core: core
    return backward(own_kernel, "backward_own", column, place, gp, lead, idx_t, [wide_far], out_shape)


def y_kernel(place_ref, own_ref, far_ref, *piece_refs):
    for d, ref in enumerate(piece_refs):
        at = (place_ref[3] + d) % own_ref.shape[1]
        ref[...] = (own_ref[:, at].astype(f32) + far_ref[:, at].astype(f32)).astype(bf16)


def x_kernel(place_ref, *refs):
    ins, outs = refs[: len(refs) // 2], refs[len(refs) // 2 :]
    for d, ref in enumerate(outs):
        for zh in range(ref.shape[0]):
            at = zh * QUARTERS + (place_ref[1] + d) % QUARTERS
            total = ins[0][at].astype(f32)
            for other in ins[1:]:
                total = total + other[at].astype(f32)
            ref[zh] = total.astype(bf16)


def small_kernel(kernel, name, place, ins, out_shape):
    size = sum(x.size for x in ins)
    return pl.pallas_call(
        kernel,
        grid_spec=prefetched(
            1, [whole(x) for x in ins], jax.tree.map(whole, out_shape), []
        ),
        out_shape=out_shape,
        compiler_params=params(),
        cost_estimate=pl.CostEstimate(flops=size, bytes_accessed=4 * size, transcendentals=0),
        name=name,
    )(place, *ins)


def join_kernel(place_ref, src_ref, *refs):
    pieces, total_ref = refs[:QUARTERS], refs[QUARTERS]
    few = pieces[0].shape[2]
    for d, ref in enumerate(pieces):
        at = pl.multiple_of(((place_ref[1] + QUARTERS - d) % QUARTERS) * few, few)
        total_ref[:, pl.ds(at, few)] = ref[...].reshape(total_ref.shape[0], few)
    total_ref[:, QUARTERS * few :] = jnp.sum(src_ref[...].astype(f32), axis=0).astype(bf16)


def last_kernel(place_ref, parts_ref, src_ref, dst_ref, out_ref):
    few, half = dst_ref.shape[1] // (2 * QUARTERS), dst_ref.shape[1] // 2
    width = out_ref.shape[1] // 2
    for core in range(2):
        total = parts_ref[core].astype(f32)
        for other in range(core + 2, parts_ref.shape[0], 2):
            total = total + parts_ref[other].astype(f32)
        for x in range(QUARTERS):
            at = (2 * x + core) * few
            dst_ref[:, at : at + few] = total[:, x * few : (x + 1) * few]
        src_ref[:, core * half : (core + 1) * half] = total[:, half : 2 * half]
        out_ref[:, core * width : (core + 1) * width] = total[:, 2 * half :]


def body(
    mesh_feats,
    grid_embed,
    w_src,
    w_dst,
    w_out,
    truth,
    area_weight,
    var_weight,
    neighbour,
    edge_mask,
):
    own = mesh_feats[0]
    node_rows, width = own.shape
    grid_rows, slots = neighbour.shape
    half = width // 2
    space_count = lax.axis_size(SPACE)
    block_id = lax.axis_index(SPACE)
    members = lax.axis_size(ENS)
    swap = [(0, 1), (1, 0)]
    here = [lax.axis_index(name) for name in ("c", "x", "zh", "y")]
    place = jnp.stack(here).astype(jnp.int32)

    below = shifted(own, SPACE, 1)
    above = shifted(own, SPACE, -1)

    dst = jnp.dot(grid_embed, w_dst, preferred_element_type=f32).astype(bf16)
    local = jnp.mod(neighbour.T - (block_id - 1) * node_rows, node_rows * space_count)
    idx_t = jnp.where(edge_mask.T > 0, local, -1)
    wout_t = w_out.T
    truth_t = truth.T
    var = var_weight[:, None]
    area = area_weight[None, :]
    dst, idx_t, place, below = lax.optimization_barrier((dst, idx_t, place, below))
    feats = (below, own, above)
    chunks = lax.axis_size(FIRST)
    gp, agg, pred, sent, kept, *pieces = forward(
        place, *feats, w_src, dst, idx_t, wout_t, members
    )
    sums = [kept] + [shifted(piece, "x", d + 1) for d, piece in enumerate(pieces)]
    everyone = lax.all_to_all(sent, ENS, 0, 0, tiled=True)
    lead, dst_own, dst_far, part = middle(
        place, everyone, pred, truth_t, area, var, wout_t, idx_t, sums, agg, grid_embed
    )
    dst_far = lax.ppermute(dst_far, "c", swap)
    wide_far, src_far = backward_far(place, gp, lead, idx_t, feats, part, chunks)
    src_far = lax.ppermute(src_far, "c", swap)
    lower, centre, upper, wide_own = backward_own(place, gp, lead, idx_t, wide_far)
    from_above = shifted(lower, SPACE, -1)
    from_below = shifted(upper, SPACE, 1)

    src_total = pack(place, feats, wide_own, part, src_far)
    src_parts = lax.all_to_all(src_total, FIRST, 0, 0, tiled=True)

    src_total, dst_own, dst_far = lax.optimization_barrier((src_total, dst_own, dst_far))
    block = jax.ShapeDtypeStruct((dst_own.shape[0],) + dst_own.shape[2:], bf16)
    kept, *pieces = small_kernel(y_kernel, "along_y", place, [dst_own, dst_far], [block] * QUARTERS)
    moved = [kept] + [shifted(piece, "y", d + 1) for d, piece in enumerate(pieces)]
    block = jax.ShapeDtypeStruct((GROUPS,) + block.shape[1:], bf16)
    kept, *pieces = small_kernel(x_kernel, "along_x", place, moved, [block] * QUARTERS)
    moved = [kept] + [shifted(piece, "x", d + 1) for d, piece in enumerate(pieces)]

    rows = GROUPS * block.shape[1]
    joint = jax.ShapeDtypeStruct((rows, QUARTERS * block.shape[2] + src_parts.shape[2]), bf16)
    total = small_kernel(join_kernel, "join", place, [src_parts] + moved, joint)
    total, from_above, from_below = lax.optimization_barrier((total, from_above, from_below))
    parts = lax.all_to_all(total, SECOND, 0, 0, tiled=True)
    dproj = (centre.astype(f32) + from_above.astype(f32) + from_below.astype(f32)).astype(bf16)
    grad_mesh = lax.dot_general(
        dproj, w_src, (((1,), (1,)), ((), ())), preferred_element_type=f32
    ).astype(bf16)
    rows_out = width // lax.axis_size(ENS + SPACE)
    finals = [
        jax.ShapeDtypeStruct((rows_out, columns), f32) for columns in (width, width, w_out.shape[1])
    ]
    parts = parts.reshape(-1, rows_out, parts.shape[1])
    src_final, dst_final, out_final = small_kernel(last_kernel, "last", place, [parts], finals)
    return grad_mesh[None], src_final, dst_final, out_final


def solution(mesh):
    fine = Mesh(mesh.devices.reshape(2, 4, 4, 4, 2), ("zh", "x", "y", "zl", "c"))
    everywhere = ENS + SPACE
    in_specs = (
        P(ENS, SPACE, None),
        P(SPACE, None),
        P(),
        P(),
        P(),
        P(SPACE, None),
        P(SPACE),
        P(),
        P(SPACE, None),
        P(SPACE, None),
    )
    out_specs = (
        P(ENS, SPACE, None),
        P(everywhere, None),
        P(everywhere, None),
        P(everywhere, None),
    )
    return jax.shard_map(body, mesh=fine, in_specs=in_specs, out_specs=out_specs, check_vma=False)
```

```python
import functools
import jax
import jax.numpy as jnp
from jax import lax
from jax.experimental import pallas as pl
from jax.experimental.pallas import tpu as pltpu
from jax.sharding import Mesh, PartitionSpec as P

loss_scale = 8.0
smooth_sq = 0.01
TILE = 64
NCOL = 256
ROWS = 32
GROUP = 4
VMEM_LIMIT = 56 * 1024 * 1024
BACK = 2
GROUPS = 2
QUARTERS = 4
f32 = jnp.float32
bf16 = jnp.bfloat16
SPACE = ("y", "zl", "c")
ENS = ("zh", "x")
FIRST = ("x", "y")
SECOND = ("zh", "zl", "c")


def shifted(block, axes, distance):
    count = lax.axis_size(axes)
    return lax.ppermute(block, axes, [(i, (i + distance) % count) for i in range(count)])


def smooth_grad(diff):
    return diff * lax.rsqrt(diff * diff + smooth_sq)


def gelu_parts(v):
    c0 = 0.7978845608
    c1 = c0 * 0.044715
    sq = v * v
    t = jnp.tanh(v * (c0 + c1 * sq))
    u = 1.0 + t
    slope = v * (c0 + (3.0 * c1) * sq)
    return v * u, u * (1.0 + (1.0 - t) * slope)


def whole(array):
    zeros = (0,) * len(array.shape)
    return pl.BlockSpec(array.shape, lambda *_: zeros)


def params():
    return pltpu.CompilerParams(vmem_limit_bytes=VMEM_LIMIT)


def give(ref, columns, values):
    chunks, rows = ref.shape[0], ref.shape[1] // GROUPS
    for zh in range(GROUPS):
        some = values[zh * chunks * rows : (zh + 1) * chunks * rows, :].astype(ref.dtype)
        ref[:, zh * rows : (zh + 1) * rows, columns] = some.reshape(chunks, rows, some.shape[1])


def scale_column(idx_ref):
    used = jnp.sum(jnp.where(idx_ref[...] >= 0, 1.0, 0.0), axis=0, keepdims=True)
    return jnp.broadcast_to(0.5 / used, (8, used.shape[1])).T[:, :1]


def forward_kernel(
    slots,
    members,
    place_ref,
    below_ref,
    here_ref,
    above_ref,
    wsrc_ref,
    dst_ref,
    idxt_ref,
    wout_ref,
    gp_ref,
    agg_ref,
    pred_ref,
    sent_ref,
    *rest,
):
    piece_refs = rest[:QUARTERS]
    forward_steps(
        slots,
        members,
        place_ref[1],
        (below_ref, here_ref, above_ref),
        wsrc_ref,
        dst_ref,
        idxt_ref,
        wout_ref,
        gp_ref,
        agg_ref,
        pred_ref,
        sent_ref,
        piece_refs,
        *rest[QUARTERS:],
    )


def forward_steps(
    slots,
    members,
    along,
    feat_refs,
    wsrc_ref,
    dst_ref,
    idxt_ref,
    wout_ref,
    gp_ref,
    agg_ref,
    pred_ref,
    sent_ref,
    piece_refs,
    feats,
    rhs,
    hot,
    pre,
    idx_all,
    scale_all,
    sums,
):
    step = pl.program_id(0)
    nodes, width = feats.shape
    depth = rhs.shape[0]
    tile = depth - nodes
    block = feat_refs[0].shape[0]

    @pl.when(step == 0)
    def _():
        idx_all[...] = idxt_ref[...].astype(f32).T.astype(jnp.int32)
        scale_all[...] = scale_column(idxt_ref)
        for i, ref in enumerate(feat_refs):
            feats[i * block : (i + 1) * block, :] = ref[...]
        for n in range(width // NCOL):
            cols = slice(n * NCOL, (n + 1) * NCOL)
            rhs[:nodes, cols] = jnp.dot(
                feats[...], wsrc_ref[:, cols], preferred_element_type=f32
            ).astype(bf16)

    base = pl.multiple_of(step * tile, tile)
    rhs[nodes:, :] = dst_ref[...]
    lane = lax.broadcasted_iota(jnp.int32, (tile, depth), 1)
    row = lax.broadcasted_iota(jnp.int32, (tile, depth), 0)
    eye = lane == row + nodes
    idx = idx_all[pl.ds(base, tile), :]
    for k in range(slots):
        col = idx[:, k : k + 1]
        hit = (lane == col) | (eye & (col >= 0))
        hot[k * tile : (k + 1) * tile, :] = jnp.where(hit, 1.0, 0.0).astype(bf16)
    for n in range(width // NCOL):
        cols = slice(n * NCOL, (n + 1) * NCOL)
        pre[n % 2] = jnp.dot(hot[...], rhs[:, cols], preferred_element_type=f32).astype(bf16)
        for r in range(0, tile, ROWS):
            acc_g = jnp.zeros((ROWS, NCOL), f32)
            acc_s = jnp.zeros((ROWS, NCOL), f32)
            for k in range(slots):
                rows = slice(k * tile + r, k * tile + r + ROWS)
                value, grad = gelu_parts(pre[n % 2, rows, :])
                gp_ref[rows, cols] = grad
                if k % GROUP == 0:
                    some_g, some_s = value, grad
                else:
                    some_g, some_s = some_g + value, some_s + grad
                if k % GROUP == GROUP - 1:
                    acc_g = acc_g + some_g.astype(f32)
                    acc_s = acc_s + some_s.astype(f32)
            scale = scale_all[pl.ds(pl.multiple_of(base + r, ROWS), ROWS), :]
            agg_ref[pl.ds(pl.multiple_of(base + r, ROWS), ROWS), cols] = (acc_g * scale).astype(bf16)
            sums[n, pl.ds(pl.multiple_of(base + r, ROWS), ROWS), :] = (
                acc_s - (slots - 0.5 / scale)
            ).astype(bf16)

    @pl.when(step == pl.num_programs(0) - 1)
    def _():
        pred = lax.dot_general(
            wout_ref[...], agg_ref[...], (((1,), (1,)), ((), ())), preferred_element_type=f32
        )
        pred_ref[...] = pred
        for e in range(members):
            sent_ref[e] = pred.astype(bf16)
        for d, ref in enumerate(piece_refs):
            ref[...] = sums[(along + d) % QUARTERS]


def forward(place, below, here, above, w_src, dst, idx_t, wout_t, members):
    grid_rows, width = dst.shape
    nodes = 3 * here.shape[0]
    slots = idx_t.shape[0]
    outs = wout_t.shape[0]
    step = lambda t, place: (t, 0)
    out_shape = [
        jax.ShapeDtypeStruct((grid_rows * slots, width), bf16),
        jax.ShapeDtypeStruct((grid_rows, width), bf16),
        jax.ShapeDtypeStruct((outs, grid_rows), f32),
        jax.ShapeDtypeStruct((members, outs, grid_rows), bf16),
    ] + [jax.ShapeDtypeStruct((grid_rows, NCOL), bf16)] * QUARTERS
    return pl.pallas_call(
        functools.partial(forward_kernel, slots, members),
        grid_spec=prefetched(
            grid_rows // TILE,
            [whole(below), whole(here), whole(above), whole(w_src)]
            + [pl.BlockSpec((TILE, width), step), whole(idx_t), whole(wout_t)],
            [pl.BlockSpec((TILE * slots, width), step)] + [whole(x) for x in out_shape[1:]],
            [
                pltpu.VMEM((nodes, width), bf16),
                pltpu.VMEM((nodes + TILE, width), bf16),
                pltpu.VMEM((TILE * slots, nodes + TILE), bf16),
                pltpu.VMEM((2, TILE * slots, NCOL), bf16),
                pltpu.VMEM((grid_rows, slots), jnp.int32),
                pltpu.VMEM((grid_rows, 1), f32),
                pltpu.VMEM((QUARTERS, grid_rows, NCOL), bf16),
            ],
        ),
        out_shape=out_shape,
        compiler_params=params(),
        cost_estimate=pl.CostEstimate(
            flops=2 * grid_rows * slots * 256 * width,
            bytes_accessed=2 * grid_rows * slots * width,
            transcendentals=grid_rows * slots * width,
        ),
        name="forward",
    )(place, below, here, above, w_src, dst, idx_t, wout_t)


def middle_kernel(
    place_ref,
    every_ref,
    pred_ref,
    truth_ref,
    area_ref,
    var_ref,
    wout_ref,
    idxt_ref,
    sum0_ref,
    sum1_ref,
    sum2_ref,
    sum3_ref,
    agg_hbm,
    grid_hbm,
    lead_hbm,
    own_ref,
    far_ref,
    agg_ref,
    grid_ref,
    lead_ref,
    ddst,
    part_ref,
    sems,
):
    loads = [
        pltpu.make_async_copy(agg_hbm, agg_ref, sems.at[0]),
        pltpu.make_async_copy(grid_hbm, grid_ref, sems.at[1]),
    ]
    store = pltpu.make_async_copy(lead_ref, lead_hbm, sems.at[2])
    for copy in loads:
        copy.start()
    width = wout_ref.shape[1]
    members = every_ref.shape[0]
    near, columns = QUARTERS, sum0_ref.shape[1]
    core, x, zh = place_ref[0], place_ref[1], place_ref[2]
    weighting = loss_scale * area_ref[...] * var_ref[...]

    def dpred_of(pred):
        pair = -smooth_grad(pred - pred.astype(bf16).astype(f32))
        for e in range(members):
            pair = pair + smooth_grad(pred - every_ref[e].astype(f32))
        against = smooth_grad(pred - truth_ref[...]) / members
        return (weighting * (against - pair / (members * (members - 1)))).astype(bf16)

    scale = scale_column(idxt_ref)
    first = (((0,), (0,)), ((), ()))
    dpred = dpred_of(pred_ref[...])
    for n in range(width // NCOL):
        cols = slice(n * NCOL, (n + 1) * NCOL)
        dagg = lax.dot_general(dpred, wout_ref[:, cols], first, preferred_element_type=f32)
        lead_ref[:, cols] = (dagg * scale).astype(bf16)
    store.start()

    quarter = wout_ref[:, pl.ds(pl.multiple_of(x * columns, columns), columns)]
    total = jnp.zeros(sum0_ref.shape, f32)
    for d, sum_ref in enumerate((sum0_ref, sum1_ref, sum2_ref, sum3_ref)):
        other = dpred_of(every_ref[zh * near + (x + near - d) % near].astype(f32))
        dagg = lax.dot_general(other, quarter, first, preferred_element_type=f32)
        total = total + dagg * sum_ref[...].astype(f32)
    ddst[...] = (total * scale).astype(bf16)

    for copy in loads:
        copy.wait()
    part_ref[...] = jnp.dot(dpred, agg_ref[...], preferred_element_type=f32)
    chunks, rows, few = own_ref.shape
    outs = part_ref.shape[0] // 2
    rows = rows - outs
    for ref, which in ((far_ref, 1 - core), (own_ref, core)):
        product = lax.dot_general(
            grid_ref[...],
            ddst[:, pl.ds(pl.multiple_of(which * few, few), few)],
            first,
            preferred_element_type=f32,
        )
        ref[:, :rows, :] = product.astype(bf16).reshape(chunks, rows, few)
        at = pl.ds(pl.multiple_of(which * outs, outs), outs)
        for chunk in range(chunks):
            ref[chunk, rows:, :] = part_ref[at, chunk * few : (chunk + 1) * few].astype(bf16)
    store.wait()


def prefetched(count, ins, outs, scratch):
    return pltpu.PrefetchScalarGridSpec(
        num_scalar_prefetch=1, grid=(count,), in_specs=ins, out_specs=outs, scratch_shapes=scratch
    )


def middle(place, everyone, pred, truth_t, area, var, wout_t, idx_t, sums, agg, grid_embed):
    grid_rows, width = agg.shape
    columns = sums[0].shape[1]
    chunks = GROUPS * QUARTERS
    product = (chunks, width // chunks + wout_t.shape[0] // 2, columns // 2)
    anywhere = pl.BlockSpec(memory_space=pl.ANY)
    small = (everyone, pred, truth_t, area, var, wout_t, idx_t, *sums)
    out_shape = [
        jax.ShapeDtypeStruct((grid_rows, width), bf16),
        jax.ShapeDtypeStruct(product, bf16),
        jax.ShapeDtypeStruct(product, bf16),
    ]
    return pl.pallas_call(
        middle_kernel,
        grid_spec=prefetched(
            1,
            [whole(x) for x in small] + [anywhere] * 2,
            [anywhere] + [whole(x) for x in out_shape[1:]],
            [
                pltpu.VMEM((grid_rows, width), bf16),
                pltpu.VMEM((grid_rows, width), bf16),
                pltpu.VMEM((grid_rows, width), bf16),
                pltpu.VMEM((grid_rows, columns), bf16),
                pltpu.VMEM(wout_t.shape, f32),
                pltpu.SemaphoreType.DMA((3,)),
            ],
        ),
        out_shape=out_shape,
        compiler_params=params(),
        cost_estimate=pl.CostEstimate(
            flops=grid_rows * width * width, bytes_accessed=10 * grid_rows * width, transcendentals=0
        ),
        name="middle",
    )(place, *small, agg, grid_embed)


def scatter_step(slots, gp_ref, lead_ref, idx_ref, hot, prod, acc):
    nodes, half = acc.shape
    wide = lead_ref.shape[0]

    @pl.when(pl.program_id(0) == 0)
    def _():
        acc[...] = jnp.zeros_like(acc)

    node = lax.broadcasted_iota(jnp.int32, (nodes, wide), 0)
    for k in range(slots):
        hot[:, k * wide : (k + 1) * wide] = jnp.where(node == idx_ref[k : k + 1, :], 1.0, 0.0).astype(bf16)
    for start in range(0, wide, TILE):
        lead = lead_ref[start : start + TILE, :]
        for k in range(slots):
            at = start * slots + k * TILE
            to = k * wide + start
            prod[to : to + TILE, :] = gp_ref[at : at + TILE, :] * lead
    for n in range(half // NCOL):
        here = slice(n * NCOL, (n + 1) * NCOL)
        acc[:, here] += jnp.dot(hot[...], prod[:, here], preferred_element_type=f32)


def backward_kernel(
    slots,
    place_ref,
    gp_ref,
    lead_ref,
    idx_ref,
    lower_ref,
    centre_ref,
    upper_ref,
    own_ref,
    far_ref,
    hot,
    prod,
    acc,
):
    scatter_step(slots, gp_ref, lead_ref, idx_ref, hot, prod, acc)

    @pl.when(pl.program_id(0) == pl.num_programs(0) - 1)
    def _():
        core = place_ref[0]
        half = own_ref.shape[1]
        block = lower_ref.shape[0]
        for i, ref in enumerate((lower_ref, centre_ref, upper_ref)):
            ref[...] = acc[i * block : (i + 1) * block, :].astype(bf16)
        own_ref[...] = acc[:, pl.ds(pl.multiple_of(core * half, half), half)].astype(bf16)
        far_ref[...] = acc[:, pl.ds(pl.multiple_of((1 - core) * half, half), half)].astype(bf16)


def backward(place, gp, lead, idx_t, nodes):
    grid_rows, width = lead.shape
    slots = idx_t.shape[0]
    rows = BACK * TILE
    out_shape = [jax.ShapeDtypeStruct((nodes // 3, width), bf16)] * 3 + [
        jax.ShapeDtypeStruct((nodes, width // 2), bf16)
    ] * 2
    return pl.pallas_call(
        functools.partial(backward_kernel, slots),
        grid_spec=prefetched(
            grid_rows // rows,
            [
                pl.BlockSpec((rows * slots, width), lambda t, place: (t, 0)),
                pl.BlockSpec((rows, width), lambda t, place: (t, 0)),
                pl.BlockSpec((slots, rows), lambda t, place: (0, t)),
            ],
            [whole(x) for x in out_shape],
            [
                pltpu.VMEM((nodes, rows * slots), bf16),
                pltpu.VMEM((rows * slots, width), bf16),
                pltpu.VMEM((nodes, width), f32),
            ],
        ),
        out_shape=out_shape,
        compiler_params=params(),
        cost_estimate=pl.CostEstimate(flops=gp.size * 512, bytes_accessed=2 * gp.size, transcendentals=0),
        name="backward",
    )(place, gp, lead, idx_t)


def pack_kernel(
    place_ref, below_ref, here_ref, above_ref, edge_ref, own_ref, far_ref, dst_ref, dstfar_ref, total_ref
):
    low = place_ref[0] == 0
    below, here, above, edge = below_ref[...], here_ref[...], above_ref[...], edge_ref[...]
    first = (((0,), (0,)), ((), ()))
    half = own_ref.shape[1]
    mine = jnp.concatenate([below, here, above], axis=0)
    other = jnp.concatenate(
        [jnp.where(low, here, edge), jnp.where(low, above, below), jnp.where(low, edge, here)], axis=0
    )
    product = lax.dot_general(mine, own_ref[...], first, preferred_element_type=f32)
    product = product + lax.dot_general(other, far_ref[...], first, preferred_element_type=f32)
    give(total_ref, slice(0, half), product)
    outs = total_ref.shape[2] - half
    chunks, rows = dst_ref.shape[0], dst_ref.shape[1] - outs
    columns = [
        dst_ref[chunk, rows:, :].astype(f32) + dstfar_ref[chunk, rows:, :].astype(f32)
        for chunk in range(chunks)
    ]
    give(total_ref, slice(half, half + outs), jnp.concatenate(columns, axis=1).T)


def pack(place, feats, edge, own, far, dst_own, dst_far, chunks, outs):
    width = feats[0].shape[1]
    ins = list(feats) + [edge, own, far, dst_own, dst_far]
    out_shape = jax.ShapeDtypeStruct((chunks, width // chunks, (width + outs) // 2), bf16)
    return pl.pallas_call(
        pack_kernel,
        grid_spec=prefetched(1, [whole(x) for x in ins], whole(out_shape), []),
        out_shape=out_shape,
        compiler_params=params(),
        cost_estimate=pl.CostEstimate(
            flops=4 * width * own.size, bytes_accessed=4 * width * width, transcendentals=0
        ),
        name="pack",
    )(place, *ins)


def quarters(array, axis, name):
    count = lax.axis_size(name)
    here = lax.axis_index(name)
    return [
        lax.dynamic_index_in_dim(array, (here + d) % count, axis, keepdims=False) for d in range(count)
    ]


def added(first, *others):
    total = first.astype(f32)
    for other in others:
        total = total + other.astype(f32)
    return total.astype(bf16)


def body(
    mesh_feats,
    grid_embed,
    w_src,
    w_dst,
    w_out,
    truth,
    area_weight,
    var_weight,
    neighbour,
    edge_mask,
):
    own = mesh_feats[0]
    node_rows, width = own.shape
    grid_rows, slots = neighbour.shape
    half = width // 2
    space_count = lax.axis_size(SPACE)
    block_id = lax.axis_index(SPACE)
    members = lax.axis_size(ENS)
    swap = [(0, 1), (1, 0)]
    here = [lax.axis_index(name) for name in ("c", "x", "zh", "y")]
    place = jnp.stack(here).astype(jnp.int32)

    below = shifted(own, SPACE, 1)
    above = shifted(own, SPACE, -1)

    dst = jnp.dot(grid_embed, w_dst, preferred_element_type=f32).astype(bf16)
    local = jnp.mod(neighbour.T - (block_id - 1) * node_rows, node_rows * space_count)
    idx_t = jnp.where(edge_mask.T > 0, local, -1)
    wout_t = w_out.T
    truth_t = truth.T
    var = var_weight[:, None]
    area = area_weight[None, :]
    dst, idx_t, place, below = lax.optimization_barrier((dst, idx_t, place, below))
    feats = (below, own, above)
    chunks = lax.axis_size(FIRST)
    gp, agg, pred, sent, kept, *pieces = forward(
        place, *feats, w_src, dst, idx_t, wout_t, members
    )
    sums = [kept] + [shifted(piece, "x", d + 1) for d, piece in enumerate(pieces)]
    everyone = lax.all_to_all(sent, ENS, 0, 0, tiled=True)
    low = place[0] == 0
    edge = lax.ppermute(jnp.where(low, below, above), "c", swap)
    everyone, edge = lax.optimization_barrier((everyone, edge))
    lead, dst_own, dst_far = middle(
        place, everyone, pred, truth_t, area, var, wout_t, idx_t, sums, agg, grid_embed
    )
    dst_far = lax.ppermute(dst_far, "c", swap)

    outs = w_out.shape[1]
    split = (members, lax.axis_size("y"), -1, dst_own.shape[2])
    both = added(dst_own[:, : width // members], dst_far[:, : width // members]).reshape(split)
    kept, *pieces = quarters(both, 1, "y")
    lead, *pieces = lax.optimization_barrier((lead, *pieces))
    moved = [shifted(piece, "y", d + 1) for d, piece in enumerate(pieces)]

    lower, centre, upper, wide_own, wide_far = backward(place, gp, lead, idx_t, 3 * node_rows)
    lower, upper, wide_far, *moved = lax.optimization_barrier((lower, upper, wide_far, *moved))
    wide_far = lax.ppermute(wide_far, "c", swap)
    from_above = shifted(lower, SPACE, -1)
    from_below = shifted(upper, SPACE, 1)

    src_total = pack(place, feats, edge, wide_own, wide_far, dst_own, dst_far, chunks, outs)
    src_total, kept, *moved = lax.optimization_barrier((src_total, kept, *moved))
    src_parts = lax.all_to_all(src_total, FIRST, 0, 0, tiled=True)

    both = added(kept, *moved).reshape((GROUPS, QUARTERS) + kept.shape[1:])
    kept, *pieces = quarters(both, 1, "x")
    dst_parts = [kept] + [shifted(piece, "x", d + 1) for d, piece in enumerate(pieces)]

    rows = GROUPS * kept.shape[1]
    src_sum = jnp.sum(src_parts.astype(f32), axis=0).astype(bf16)
    dst_sum = jnp.concatenate([x.reshape(rows, -1) for x in dst_parts], axis=1)
    total = jnp.concatenate([dst_sum, src_sum], axis=1)
    total, from_above, from_below = lax.optimization_barrier((total, from_above, from_below))
    parts = lax.all_to_all(total, SECOND, 0, 0, tiled=True)
    dproj = (centre.astype(f32) + from_above.astype(f32) + from_below.astype(f32)).astype(bf16)
    grad_mesh = lax.dot_general(
        dproj, w_src, (((1,), (1,)), ((), ())), preferred_element_type=f32
    ).astype(bf16)
    rows_out = width // lax.axis_size(ENS + SPACE)
    total = jnp.sum(parts.reshape(-1, 2, rows_out, parts.shape[1]).astype(f32), axis=0)
    joined = lambda a, b: jnp.concatenate([total[0, :, a:b], total[1, :, a:b]], axis=1)
    by_distance = total[:, :, :half].reshape(2, rows_out, QUARTERS, -1)
    along = lax.axis_index("x")
    x = jnp.arange(QUARTERS)
    chosen = ((along - x[:, None]) % QUARTERS == x[None, :])[None, :, None, :, None]
    by_distance = by_distance.transpose(1, 0, 2, 3)[:, None]
    dst_final = jnp.sum(jnp.where(chosen, by_distance, 0.0), axis=3).reshape(rows_out, width)
    return (
        grad_mesh[None],
        joined(half, 2 * half),
        dst_final,
        joined(2 * half, total.shape[-1]),
    )


def solution(mesh):
    fine = Mesh(mesh.devices.reshape(2, 4, 4, 4, 2), ("zh", "x", "y", "zl", "c"))
    everywhere = ENS + SPACE
    in_specs = (
        P(ENS, SPACE, None),
        P(SPACE, None),
        P(),
        P(),
        P(),
        P(SPACE, None),
        P(SPACE),
        P(),
        P(SPACE, None),
        P(SPACE, None),
    )
    out_specs = (
        P(ENS, SPACE, None),
        P(everywhere, None),
        P(everywhere, None),
        P(everywhere, None),
    )
    return jax.shard_map(body, mesh=fine, in_specs=in_specs, out_specs=out_specs, check_vma=False)
```

```python
import functools
import jax
import jax.numpy as jnp
from jax import lax
from jax.experimental import pallas as pl
from jax.experimental.pallas import tpu as pltpu
from jax.sharding import Mesh, PartitionSpec as P

loss_scale = 8.0
smooth_sq = 0.01
TILE = 64
NCOL = 256
ROWS = 32
GROUP = 4
VMEM_LIMIT = 56 * 1024 * 1024
BACK = 2
GROUPS = 2
QUARTERS = 4
f32 = jnp.float32
bf16 = jnp.bfloat16
SPACE = ("y", "zl", "c")
ENS = ("zh", "x")
FIRST = ("x", "y")
SECOND = ("zh", "zl", "c")


def shifted(block, axes, distance):
    count = lax.axis_size(axes)
    return lax.ppermute(block, axes, [(i, (i + distance) % count) for i in range(count)])


def smooth_grad(diff):
    return diff * lax.rsqrt(diff * diff + smooth_sq)


def gelu_parts(v):
    c0 = 0.7978845608
    c1 = c0 * 0.044715
    sq = v * v
    t = jnp.tanh(v * (c0 + c1 * sq))
    u = 1.0 + t
    slope = v * (c0 + (3.0 * c1) * sq)
    return v * u, u * (1.0 + (1.0 - t) * slope)


def whole(array):
    zeros = (0,) * len(array.shape)
    return pl.BlockSpec(array.shape, lambda *_: zeros)


def params():
    return pltpu.CompilerParams(vmem_limit_bytes=VMEM_LIMIT)


def give(ref, columns, values):
    chunks, rows = ref.shape[0], ref.shape[1] // GROUPS
    for zh in range(GROUPS):
        some = values[zh * chunks * rows : (zh + 1) * chunks * rows, :].astype(ref.dtype)
        ref[:, zh * rows : (zh + 1) * rows, columns] = some.reshape(chunks, rows, some.shape[1])


def scale_column(idx_ref):
    used = jnp.sum(jnp.where(idx_ref[...] >= 0, 1.0, 0.0), axis=0, keepdims=True)
    return jnp.broadcast_to(0.5 / used, (8, used.shape[1])).T[:, :1]


def forward_kernel(
    slots,
    members,
    place_ref,
    below_ref,
    here_ref,
    above_ref,
    wsrc_ref,
    dst_ref,
    idxt_ref,
    wout_ref,
    gp_ref,
    agg_ref,
    pred_ref,
    sent_ref,
    *rest,
):
    piece_refs = rest[:QUARTERS]
    forward_steps(
        slots,
        members,
        place_ref[1],
        (below_ref, here_ref, above_ref),
        wsrc_ref,
        dst_ref,
        idxt_ref,
        wout_ref,
        gp_ref,
        agg_ref,
        pred_ref,
        sent_ref,
        piece_refs,
        *rest[QUARTERS:],
    )


def forward_steps(
    slots,
    members,
    along,
    feat_refs,
    wsrc_ref,
    dst_ref,
    idxt_ref,
    wout_ref,
    gp_ref,
    agg_ref,
    pred_ref,
    sent_ref,
    piece_refs,
    feats,
    rhs,
    hot,
    pre,
    idx_all,
    scale_all,
    sums,
):
    step = pl.program_id(0)
    nodes, width = feats.shape
    depth = rhs.shape[0]
    tile = depth - nodes
    block = feat_refs[0].shape[0]

    @pl.when(step == 0)
    def _():
        idx_all[...] = idxt_ref[...].astype(f32).T.astype(jnp.int32)
        scale_all[...] = scale_column(idxt_ref)
        for i, ref in enumerate(feat_refs):
            feats[i * block : (i + 1) * block, :] = ref[...]
        for n in range(width // NCOL):
            cols = slice(n * NCOL, (n + 1) * NCOL)
            rhs[:nodes, cols] = jnp.dot(
                feats[...], wsrc_ref[:, cols], preferred_element_type=f32
            ).astype(bf16)

    base = pl.multiple_of(step * tile, tile)
    rhs[nodes:, :] = dst_ref[...]
    lane = lax.broadcasted_iota(jnp.int32, (tile, depth), 1)
    row = lax.broadcasted_iota(jnp.int32, (tile, depth), 0)
    eye = lane == row + nodes
    idx = idx_all[pl.ds(base, tile), :]
    for k in range(slots):
        col = idx[:, k : k + 1]
        hit = (lane == col) | (eye & (col >= 0))
        hot[k * tile : (k + 1) * tile, :] = jnp.where(hit, 1.0, 0.0).astype(bf16)
    for n in range(width // NCOL):
        cols = slice(n * NCOL, (n + 1) * NCOL)
        pre[n % 2] = jnp.dot(hot[...], rhs[:, cols], preferred_element_type=f32).astype(bf16)
        for r in range(0, tile, ROWS):
            acc_g = jnp.zeros((ROWS, NCOL), f32)
            acc_s = jnp.zeros((ROWS, NCOL), f32)
            for k in range(slots):
                rows = slice(k * tile + r, k * tile + r + ROWS)
                value, grad = gelu_parts(pre[n % 2, rows, :])
                gp_ref[rows, cols] = grad
                if k % GROUP == 0:
                    some_g, some_s = value, grad
                else:
                    some_g, some_s = some_g + value, some_s + grad
                if k % GROUP == GROUP - 1:
                    acc_g = acc_g + some_g.astype(f32)
                    acc_s = acc_s + some_s.astype(f32)
            scale = scale_all[pl.ds(pl.multiple_of(base + r, ROWS), ROWS), :]
            agg_ref[pl.ds(pl.multiple_of(base + r, ROWS), ROWS), cols] = (acc_g * scale).astype(bf16)
            sums[n, r : r + ROWS, :] = (acc_s - (slots - 0.5 / scale)).astype(bf16)

    for d, ref in enumerate(piece_refs):
        ref[...] = sums[(along + d) % QUARTERS]

    @pl.when(step == pl.num_programs(0) - 1)
    def _():
        pred = lax.dot_general(
            wout_ref[...], agg_ref[...], (((1,), (1,)), ((), ())), preferred_element_type=f32
        )
        pred_ref[...] = pred
        for e in range(members):
            sent_ref[e] = pred.astype(bf16)


def forward(place, below, here, above, w_src, dst, idx_t, wout_t, members):
    grid_rows, width = dst.shape
    nodes = 3 * here.shape[0]
    slots = idx_t.shape[0]
    outs = wout_t.shape[0]
    step = lambda t, place: (t, 0)
    out_shape = [
        jax.ShapeDtypeStruct((grid_rows * slots, width), bf16),
        jax.ShapeDtypeStruct((grid_rows, width), bf16),
        jax.ShapeDtypeStruct((outs, grid_rows), f32),
        jax.ShapeDtypeStruct((members, outs, grid_rows), bf16),
    ] + [jax.ShapeDtypeStruct((grid_rows, NCOL), bf16)] * QUARTERS
    return pl.pallas_call(
        functools.partial(forward_kernel, slots, members),
        grid_spec=prefetched(
            grid_rows // TILE,
            [whole(below), whole(here), whole(above), whole(w_src)]
            + [pl.BlockSpec((TILE, width), step), whole(idx_t), whole(wout_t)],
            [pl.BlockSpec((TILE * slots, width), step)]
            + [whole(x) for x in out_shape[1:4]]
            + [pl.BlockSpec((TILE, NCOL), step)] * QUARTERS,
            [
                pltpu.VMEM((nodes, width), bf16),
                pltpu.VMEM((nodes + TILE, width), bf16),
                pltpu.VMEM((TILE * slots, nodes + TILE), bf16),
                pltpu.VMEM((2, TILE * slots, NCOL), bf16),
                pltpu.VMEM((grid_rows, slots), jnp.int32),
                pltpu.VMEM((grid_rows, 1), f32),
                pltpu.VMEM((QUARTERS, TILE, NCOL), bf16),
            ],
        ),
        out_shape=out_shape,
        compiler_params=params(),
        cost_estimate=pl.CostEstimate(
            flops=2 * grid_rows * slots * 256 * width,
            bytes_accessed=2 * grid_rows * slots * width,
            transcendentals=grid_rows * slots * width,
        ),
        name="forward",
    )(place, below, here, above, w_src, dst, idx_t, wout_t)


def middle_kernel(
    place_ref,
    every_ref,
    pred_ref,
    truth_ref,
    area_ref,
    var_ref,
    wout_ref,
    idxt_ref,
    sum0_ref,
    sum1_ref,
    sum2_ref,
    sum3_ref,
    agg_hbm,
    grid_hbm,
    lead_hbm,
    own_ref,
    far_ref,
    agg_ref,
    grid_ref,
    lead_ref,
    ddst,
    part_ref,
    sems,
):
    loads = [
        pltpu.make_async_copy(agg_hbm, agg_ref, sems.at[0]),
        pltpu.make_async_copy(grid_hbm, grid_ref, sems.at[1]),
    ]
    store = pltpu.make_async_copy(lead_ref, lead_hbm, sems.at[2])
    for copy in loads:
        copy.start()
    width = wout_ref.shape[1]
    members = every_ref.shape[0]
    near, columns = QUARTERS, sum0_ref.shape[1]
    core, x, zh = place_ref[0], place_ref[1], place_ref[2]
    weighting = loss_scale * area_ref[...] * var_ref[...]

    def dpred_of(pred):
        pair = -smooth_grad(pred - pred.astype(bf16).astype(f32))
        for e in range(members):
            pair = pair + smooth_grad(pred - every_ref[e].astype(f32))
        against = smooth_grad(pred - truth_ref[...]) / members
        return (weighting * (against - pair / (members * (members - 1)))).astype(bf16)

    scale = scale_column(idxt_ref)
    first = (((0,), (0,)), ((), ()))
    dpred = dpred_of(pred_ref[...])
    for n in range(width // NCOL):
        cols = slice(n * NCOL, (n + 1) * NCOL)
        dagg = lax.dot_general(dpred, wout_ref[:, cols], first, preferred_element_type=f32)
        lead_ref[:, cols] = (dagg * scale).astype(bf16)
    store.start()

    quarter = wout_ref[:, pl.ds(pl.multiple_of(x * columns, columns), columns)]
    total = jnp.zeros(sum0_ref.shape, f32)
    for d, sum_ref in enumerate((sum0_ref, sum1_ref, sum2_ref, sum3_ref)):
        other = dpred_of(every_ref[zh * near + (x + near - d) % near].astype(f32))
        dagg = lax.dot_general(other, quarter, first, preferred_element_type=f32)
        total = total + dagg * sum_ref[...].astype(f32)
    ddst[...] = (total * scale).astype(bf16)

    for copy in loads:
        copy.wait()
    part_ref[...] = jnp.dot(dpred, agg_ref[...], preferred_element_type=f32)
    chunks, rows, few = own_ref.shape
    outs = part_ref.shape[0] // 2
    rows = rows - outs
    for ref, which in ((far_ref, 1 - core), (own_ref, core)):
        product = lax.dot_general(
            grid_ref[...],
            ddst[:, pl.ds(pl.multiple_of(which * few, few), few)],
            first,
            preferred_element_type=f32,
        )
        ref[:, :rows, :] = product.astype(bf16).reshape(chunks, rows, few)
        at = pl.ds(pl.multiple_of(which * outs, outs), outs)
        for chunk in range(chunks):
            ref[chunk, rows:, :] = part_ref[at, chunk * few : (chunk + 1) * few].astype(bf16)
    store.wait()


def prefetched(count, ins, outs, scratch):
    return pltpu.PrefetchScalarGridSpec(
        num_scalar_prefetch=1, grid=(count,), in_specs=ins, out_specs=outs, scratch_shapes=scratch
    )


def middle(place, everyone, pred, truth_t, area, var, wout_t, idx_t, sums, agg, grid_embed):
    grid_rows, width = agg.shape
    columns = sums[0].shape[1]
    chunks = GROUPS * QUARTERS
    product = (chunks, width // chunks + wout_t.shape[0] // 2, columns // 2)
    anywhere = pl.BlockSpec(memory_space=pl.ANY)
    small = (everyone, pred, truth_t, area, var, wout_t, idx_t, *sums)
    out_shape = [
        jax.ShapeDtypeStruct((grid_rows, width), bf16),
        jax.ShapeDtypeStruct(product, bf16),
        jax.ShapeDtypeStruct(product, bf16),
    ]
    return pl.pallas_call(
        middle_kernel,
        grid_spec=prefetched(
            1,
            [whole(x) for x in small] + [anywhere] * 2,
            [anywhere] + [whole(x) for x in out_shape[1:]],
            [
                pltpu.VMEM((grid_rows, width), bf16),
                pltpu.VMEM((grid_rows, width), bf16),
                pltpu.VMEM((grid_rows, width), bf16),
                pltpu.VMEM((grid_rows, columns), bf16),
                pltpu.VMEM(wout_t.shape, f32),
                pltpu.SemaphoreType.DMA((3,)),
            ],
        ),
        out_shape=out_shape,
        compiler_params=params(),
        cost_estimate=pl.CostEstimate(
            flops=grid_rows * width * width, bytes_accessed=10 * grid_rows * width, transcendentals=0
        ),
        name="middle",
    )(place, *small, agg, grid_embed)


def scatter_step(slots, gp_ref, lead_ref, idx_ref, hot, prod, acc):
    nodes, half = acc.shape
    wide = lead_ref.shape[0]

    @pl.when(pl.program_id(0) == 0)
    def _():
        acc[...] = jnp.zeros_like(acc)

    node = lax.broadcasted_iota(jnp.int32, (nodes, wide), 0)
    for k in range(slots):
        hot[:, k * wide : (k + 1) * wide] = jnp.where(node == idx_ref[k : k + 1, :], 1.0, 0.0).astype(bf16)
    for start in range(0, wide, TILE):
        lead = lead_ref[start : start + TILE, :]
        for k in range(slots):
            at = start * slots + k * TILE
            to = k * wide + start
            prod[to : to + TILE, :] = gp_ref[at : at + TILE, :] * lead
    for n in range(half // NCOL):
        here = slice(n * NCOL, (n + 1) * NCOL)
        acc[:, here] += jnp.dot(hot[...], prod[:, here], preferred_element_type=f32)


def backward_kernel(
    slots,
    place_ref,
    gp_ref,
    lead_ref,
    idx_ref,
    lower_ref,
    centre_ref,
    upper_ref,
    own_ref,
    far_ref,
    hot,
    prod,
    acc,
):
    scatter_step(slots, gp_ref, lead_ref, idx_ref, hot, prod, acc)

    @pl.when(pl.program_id(0) == pl.num_programs(0) - 1)
    def _():
        core = place_ref[0]
        half = own_ref.shape[1]
        block = lower_ref.shape[0]
        for i, ref in enumerate((lower_ref, centre_ref, upper_ref)):
            ref[...] = acc[i * block : (i + 1) * block, :].astype(bf16)
        own_ref[...] = acc[:, pl.ds(pl.multiple_of(core * half, half), half)].astype(bf16)
        far_ref[...] = acc[:, pl.ds(pl.multiple_of((1 - core) * half, half), half)].astype(bf16)


def backward(place, gp, lead, idx_t, nodes):
    grid_rows, width = lead.shape
    slots = idx_t.shape[0]
    rows = BACK * TILE
    out_shape = [jax.ShapeDtypeStruct((nodes // 3, width), bf16)] * 3 + [
        jax.ShapeDtypeStruct((nodes, width // 2), bf16)
    ] * 2
    return pl.pallas_call(
        functools.partial(backward_kernel, slots),
        grid_spec=prefetched(
            grid_rows // rows,
            [
                pl.BlockSpec((rows * slots, width), lambda t, place: (t, 0)),
                pl.BlockSpec((rows, width), lambda t, place: (t, 0)),
                pl.BlockSpec((slots, rows), lambda t, place: (0, t)),
            ],
            [whole(x) for x in out_shape],
            [
                pltpu.VMEM((nodes, rows * slots), bf16),
                pltpu.VMEM((rows * slots, width), bf16),
                pltpu.VMEM((nodes, width), f32),
            ],
        ),
        out_shape=out_shape,
        compiler_params=params(),
        cost_estimate=pl.CostEstimate(flops=gp.size * 512, bytes_accessed=2 * gp.size, transcendentals=0),
        name="backward",
    )(place, gp, lead, idx_t)


def pack_kernel(
    place_ref, below_ref, here_ref, above_ref, edge_ref, own_ref, far_ref, dst_ref, dstfar_ref, total_ref
):
    low = place_ref[0] == 0
    below, here, above, edge = below_ref[...], here_ref[...], above_ref[...], edge_ref[...]
    first = (((0,), (0,)), ((), ()))
    half = own_ref.shape[1]
    mine = jnp.concatenate([below, here, above], axis=0)
    other = jnp.concatenate(
        [jnp.where(low, here, edge), jnp.where(low, above, below), jnp.where(low, edge, here)], axis=0
    )
    product = lax.dot_general(mine, own_ref[...], first, preferred_element_type=f32)
    product = product + lax.dot_general(other, far_ref[...], first, preferred_element_type=f32)
    chunks, rows, columns = total_ref.shape
    total_ref[:, :, :half] = product.astype(bf16).reshape(chunks, rows, half)
    both = dst_ref[...].astype(f32) + dstfar_ref[...].astype(f32)
    few = both.shape[2]
    outs = columns - half - few
    some = both[:, : both.shape[1] - outs].astype(bf16)
    total_ref[:, :, half : half + few] = some.reshape(chunks, rows, few)
    some = jnp.concatenate([both[i, both.shape[1] - outs :] for i in range(both.shape[0])], axis=1)
    total_ref[:, :, half + few :] = some.T.astype(bf16).reshape(chunks, rows, outs)


def pack(place, feats, edge, own, far, dst_own, dst_far, chunks):
    nodes, width = feats[0].shape
    per_zh = (dst_own.shape[0] // GROUPS,) + dst_own.shape[1:]
    outs = dst_own.shape[1] - width // dst_own.shape[0]
    columns = width // 2 + dst_own.shape[2] + outs
    rows = width // chunks
    feat = pl.BlockSpec((nodes, width // GROUPS), lambda t, place: (0, t))
    dst = pl.BlockSpec(per_zh, lambda t, place: (t, 0, 0))
    return pl.pallas_call(
        pack_kernel,
        grid_spec=prefetched(
            GROUPS,
            [feat] * 4 + [whole(own), whole(far), dst, dst],
            pl.BlockSpec((chunks, rows // GROUPS, columns), lambda t, place: (0, t, 0)),
            [],
        ),
        out_shape=jax.ShapeDtypeStruct((chunks, rows, columns), bf16),
        compiler_params=params(),
        cost_estimate=pl.CostEstimate(
            flops=4 * width * own.size, bytes_accessed=4 * width * width, transcendentals=0
        ),
        name="pack",
    )(place, *feats, edge, own, far, dst_own, dst_far)


def join_kernel(parts_ref, total_ref):
    half = total_ref.shape[2] - parts_ref.shape[2]
    half = half * QUARTERS // (QUARTERS - 1)
    few = half // QUARTERS
    each = parts_ref.shape[0] // QUARTERS
    pieces = []
    ends = 0.0
    for x in range(QUARTERS):
        some = parts_ref[x * each].astype(f32)
        for y in range(1, each):
            some = some + parts_ref[x * each + y].astype(f32)
        pieces.append(some[:, half : half + few])
        ends = ends + some
    total = jnp.concatenate([ends[:, :half]] + pieces + [ends[:, half + few :]], axis=1).astype(bf16)
    for i in range(total_ref.shape[0]):
        rows = total_ref.shape[1]
        total_ref[i] = total[i * rows : (i + 1) * rows, :]


def join(parts, rows_out, half):
    sources, rows, columns = parts.shape
    wide = columns - half // QUARTERS + half
    count = rows // rows_out
    return pl.pallas_call(
        join_kernel,
        grid=(GROUPS,),
        in_specs=[pl.BlockSpec((sources, rows // GROUPS, columns), lambda t: (0, t, 0))],
        out_specs=pl.BlockSpec((count // GROUPS, rows_out, wide), lambda t: (t, 0, 0)),
        out_shape=jax.ShapeDtypeStruct((count, rows_out, wide), bf16),
        compiler_params=params(),
        cost_estimate=pl.CostEstimate(flops=parts.size, bytes_accessed=2 * parts.size, transcendentals=0),
        name="join",
    )(parts)


def body(
    mesh_feats,
    grid_embed,
    w_src,
    w_dst,
    w_out,
    truth,
    area_weight,
    var_weight,
    neighbour,
    edge_mask,
):
    own = mesh_feats[0]
    node_rows, width = own.shape
    grid_rows, slots = neighbour.shape
    half = width // 2
    space_count = lax.axis_size(SPACE)
    block_id = lax.axis_index(SPACE)
    members = lax.axis_size(ENS)
    swap = [(0, 1), (1, 0)]
    here = [lax.axis_index(name) for name in ("c", "x", "zh", "y")]
    place = jnp.stack(here).astype(jnp.int32)

    below = shifted(own, SPACE, 1)
    above = shifted(own, SPACE, -1)

    dst = jnp.dot(grid_embed, w_dst, preferred_element_type=f32).astype(bf16)
    local = jnp.mod(neighbour.T - (block_id - 1) * node_rows, node_rows * space_count)
    idx_t = jnp.where(edge_mask.T > 0, local, -1)
    wout_t = w_out.T
    truth_t = truth.T
    var = var_weight[:, None]
    area = area_weight[None, :]
    dst, idx_t, place, below = lax.optimization_barrier((dst, idx_t, place, below))
    feats = (below, own, above)
    chunks = lax.axis_size(FIRST)
    gp, agg, pred, sent, kept, *pieces = forward(
        place, *feats, w_src, dst, idx_t, wout_t, members
    )
    sums = [kept] + [shifted(piece, "x", d + 1) for d, piece in enumerate(pieces)]
    everyone = lax.all_to_all(sent, ENS, 0, 0, tiled=True)
    low = place[0] == 0
    edge = lax.ppermute(jnp.where(low, below, above), "c", swap)
    everyone, edge = lax.optimization_barrier((everyone, edge))
    lead, dst_own, dst_far = middle(
        place, everyone, pred, truth_t, area, var, wout_t, idx_t, sums, agg, grid_embed
    )
    dst_far = lax.ppermute(dst_far, "c", swap)

    lower, centre, upper, wide_own, wide_far = backward(place, gp, lead, idx_t, 3 * node_rows)
    wide_far = lax.ppermute(wide_far, "c", swap)
    from_above = shifted(lower, SPACE, -1)
    from_below = shifted(upper, SPACE, 1)

    total = pack(place, feats, edge, wide_own, wide_far, dst_own, dst_far, chunks)
    parts = lax.all_to_all(total, FIRST, 0, 0, tiled=True)
    few = half // QUARTERS
    rows_out = width // lax.axis_size(ENS + SPACE)

    total = join(parts, rows_out, half)
    total, from_above, from_below = lax.optimization_barrier((total, from_above, from_below))
    parts = lax.all_to_all(total, SECOND, 0, 0, tiled=True)
    dproj = (centre.astype(f32) + from_above.astype(f32) + from_below.astype(f32)).astype(bf16)
    grad_mesh = lax.dot_general(
        dproj, w_src, (((1,), (1,)), ((), ())), preferred_element_type=f32
    ).astype(bf16)
    total = jnp.sum(parts.reshape(-1, 2, rows_out, parts.shape[2]).astype(f32), axis=0)
    joined = lambda a, b: jnp.concatenate([total[0, :, a:b], total[1, :, a:b]], axis=1)
    dst_final = total[:, :, half : 2 * half].reshape(2, rows_out, QUARTERS, few)
    dst_final = dst_final.transpose(1, 2, 0, 3).reshape(rows_out, width)
    return (
        grad_mesh[None],
        joined(0, half),
        dst_final,
        joined(2 * half, total.shape[-1]),
    )


def solution(mesh):
    fine = Mesh(mesh.devices.reshape(2, 4, 4, 4, 2), ("zh", "x", "y", "zl", "c"))
    everywhere = ENS + SPACE
    in_specs = (
        P(ENS, SPACE, None),
        P(SPACE, None),
        P(),
        P(),
        P(),
        P(SPACE, None),
        P(SPACE),
        P(),
        P(SPACE, None),
        P(SPACE, None),
    )
    out_specs = (
        P(ENS, SPACE, None),
        P(everywhere, None),
        P(everywhere, None),
        P(everywhere, None),
    )
    return jax.shard_map(body, mesh=fine, in_specs=in_specs, out_specs=out_specs, check_vma=False)
```

```python
import functools
import jax
import jax.numpy as jnp
from jax import lax
from jax.experimental import pallas as pl
from jax.experimental.pallas import tpu as pltpu
from jax.sharding import Mesh, PartitionSpec as P

loss_scale = 8.0
smooth_sq = 0.01
TILE = 64
NCOL = 256
ROWS = 32
GROUP = 4
VMEM_LIMIT = 56 * 1024 * 1024
BACK = 2
GROUPS = 2
QUARTERS = 4
f32 = jnp.float32
bf16 = jnp.bfloat16
SPACE = ("y", "zl", "c")
ENS = ("zh", "x")
FIRST = ("x", "y")
SECOND = ("zh", "zl", "c")


def shifted(block, axes, distance):
    count = lax.axis_size(axes)
    return lax.ppermute(block, axes, [(i, (i + distance) % count) for i in range(count)])


def smooth_grad(diff):
    return diff * lax.rsqrt(diff * diff + smooth_sq)


def gelu_parts(v):
    c0 = 0.7978845608
    c1 = c0 * 0.044715
    sq = v * v
    t = jnp.tanh(v * (c0 + c1 * sq))
    u = 1.0 + t
    slope = v * (c0 + (3.0 * c1) * sq)
    return v * u, u * (1.0 + (1.0 - t) * slope)


def whole(array):
    zeros = (0,) * len(array.shape)
    return pl.BlockSpec(array.shape, lambda *_: zeros)


def landed():
    return pl.BlockSpec(memory_space=pltpu.VMEM)


def kept_near(array):
    return pltpu.with_memory_space_constraint(array, pltpu.VMEM)


def params():
    return pltpu.CompilerParams(vmem_limit_bytes=VMEM_LIMIT)


def give(ref, columns, values):
    chunks, rows = ref.shape[0], ref.shape[1] // GROUPS
    for zh in range(GROUPS):
        some = values[zh * chunks * rows : (zh + 1) * chunks * rows, :].astype(ref.dtype)
        ref[:, zh * rows : (zh + 1) * rows, columns] = some.reshape(chunks, rows, some.shape[1])


def scale_column(idx_ref):
    used = jnp.sum(jnp.where(idx_ref[...] >= 0, 1.0, 0.0), axis=0, keepdims=True)
    return jnp.broadcast_to(0.5 / used, (8, used.shape[1])).T[:, :1]


def forward_kernel(
    slots,
    members,
    place_ref,
    below_ref,
    here_ref,
    above_ref,
    wsrc_ref,
    dst_ref,
    idxt_ref,
    wout_ref,
    gp_ref,
    agg_ref,
    pred_ref,
    sent_ref,
    *rest,
):
    piece_refs = rest[:QUARTERS]
    forward_steps(
        slots,
        members,
        place_ref[1],
        (below_ref, here_ref, above_ref),
        wsrc_ref,
        dst_ref,
        idxt_ref,
        wout_ref,
        gp_ref,
        agg_ref,
        pred_ref,
        sent_ref,
        piece_refs,
        *rest[QUARTERS:],
    )


def forward_steps(
    slots,
    members,
    along,
    feat_refs,
    wsrc_ref,
    dst_ref,
    idxt_ref,
    wout_ref,
    gp_ref,
    agg_ref,
    pred_ref,
    sent_ref,
    piece_refs,
    feats,
    rhs,
    hot,
    pre,
    idx_all,
    scale_all,
    sums,
):
    step = pl.program_id(0)
    nodes, width = feats.shape
    depth = rhs.shape[0]
    tile = depth - nodes
    block = feat_refs[0].shape[0]

    @pl.when(step == 0)
    def _():
        idx_all[...] = idxt_ref[...].astype(f32).T.astype(jnp.int32)
        scale_all[...] = scale_column(idxt_ref)
        for i, ref in enumerate(feat_refs):
            feats[i * block : (i + 1) * block, :] = ref[...]
        for n in range(width // NCOL):
            cols = slice(n * NCOL, (n + 1) * NCOL)
            rhs[:nodes, cols] = jnp.dot(
                feats[...], wsrc_ref[:, cols], preferred_element_type=f32
            ).astype(bf16)

    base = pl.multiple_of(step * tile, tile)
    rhs[nodes:, :] = dst_ref[...]
    lane = lax.broadcasted_iota(jnp.int32, (tile, depth), 1)
    row = lax.broadcasted_iota(jnp.int32, (tile, depth), 0)
    eye = lane == row + nodes
    idx = idx_all[pl.ds(base, tile), :]
    for k in range(slots):
        col = idx[:, k : k + 1]
        hit = (lane == col) | (eye & (col >= 0))
        hot[k * tile : (k + 1) * tile, :] = jnp.where(hit, 1.0, 0.0).astype(bf16)
    for n in range(width // NCOL):
        cols = slice(n * NCOL, (n + 1) * NCOL)
        pre[n % 2] = jnp.dot(hot[...], rhs[:, cols], preferred_element_type=f32).astype(bf16)
        for r in range(0, tile, ROWS):
            acc_g = jnp.zeros((ROWS, NCOL), f32)
            acc_s = jnp.zeros((ROWS, NCOL), f32)
            for k in range(slots):
                rows = slice(k * tile + r, k * tile + r + ROWS)
                value, grad = gelu_parts(pre[n % 2, rows, :])
                gp_ref[rows, cols] = grad
                if k % GROUP == 0:
                    some_g, some_s = value, grad
                else:
                    some_g, some_s = some_g + value, some_s + grad
                if k % GROUP == GROUP - 1:
                    acc_g = acc_g + some_g.astype(f32)
                    acc_s = acc_s + some_s.astype(f32)
            scale = scale_all[pl.ds(pl.multiple_of(base + r, ROWS), ROWS), :]
            agg_ref[pl.ds(pl.multiple_of(base + r, ROWS), ROWS), cols] = (acc_g * scale).astype(bf16)
            sums[n, r : r + ROWS, :] = (acc_s - (slots - 0.5 / scale)).astype(bf16)

    for d, ref in enumerate(piece_refs):
        ref[...] = sums[(along + d) % QUARTERS]

    @pl.when(step == pl.num_programs(0) - 1)
    def _():
        pred = lax.dot_general(
            wout_ref[...], agg_ref[...], (((1,), (1,)), ((), ())), preferred_element_type=f32
        )
        pred_ref[...] = pred
        for e in range(members):
            sent_ref[e] = pred.astype(bf16)


def forward(place, below, here, above, w_src, dst, idx_t, wout_t, members):
    grid_rows, width = dst.shape
    nodes = 3 * here.shape[0]
    slots = idx_t.shape[0]
    outs = wout_t.shape[0]
    step = lambda t, place: (t, 0)
    out_shape = [
        jax.ShapeDtypeStruct((grid_rows * slots, width), bf16),
        jax.ShapeDtypeStruct((grid_rows, width), bf16),
        jax.ShapeDtypeStruct((outs, grid_rows), f32),
        jax.ShapeDtypeStruct((members, outs, grid_rows), bf16),
    ] + [jax.ShapeDtypeStruct((grid_rows, NCOL), bf16)] * QUARTERS
    return pl.pallas_call(
        functools.partial(forward_kernel, slots, members),
        grid_spec=prefetched(
            grid_rows // TILE,
            [landed(), whole(here), landed(), whole(w_src)]
            + [pl.BlockSpec((TILE, width), step), whole(idx_t), whole(wout_t)],
            [pl.BlockSpec((TILE * slots, width), step)]
            + [whole(x) for x in out_shape[1:4]]
            + [pl.BlockSpec((TILE, NCOL), step)] * QUARTERS,
            [
                pltpu.VMEM((nodes, width), bf16),
                pltpu.VMEM((nodes + TILE, width), bf16),
                pltpu.VMEM((TILE * slots, nodes + TILE), bf16),
                pltpu.VMEM((2, TILE * slots, NCOL), bf16),
                pltpu.VMEM((grid_rows, slots), jnp.int32),
                pltpu.VMEM((grid_rows, 1), f32),
                pltpu.VMEM((QUARTERS, TILE, NCOL), bf16),
            ],
        ),
        out_shape=out_shape,
        compiler_params=params(),
        cost_estimate=pl.CostEstimate(
            flops=2 * grid_rows * slots * 256 * width,
            bytes_accessed=2 * grid_rows * slots * width,
            transcendentals=grid_rows * slots * width,
        ),
        name="forward",
    )(place, kept_near(below), here, kept_near(above), w_src, dst, idx_t, wout_t)


def middle_kernel(
    place_ref,
    every_ref,
    pred_ref,
    truth_ref,
    area_ref,
    var_ref,
    wout_ref,
    idxt_ref,
    sum0_ref,
    sum1_ref,
    sum2_ref,
    sum3_ref,
    agg_hbm,
    grid_hbm,
    lead_hbm,
    own_ref,
    far_ref,
    agg_ref,
    grid_ref,
    lead_ref,
    ddst,
    part_ref,
    sems,
):
    loads = [
        pltpu.make_async_copy(agg_hbm, agg_ref, sems.at[0]),
        pltpu.make_async_copy(grid_hbm, grid_ref, sems.at[1]),
    ]
    store = pltpu.make_async_copy(lead_ref, lead_hbm, sems.at[2])
    for copy in loads:
        copy.start()
    width = wout_ref.shape[1]
    members = every_ref.shape[0]
    near, columns = QUARTERS, sum0_ref.shape[1]
    core, x, zh = place_ref[0], place_ref[1], place_ref[2]
    weighting = loss_scale * area_ref[...] * var_ref[...]

    def dpred_of(pred):
        pair = -smooth_grad(pred - pred.astype(bf16).astype(f32))
        for e in range(members):
            pair = pair + smooth_grad(pred - every_ref[e].astype(f32))
        against = smooth_grad(pred - truth_ref[...]) / members
        return (weighting * (against - pair / (members * (members - 1)))).astype(bf16)

    scale = scale_column(idxt_ref)
    first = (((0,), (0,)), ((), ()))
    dpred = dpred_of(pred_ref[...])
    for n in range(width // NCOL):
        cols = slice(n * NCOL, (n + 1) * NCOL)
        dagg = lax.dot_general(dpred, wout_ref[:, cols], first, preferred_element_type=f32)
        lead_ref[:, cols] = (dagg * scale).astype(bf16)
    store.start()

    quarter = wout_ref[:, pl.ds(pl.multiple_of(x * columns, columns), columns)]
    total = jnp.zeros(sum0_ref.shape, f32)
    for d, sum_ref in enumerate((sum0_ref, sum1_ref, sum2_ref, sum3_ref)):
        other = dpred_of(every_ref[zh * near + (x + near - d) % near].astype(f32))
        dagg = lax.dot_general(other, quarter, first, preferred_element_type=f32)
        total = total + dagg * sum_ref[...].astype(f32)
    ddst[...] = (total * scale).astype(bf16)

    for copy in loads:
        copy.wait()
    part_ref[...] = jnp.dot(dpred, agg_ref[...], preferred_element_type=f32)
    chunks, rows, few = own_ref.shape
    outs = part_ref.shape[0] // 2
    rows = rows - outs
    for ref, which in ((far_ref, 1 - core), (own_ref, core)):
        product = lax.dot_general(
            grid_ref[...],
            ddst[:, pl.ds(pl.multiple_of(which * few, few), few)],
            first,
            preferred_element_type=f32,
        )
        ref[:, :rows, :] = product.astype(bf16).reshape(chunks, rows, few)
        at = pl.ds(pl.multiple_of(which * outs, outs), outs)
        for chunk in range(chunks):
            ref[chunk, rows:, :] = part_ref[at, chunk * few : (chunk + 1) * few].astype(bf16)
    store.wait()


def prefetched(count, ins, outs, scratch):
    return pltpu.PrefetchScalarGridSpec(
        num_scalar_prefetch=1, grid=(count,), in_specs=ins, out_specs=outs, scratch_shapes=scratch
    )


def middle(place, everyone, pred, truth_t, area, var, wout_t, idx_t, sums, agg, grid_embed):
    grid_rows, width = agg.shape
    columns = sums[0].shape[1]
    chunks = GROUPS * QUARTERS
    product = (chunks, width // chunks + wout_t.shape[0] // 2, columns // 2)
    anywhere = pl.BlockSpec(memory_space=pl.ANY)
    small = (everyone, pred, truth_t, area, var, wout_t, idx_t, *sums)
    out_shape = [
        jax.ShapeDtypeStruct((grid_rows, width), bf16),
        jax.ShapeDtypeStruct(product, bf16),
        jax.ShapeDtypeStruct(product, bf16),
    ]
    return pl.pallas_call(
        middle_kernel,
        grid_spec=prefetched(
            1,
            [landed()]
            + [whole(x) for x in small[1 : -len(sums)]]
            + [whole(sums[0])]
            + [landed()] * (len(sums) - 1)
            + [anywhere] * 2,
            [anywhere] + [whole(x) for x in out_shape[1:]],
            [
                pltpu.VMEM((grid_rows, width), bf16),
                pltpu.VMEM((grid_rows, width), bf16),
                pltpu.VMEM((grid_rows, width), bf16),
                pltpu.VMEM((grid_rows, columns), bf16),
                pltpu.VMEM(wout_t.shape, f32),
                pltpu.SemaphoreType.DMA((3,)),
            ],
        ),
        out_shape=out_shape,
        compiler_params=params(),
        cost_estimate=pl.CostEstimate(
            flops=grid_rows * width * width, bytes_accessed=10 * grid_rows * width, transcendentals=0
        ),
        name="middle",
    )(place, kept_near(everyone), *small[1:-3], *map(kept_near, sums[1:]), agg, grid_embed)


def scatter_step(slots, gp_ref, lead_ref, idx_ref, hot, prod, acc):
    nodes, half = acc.shape
    wide = lead_ref.shape[0]

    @pl.when(pl.program_id(0) == 0)
    def _():
        acc[...] = jnp.zeros_like(acc)

    node = lax.broadcasted_iota(jnp.int32, (nodes, wide), 0)
    for k in range(slots):
        hot[:, k * wide : (k + 1) * wide] = jnp.where(node == idx_ref[k : k + 1, :], 1.0, 0.0).astype(bf16)
    for start in range(0, wide, TILE):
        lead = lead_ref[start : start + TILE, :]
        for k in range(slots):
            at = start * slots + k * TILE
            to = k * wide + start
            prod[to : to + TILE, :] = gp_ref[at : at + TILE, :] * lead
    for n in range(half // NCOL):
        here = slice(n * NCOL, (n + 1) * NCOL)
        acc[:, here] += jnp.dot(hot[...], prod[:, here], preferred_element_type=f32)


def backward_kernel(
    slots,
    place_ref,
    gp_ref,
    lead_ref,
    idx_ref,
    lower_ref,
    centre_ref,
    upper_ref,
    own_ref,
    far_ref,
    hot,
    prod,
    acc,
):
    scatter_step(slots, gp_ref, lead_ref, idx_ref, hot, prod, acc)

    @pl.when(pl.program_id(0) == pl.num_programs(0) - 1)
    def _():
        core = place_ref[0]
        half = own_ref.shape[1]
        block = lower_ref.shape[0]
        for i, ref in enumerate((lower_ref, centre_ref, upper_ref)):
            ref[...] = acc[i * block : (i + 1) * block, :].astype(bf16)
        own_ref[...] = acc[:, pl.ds(pl.multiple_of(core * half, half), half)].astype(bf16)
        far_ref[...] = acc[:, pl.ds(pl.multiple_of((1 - core) * half, half), half)].astype(bf16)


def backward(place, gp, lead, idx_t, nodes):
    grid_rows, width = lead.shape
    slots = idx_t.shape[0]
    rows = BACK * TILE
    out_shape = [jax.ShapeDtypeStruct((nodes // 3, width), bf16)] * 3 + [
        pltpu.VMEM((nodes, width // 2), bf16)
    ] * 2
    return pl.pallas_call(
        functools.partial(backward_kernel, slots),
        grid_spec=prefetched(
            grid_rows // rows,
            [
                pl.BlockSpec((rows * slots, width), lambda t, place: (t, 0)),
                pl.BlockSpec((rows, width), lambda t, place: (t, 0)),
                pl.BlockSpec((slots, rows), lambda t, place: (0, t)),
            ],
            [whole(x) for x in out_shape[:3]] + [landed()] * 2,
            [
                pltpu.VMEM((nodes, rows * slots), bf16),
                pltpu.VMEM((rows * slots, width), bf16),
                pltpu.VMEM((nodes, width), f32),
            ],
        ),
        out_shape=out_shape,
        compiler_params=params(),
        cost_estimate=pl.CostEstimate(flops=gp.size * 512, bytes_accessed=2 * gp.size, transcendentals=0),
        name="backward",
    )(place, gp, lead, idx_t)


def pack_kernel(
    place_ref, below_ref, here_ref, above_ref, edge_ref, own_ref, far_ref, dst_ref, dstfar_ref, total_ref
):
    low = place_ref[0] == 0
    below, here, above, edge = below_ref[...], here_ref[...], above_ref[...], edge_ref[...]
    first = (((0,), (0,)), ((), ()))
    half = own_ref.shape[1]
    mine = jnp.concatenate([below, here, above], axis=0)
    other = jnp.concatenate(
        [jnp.where(low, here, edge), jnp.where(low, above, below), jnp.where(low, edge, here)], axis=0
    )
    product = lax.dot_general(mine, own_ref[...], first, preferred_element_type=f32)
    product = product + lax.dot_general(other, far_ref[...], first, preferred_element_type=f32)
    chunks, rows, columns = total_ref.shape
    total_ref[:, :, :half] = product.astype(bf16).reshape(chunks, rows, half)
    per_zh = dst_ref.shape[0]
    at = pl.ds(pl.program_id(0) * per_zh, per_zh)
    both = dst_ref[...].astype(f32) + dstfar_ref[at].astype(f32)
    few = both.shape[2]
    outs = columns - half - few
    some = both[:, : both.shape[1] - outs].astype(bf16)
    total_ref[:, :, half : half + few] = some.reshape(chunks, rows, few)
    some = jnp.concatenate([both[i, both.shape[1] - outs :] for i in range(both.shape[0])], axis=1)
    total_ref[:, :, half + few :] = some.T.astype(bf16).reshape(chunks, rows, outs)


def pack(place, feats, edge, own, far, dst_own, dst_far, chunks):
    nodes, width = feats[0].shape
    per_zh = (dst_own.shape[0] // GROUPS,) + dst_own.shape[1:]
    outs = dst_own.shape[1] - width // dst_own.shape[0]
    columns = width // 2 + dst_own.shape[2] + outs
    rows = width // chunks
    feat = pl.BlockSpec((nodes, width // GROUPS), lambda t, place: (0, t))
    dst = pl.BlockSpec(per_zh, lambda t, place: (t, 0, 0))
    return pl.pallas_call(
        pack_kernel,
        grid_spec=prefetched(
            GROUPS,
            [feat] * 4 + [landed(), landed(), dst, landed()],
            pl.BlockSpec((chunks, rows // GROUPS, columns), lambda t, place: (0, t, 0)),
            [],
        ),
        out_shape=jax.ShapeDtypeStruct((chunks, rows, columns), bf16),
        compiler_params=params(),
        cost_estimate=pl.CostEstimate(
            flops=4 * width * own.size, bytes_accessed=4 * width * width, transcendentals=0
        ),
        name="pack",
    )(place, *feats, edge, kept_near(own), kept_near(far), dst_own, kept_near(dst_far))


def join_kernel(parts_ref, total_ref):
    half = total_ref.shape[2] - parts_ref.shape[2]
    half = half * QUARTERS // (QUARTERS - 1)
    few = half // QUARTERS
    each = parts_ref.shape[0] // QUARTERS
    pieces = []
    ends = 0.0
    for x in range(QUARTERS):
        some = parts_ref[x * each].astype(f32)
        for y in range(1, each):
            some = some + parts_ref[x * each + y].astype(f32)
        pieces.append(some[:, half : half + few])
        ends = ends + some
    total = jnp.concatenate([ends[:, :half]] + pieces + [ends[:, half + few :]], axis=1).astype(bf16)
    for i in range(total_ref.shape[0]):
        rows = total_ref.shape[1]
        total_ref[i] = total[i * rows : (i + 1) * rows, :]


def join(parts, rows_out, half):
    sources, rows, columns = parts.shape
    wide = columns - half // QUARTERS + half
    count = rows // rows_out
    return pl.pallas_call(
        join_kernel,
        grid=(GROUPS,),
        in_specs=[pl.BlockSpec((sources, rows // GROUPS, columns), lambda t: (0, t, 0))],
        out_specs=pl.BlockSpec((count // GROUPS, rows_out, wide), lambda t: (t, 0, 0)),
        out_shape=jax.ShapeDtypeStruct((count, rows_out, wide), bf16),
        compiler_params=params(),
        cost_estimate=pl.CostEstimate(flops=parts.size, bytes_accessed=2 * parts.size, transcendentals=0),
        name="join",
    )(parts)


def body(
    mesh_feats,
    grid_embed,
    w_src,
    w_dst,
    w_out,
    truth,
    area_weight,
    var_weight,
    neighbour,
    edge_mask,
):
    own = mesh_feats[0]
    node_rows, width = own.shape
    grid_rows, slots = neighbour.shape
    half = width // 2
    space_count = lax.axis_size(SPACE)
    block_id = lax.axis_index(SPACE)
    members = lax.axis_size(ENS)
    swap = [(0, 1), (1, 0)]
    here = [lax.axis_index(name) for name in ("c", "x", "zh", "y")]
    place = jnp.stack(here).astype(jnp.int32)

    below = shifted(own, SPACE, 1)
    above = shifted(own, SPACE, -1)

    dst = jnp.dot(grid_embed, w_dst, preferred_element_type=f32).astype(bf16)
    local = jnp.mod(neighbour.T - (block_id - 1) * node_rows, node_rows * space_count)
    idx_t = jnp.where(edge_mask.T > 0, local, -1)
    wout_t = w_out.T
    truth_t = truth.T
    var = var_weight[:, None]
    area = area_weight[None, :]
    dst, idx_t, place, below = lax.optimization_barrier((dst, idx_t, place, below))
    feats = (below, own, above)
    chunks = lax.axis_size(FIRST)
    gp, agg, pred, sent, kept, *pieces = forward(
        place, *feats, w_src, dst, idx_t, wout_t, members
    )
    sums = [kept] + [shifted(piece, "x", d + 1) for d, piece in enumerate(pieces)]
    everyone = lax.all_to_all(sent, ENS, 0, 0, tiled=True)
    low = place[0] == 0
    edge = lax.ppermute(jnp.where(low, below, above), "c", swap)
    everyone, edge = lax.optimization_barrier((everyone, edge))
    lead, dst_own, dst_far = middle(
        place, everyone, pred, truth_t, area, var, wout_t, idx_t, sums, agg, grid_embed
    )
    dst_far = lax.ppermute(dst_far, "c", swap)

    lower, centre, upper, wide_own, wide_far = backward(place, gp, lead, idx_t, 3 * node_rows)
    wide_far = lax.ppermute(wide_far, "c", swap)
    from_above = shifted(lower, SPACE, -1)
    from_below = shifted(upper, SPACE, 1)

    total = pack(place, feats, edge, wide_own, wide_far, dst_own, dst_far, chunks)
    parts = lax.all_to_all(total, FIRST, 0, 0, tiled=True)
    few = half // QUARTERS
    rows_out = width // lax.axis_size(ENS + SPACE)

    total = join(parts, rows_out, half)
    total, from_above, from_below = lax.optimization_barrier((total, from_above, from_below))
    parts = lax.all_to_all(total, SECOND, 0, 0, tiled=True)
    dproj = (centre.astype(f32) + from_above.astype(f32) + from_below.astype(f32)).astype(bf16)
    grad_mesh = lax.dot_general(
        dproj, w_src, (((1,), (1,)), ((), ())), preferred_element_type=f32
    ).astype(bf16)
    total = jnp.sum(parts.reshape(-1, 2, rows_out, parts.shape[2]).astype(f32), axis=0)
    joined = lambda a, b: jnp.concatenate([total[0, :, a:b], total[1, :, a:b]], axis=1)
    dst_final = total[:, :, half : 2 * half].reshape(2, rows_out, QUARTERS, few)
    dst_final = dst_final.transpose(1, 2, 0, 3).reshape(rows_out, width)
    return (
        grad_mesh[None],
        joined(0, half),
        dst_final,
        joined(2 * half, total.shape[-1]),
    )


def solution(mesh):
    fine = Mesh(mesh.devices.reshape(2, 4, 4, 4, 2), ("zh", "x", "y", "zl", "c"))
    everywhere = ENS + SPACE
    in_specs = (
        P(ENS, SPACE, None),
        P(SPACE, None),
        P(),
        P(),
        P(),
        P(SPACE, None),
        P(SPACE),
        P(),
        P(SPACE, None),
        P(SPACE, None),
    )
    out_specs = (
        P(ENS, SPACE, None),
        P(everywhere, None),
        P(everywhere, None),
        P(everywhere, None),
    )
    return jax.shard_map(body, mesh=fine, in_specs=in_specs, out_specs=out_specs, check_vma=False)
```

```python
import functools
import jax
import jax.numpy as jnp
from jax import lax
from jax.experimental import pallas as pl
from jax.experimental.pallas import tpu as pltpu
from jax.sharding import Mesh, PartitionSpec as P

loss_scale = 8.0
smooth_sq = 0.01
TILE = 64
NCOL = 256
ROWS = 32
GROUP = 4
VMEM_LIMIT = 56 * 1024 * 1024
BACK = 2
GROUPS = 2
QUARTERS = 4
f32 = jnp.float32
bf16 = jnp.bfloat16
SPACE = ("y", "zl", "c")
ENS = ("zh", "x")
FIRST = ("x", "y")
SECOND = ("zh", "zl", "c")


def shifted(block, axes, distance):
    count = lax.axis_size(axes)
    return lax.ppermute(block, axes, [(i, (i + distance) % count) for i in range(count)])


def smooth_grad(diff):
    return diff * lax.rsqrt(diff * diff + smooth_sq)


def gelu_parts(v):
    c0 = 0.7978845608
    c1 = c0 * 0.044715
    sq = v * v
    t = jnp.tanh(v * (c0 + c1 * sq))
    u = 1.0 + t
    slope = v * (c0 + (3.0 * c1) * sq)
    return v * u, u * (1.0 + (1.0 - t) * slope)


def whole(array):
    zeros = (0,) * len(array.shape)
    return pl.BlockSpec(array.shape, lambda *_: zeros)


def landed():
    return pl.BlockSpec(memory_space=pltpu.VMEM)


def kept_near(array):
    return pltpu.with_memory_space_constraint(array, pltpu.VMEM)


def params():
    return pltpu.CompilerParams(vmem_limit_bytes=VMEM_LIMIT)


def give(ref, columns, values):
    chunks, rows = ref.shape[0], ref.shape[1] // GROUPS
    for zh in range(GROUPS):
        some = values[zh * chunks * rows : (zh + 1) * chunks * rows, :].astype(ref.dtype)
        ref[:, zh * rows : (zh + 1) * rows, columns] = some.reshape(chunks, rows, some.shape[1])


def scale_column(idx_ref):
    used = jnp.sum(jnp.where(idx_ref[...] >= 0, 1.0, 0.0), axis=0, keepdims=True)
    return jnp.broadcast_to(0.5 / used, (8, used.shape[1])).T[:, :1]


def forward_kernel(
    slots,
    members,
    place_ref,
    below_ref,
    here_ref,
    above_ref,
    wsrc_ref,
    dst_ref,
    idxt_ref,
    wout_ref,
    gp_ref,
    agg_ref,
    pred_ref,
    sent_ref,
    *rest,
):
    piece_refs = rest[:QUARTERS]
    forward_steps(
        slots,
        members,
        place_ref[1],
        (below_ref, here_ref, above_ref),
        wsrc_ref,
        dst_ref,
        idxt_ref,
        wout_ref,
        gp_ref,
        agg_ref,
        pred_ref,
        sent_ref,
        piece_refs,
        *rest[QUARTERS:],
    )


def forward_steps(
    slots,
    members,
    along,
    feat_refs,
    wsrc_ref,
    dst_ref,
    idxt_ref,
    wout_ref,
    gp_ref,
    agg_ref,
    pred_ref,
    sent_ref,
    piece_refs,
    feats,
    rhs,
    hot,
    pre,
    idx_all,
    scale_all,
    sums,
):
    step = pl.program_id(0)
    nodes, width = feats.shape
    depth = rhs.shape[0]
    tile = depth - nodes
    block = feat_refs[0].shape[0]

    @pl.when(step == 0)
    def _():
        idx_all[...] = idxt_ref[...].astype(f32).T.astype(jnp.int32)
        scale_all[...] = scale_column(idxt_ref)
        for i, ref in enumerate(feat_refs):
            feats[i * block : (i + 1) * block, :] = ref[...]
        for n in range(width // NCOL):
            cols = slice(n * NCOL, (n + 1) * NCOL)
            rhs[:nodes, cols] = jnp.dot(
                feats[...], wsrc_ref[:, cols], preferred_element_type=f32
            ).astype(bf16)

    base = pl.multiple_of(step * tile, tile)
    rhs[nodes:, :] = dst_ref[...]
    lane = lax.broadcasted_iota(jnp.int32, (tile, depth), 1)
    row = lax.broadcasted_iota(jnp.int32, (tile, depth), 0)
    eye = lane == row + nodes
    idx = idx_all[pl.ds(base, tile), :]
    for k in range(slots):
        col = idx[:, k : k + 1]
        hit = (lane == col) | (eye & (col >= 0))
        hot[k * tile : (k + 1) * tile, :] = jnp.where(hit, 1.0, 0.0).astype(bf16)
    for n in range(width // NCOL):
        cols = slice(n * NCOL, (n + 1) * NCOL)
        pre[n % 2] = jnp.dot(hot[...], rhs[:, cols], preferred_element_type=f32).astype(bf16)
        for r in range(0, tile, ROWS):
            acc_g = jnp.zeros((ROWS, NCOL), f32)
            acc_s = jnp.zeros((ROWS, NCOL), f32)
            for k in range(slots):
                rows = slice(k * tile + r, k * tile + r + ROWS)
                value, grad = gelu_parts(pre[n % 2, rows, :])
                gp_ref[rows, cols] = grad
                if k % GROUP == 0:
                    some_g, some_s = value, grad
                else:
                    some_g, some_s = some_g + value, some_s + grad
                if k % GROUP == GROUP - 1:
                    acc_g = acc_g + some_g.astype(f32)
                    acc_s = acc_s + some_s.astype(f32)
            scale = scale_all[pl.ds(pl.multiple_of(base + r, ROWS), ROWS), :]
            agg_ref[pl.ds(pl.multiple_of(base + r, ROWS), ROWS), cols] = (acc_g * scale).astype(bf16)
            sums[n, r : r + ROWS, :] = (acc_s - (slots - 0.5 / scale)).astype(bf16)

    for d, ref in enumerate(piece_refs):
        ref[...] = sums[(along + d) % QUARTERS]

    @pl.when(step == pl.num_programs(0) - 1)
    def _():
        pred = lax.dot_general(
            wout_ref[...], agg_ref[...], (((1,), (1,)), ((), ())), preferred_element_type=f32
        )
        pred_ref[...] = pred
        for e in range(members):
            sent_ref[e] = pred.astype(bf16)


def forward(place, below, here, above, w_src, dst, idx_t, wout_t, members):
    grid_rows, width = dst.shape
    nodes = 3 * here.shape[0]
    slots = idx_t.shape[0]
    outs = wout_t.shape[0]
    step = lambda t, place: (t, 0)
    out_shape = [
        jax.ShapeDtypeStruct((grid_rows * slots, width), bf16),
        jax.ShapeDtypeStruct((grid_rows, width), bf16),
        jax.ShapeDtypeStruct((outs, grid_rows), f32),
        jax.ShapeDtypeStruct((members, outs, grid_rows), bf16),
    ] + [jax.ShapeDtypeStruct((grid_rows, NCOL), bf16)] * QUARTERS
    return pl.pallas_call(
        functools.partial(forward_kernel, slots, members),
        grid_spec=prefetched(
            grid_rows // TILE,
            [landed(), whole(here), landed(), whole(w_src)]
            + [pl.BlockSpec((TILE, width), step), whole(idx_t), whole(wout_t)],
            [pl.BlockSpec((TILE * slots, width), step)]
            + [whole(x) for x in out_shape[1:4]]
            + [pl.BlockSpec((TILE, NCOL), step)] * QUARTERS,
            [
                pltpu.VMEM((nodes, width), bf16),
                pltpu.VMEM((nodes + TILE, width), bf16),
                pltpu.VMEM((TILE * slots, nodes + TILE), bf16),
                pltpu.VMEM((2, TILE * slots, NCOL), bf16),
                pltpu.VMEM((grid_rows, slots), jnp.int32),
                pltpu.VMEM((grid_rows, 1), f32),
                pltpu.VMEM((QUARTERS, TILE, NCOL), bf16),
            ],
        ),
        out_shape=out_shape,
        compiler_params=params(),
        cost_estimate=pl.CostEstimate(
            flops=2 * grid_rows * slots * 256 * width,
            bytes_accessed=2 * grid_rows * slots * width,
            transcendentals=grid_rows * slots * width,
        ),
        name="forward",
    )(place, kept_near(below), here, kept_near(above), w_src, dst, idx_t, wout_t)


def middle_kernel(
    place_ref,
    every_ref,
    pred_ref,
    truth_ref,
    area_ref,
    var_ref,
    wout_ref,
    idxt_ref,
    sum0_ref,
    sum1_ref,
    sum2_ref,
    sum3_ref,
    agg_hbm,
    grid_hbm,
    lead_hbm,
    own_ref,
    far_ref,
    agg_ref,
    grid_ref,
    lead_ref,
    ddst,
    part_ref,
    sems,
):
    loads = [
        pltpu.make_async_copy(agg_hbm, agg_ref, sems.at[0]),
        pltpu.make_async_copy(grid_hbm, grid_ref, sems.at[1]),
    ]
    store = pltpu.make_async_copy(lead_ref, lead_hbm, sems.at[2])
    for copy in loads:
        copy.start()
    width = wout_ref.shape[1]
    members = every_ref.shape[0]
    near, columns = QUARTERS, sum0_ref.shape[1]
    core, x, zh = place_ref[0], place_ref[1], place_ref[2]
    weighting = loss_scale * area_ref[...] * var_ref[...]

    def dpred_of(pred):
        pair = -smooth_grad(pred - pred.astype(bf16).astype(f32))
        for e in range(members):
            pair = pair + smooth_grad(pred - every_ref[e].astype(f32))
        against = smooth_grad(pred - truth_ref[...]) / members
        return (weighting * (against - pair / (members * (members - 1)))).astype(bf16)

    scale = scale_column(idxt_ref)
    first = (((0,), (0,)), ((), ()))
    dpred = dpred_of(pred_ref[...])
    for n in range(width // NCOL):
        cols = slice(n * NCOL, (n + 1) * NCOL)
        dagg = lax.dot_general(dpred, wout_ref[:, cols], first, preferred_element_type=f32)
        lead_ref[:, cols] = (dagg * scale).astype(bf16)
    store.start()

    quarter = wout_ref[:, pl.ds(pl.multiple_of(x * columns, columns), columns)]
    total = jnp.zeros(sum0_ref.shape, f32)
    for d, sum_ref in enumerate((sum0_ref, sum1_ref, sum2_ref, sum3_ref)):
        other = dpred_of(every_ref[zh * near + (x + near - d) % near].astype(f32))
        dagg = lax.dot_general(other, quarter, first, preferred_element_type=f32)
        total = total + dagg * sum_ref[...].astype(f32)
    ddst[...] = (total * scale).astype(bf16)

    for copy in loads:
        copy.wait()
    part_ref[...] = jnp.dot(dpred, agg_ref[...], preferred_element_type=f32)
    chunks, rows, few = own_ref.shape
    outs = part_ref.shape[0] // 2
    rows = rows - outs
    for ref, which in ((far_ref, 1 - core), (own_ref, core)):
        product = jnp.dot(
            grid_ref[...],
            ddst[:, pl.ds(pl.multiple_of(which * few, few), few)],
            preferred_element_type=f32,
        )
        ref[:, :rows, :] = product.astype(bf16).reshape(chunks, rows, few)
        at = pl.ds(pl.multiple_of(which * outs, outs), outs)
        for chunk in range(chunks):
            ref[chunk, rows:, :] = part_ref[at, chunk * few : (chunk + 1) * few].astype(bf16)
    store.wait()


def prefetched(count, ins, outs, scratch):
    return pltpu.PrefetchScalarGridSpec(
        num_scalar_prefetch=1, grid=(count,), in_specs=ins, out_specs=outs, scratch_shapes=scratch
    )


def middle(place, everyone, pred, truth_t, area, var, wout_t, idx_t, sums, agg, grid_t):
    grid_rows, width = agg.shape
    columns = sums[0].shape[1]
    chunks = GROUPS * QUARTERS
    product = (chunks, width // chunks + wout_t.shape[0] // 2, columns // 2)
    anywhere = pl.BlockSpec(memory_space=pl.ANY)
    small = (everyone, pred, truth_t, area, var, wout_t, idx_t, *sums)
    out_shape = [
        jax.ShapeDtypeStruct((grid_rows, width), bf16),
        jax.ShapeDtypeStruct(product, bf16),
        jax.ShapeDtypeStruct(product, bf16),
    ]
    return pl.pallas_call(
        middle_kernel,
        grid_spec=prefetched(
            1,
            [landed()]
            + [whole(x) for x in small[1 : -len(sums)]]
            + [whole(sums[0])]
            + [landed()] * (len(sums) - 1)
            + [anywhere] * 2,
            [anywhere] + [whole(x) for x in out_shape[1:]],
            [
                pltpu.VMEM((grid_rows, width), bf16),
                pltpu.VMEM((width, grid_rows), bf16),
                pltpu.VMEM((grid_rows, width), bf16),
                pltpu.VMEM((grid_rows, columns), bf16),
                pltpu.VMEM(wout_t.shape, f32),
                pltpu.SemaphoreType.DMA((3,)),
            ],
        ),
        out_shape=out_shape,
        compiler_params=params(),
        cost_estimate=pl.CostEstimate(
            flops=grid_rows * width * width, bytes_accessed=10 * grid_rows * width, transcendentals=0
        ),
        name="middle",
    )(place, kept_near(everyone), *small[1:-3], *map(kept_near, sums[1:]), agg, grid_t)


def scatter_step(slots, gp_ref, lead_ref, idx_ref, hot, prod, acc):
    nodes, half = acc.shape
    wide = lead_ref.shape[0]

    @pl.when(pl.program_id(0) == 0)
    def _():
        acc[...] = jnp.zeros_like(acc)

    node = lax.broadcasted_iota(jnp.int32, (nodes, wide), 0)
    for k in range(slots):
        hot[:, k * wide : (k + 1) * wide] = jnp.where(node == idx_ref[k : k + 1, :], 1.0, 0.0).astype(bf16)
    for start in range(0, wide, TILE):
        lead = lead_ref[start : start + TILE, :]
        for k in range(slots):
            at = start * slots + k * TILE
            to = k * wide + start
            prod[to : to + TILE, :] = gp_ref[at : at + TILE, :] * lead
    for n in range(half // NCOL):
        here = slice(n * NCOL, (n + 1) * NCOL)
        acc[:, here] += jnp.dot(hot[...], prod[:, here], preferred_element_type=f32)


def backward_kernel(
    slots,
    place_ref,
    gp_ref,
    lead_ref,
    idx_ref,
    lower_ref,
    centre_ref,
    upper_ref,
    own_ref,
    far_ref,
    hot,
    prod,
    acc,
):
    scatter_step(slots, gp_ref, lead_ref, idx_ref, hot, prod, acc)

    @pl.when(pl.program_id(0) == pl.num_programs(0) - 1)
    def _():
        core = place_ref[0]
        half = own_ref.shape[1]
        block = lower_ref.shape[0]
        for i, ref in enumerate((lower_ref, centre_ref, upper_ref)):
            ref[...] = acc[i * block : (i + 1) * block, :].astype(bf16)
        own_ref[...] = acc[:, pl.ds(pl.multiple_of(core * half, half), half)].astype(bf16)
        far_ref[...] = acc[:, pl.ds(pl.multiple_of((1 - core) * half, half), half)].astype(bf16)


def backward(place, gp, lead, idx_t, nodes):
    grid_rows, width = lead.shape
    slots = idx_t.shape[0]
    rows = BACK * TILE
    out_shape = [jax.ShapeDtypeStruct((nodes // 3, width), bf16)] * 3 + [
        pltpu.VMEM((nodes, width // 2), bf16)
    ] * 2
    return pl.pallas_call(
        functools.partial(backward_kernel, slots),
        grid_spec=prefetched(
            grid_rows // rows,
            [
                pl.BlockSpec((rows * slots, width), lambda t, place: (t, 0)),
                pl.BlockSpec((rows, width), lambda t, place: (t, 0)),
                pl.BlockSpec((slots, rows), lambda t, place: (0, t)),
            ],
            [whole(x) for x in out_shape[:3]] + [landed()] * 2,
            [
                pltpu.VMEM((nodes, rows * slots), bf16),
                pltpu.VMEM((rows * slots, width), bf16),
                pltpu.VMEM((nodes, width), f32),
            ],
        ),
        out_shape=out_shape,
        compiler_params=params(),
        cost_estimate=pl.CostEstimate(flops=gp.size * 512, bytes_accessed=2 * gp.size, transcendentals=0),
        name="backward",
    )(place, gp, lead, idx_t)


def pack_kernel(
    place_ref, below_ref, here_ref, above_ref, edge_ref, own_ref, far_ref, dst_ref, dstfar_ref, total_ref
):
    low = place_ref[0] == 0
    below, here, above, edge = below_ref[...], here_ref[...], above_ref[...], edge_ref[...]
    first = (((0,), (0,)), ((), ()))
    half = own_ref.shape[1]
    mine = jnp.concatenate([below, here, above], axis=0)
    other = jnp.concatenate(
        [jnp.where(low, here, edge), jnp.where(low, above, below), jnp.where(low, edge, here)], axis=0
    )
    product = lax.dot_general(mine, own_ref[...], first, preferred_element_type=f32)
    product = product + lax.dot_general(other, far_ref[...], first, preferred_element_type=f32)
    chunks, rows, columns = total_ref.shape
    total_ref[:, :, :half] = product.astype(bf16).reshape(chunks, rows, half)
    per_zh = dst_ref.shape[0]
    at = pl.ds(pl.program_id(0) * per_zh, per_zh)
    both = dst_ref[...].astype(f32) + dstfar_ref[at].astype(f32)
    few = both.shape[2]
    outs = columns - half - few
    some = both[:, : both.shape[1] - outs].astype(bf16)
    total_ref[:, :, half : half + few] = some.reshape(chunks, rows, few)
    some = jnp.concatenate([both[i, both.shape[1] - outs :] for i in range(both.shape[0])], axis=1)
    total_ref[:, :, half + few :] = some.T.astype(bf16).reshape(chunks, rows, outs)


def pack(place, feats, edge, own, far, dst_own, dst_far, chunks):
    nodes, width = feats[0].shape
    per_zh = (dst_own.shape[0] // GROUPS,) + dst_own.shape[1:]
    outs = dst_own.shape[1] - width // dst_own.shape[0]
    columns = width // 2 + dst_own.shape[2] + outs
    rows = width // chunks
    feat = pl.BlockSpec((nodes, width // GROUPS), lambda t, place: (0, t))
    dst = pl.BlockSpec(per_zh, lambda t, place: (t, 0, 0))
    return pl.pallas_call(
        pack_kernel,
        grid_spec=prefetched(
            GROUPS,
            [feat] * 4 + [landed(), landed(), dst, landed()],
            pl.BlockSpec((chunks, rows // GROUPS, columns), lambda t, place: (0, t, 0)),
            [],
        ),
        out_shape=jax.ShapeDtypeStruct((chunks, rows, columns), bf16),
        compiler_params=params(),
        cost_estimate=pl.CostEstimate(
            flops=4 * width * own.size, bytes_accessed=4 * width * width, transcendentals=0
        ),
        name="pack",
    )(place, *feats, edge, kept_near(own), kept_near(far), dst_own, kept_near(dst_far))


def join_kernel(parts_ref, total_ref):
    half = total_ref.shape[2] - parts_ref.shape[2]
    half = half * QUARTERS // (QUARTERS - 1)
    few = half // QUARTERS
    each = parts_ref.shape[0] // QUARTERS
    pieces = []
    ends = 0.0
    for x in range(QUARTERS):
        some = parts_ref[x * each].astype(f32)
        for y in range(1, each):
            some = some + parts_ref[x * each + y].astype(f32)
        pieces.append(some[:, half : half + few])
        ends = ends + some
    total = jnp.concatenate([ends[:, :half]] + pieces + [ends[:, half + few :]], axis=1).astype(bf16)
    for i in range(total_ref.shape[0]):
        rows = total_ref.shape[1]
        total_ref[i] = total[i * rows : (i + 1) * rows, :]


def join(parts, rows_out, half):
    sources, rows, columns = parts.shape
    wide = columns - half // QUARTERS + half
    count = rows // rows_out
    return pl.pallas_call(
        join_kernel,
        grid=(GROUPS,),
        in_specs=[pl.BlockSpec((sources, rows // GROUPS, columns), lambda t: (0, t, 0))],
        out_specs=pl.BlockSpec((count // GROUPS, rows_out, wide), lambda t: (t, 0, 0)),
        out_shape=jax.ShapeDtypeStruct((count, rows_out, wide), bf16),
        compiler_params=params(),
        cost_estimate=pl.CostEstimate(flops=parts.size, bytes_accessed=2 * parts.size, transcendentals=0),
        name="join",
    )(parts)


def body(
    mesh_feats,
    grid_embed,
    w_src,
    w_dst,
    w_out,
    truth,
    area_weight,
    var_weight,
    neighbour,
    edge_mask,
):
    own = mesh_feats[0]
    node_rows, width = own.shape
    grid_rows, slots = neighbour.shape
    half = width // 2
    space_count = lax.axis_size(SPACE)
    block_id = lax.axis_index(SPACE)
    members = lax.axis_size(ENS)
    swap = [(0, 1), (1, 0)]
    here = [lax.axis_index(name) for name in ("c", "x", "zh", "y")]
    place = jnp.stack(here).astype(jnp.int32)

    below = shifted(own, SPACE, 1)
    above = shifted(own, SPACE, -1)

    dst = jnp.dot(grid_embed, w_dst, preferred_element_type=f32).astype(bf16)
    local = jnp.mod(neighbour.T - (block_id - 1) * node_rows, node_rows * space_count)
    idx_t = jnp.where(edge_mask.T > 0, local, -1)
    wout_t = w_out.T
    truth_t = truth.T
    var = var_weight[:, None]
    area = area_weight[None, :]
    grid_t = grid_embed.T
    dst, idx_t, place, grid_t, var, below = lax.optimization_barrier(
        (dst, idx_t, place, grid_t, var, below)
    )
    feats = (below, own, above)
    chunks = lax.axis_size(FIRST)
    gp, agg, pred, sent, kept, *pieces = forward(
        place, *feats, w_src, dst, idx_t, wout_t, members
    )
    sums = [kept] + [shifted(piece, "x", d + 1) for d, piece in enumerate(pieces)]
    everyone = lax.all_to_all(sent, ENS, 0, 0, tiled=True)
    low = place[0] == 0
    edge = lax.ppermute(jnp.where(low, below, above), "c", swap)
    everyone, edge = lax.optimization_barrier((everyone, edge))
    lead, dst_own, dst_far = middle(
        place, everyone, pred, truth_t, area, var, wout_t, idx_t, sums, agg, grid_t
    )
    dst_far = lax.ppermute(dst_far, "c", swap)

    lower, centre, upper, wide_own, wide_far = backward(place, gp, lead, idx_t, 3 * node_rows)
    wide_far = lax.ppermute(wide_far, "c", swap)
    total = pack(place, feats, edge, wide_own, wide_far, dst_own, dst_far, chunks)
    parts = lax.all_to_all(total, FIRST, 0, 0, tiled=True)

    parts, lower, upper = lax.optimization_barrier((parts, lower, upper))
    from_above = shifted(lower, SPACE, -1)
    from_below = shifted(upper, SPACE, 1)
    few = half // QUARTERS
    rows_out = width // lax.axis_size(ENS + SPACE)

    total = join(parts, rows_out, half)
    parts = lax.all_to_all(total, SECOND, 0, 0, tiled=True)
    dproj = (centre.astype(f32) + from_above.astype(f32) + from_below.astype(f32)).astype(bf16)
    grad_mesh = lax.dot_general(
        dproj, w_src, (((1,), (1,)), ((), ())), preferred_element_type=f32
    ).astype(bf16)
    total = jnp.sum(parts.reshape(-1, 2, rows_out, parts.shape[2]).astype(f32), axis=0)
    joined = lambda a, b: jnp.concatenate([total[0, :, a:b], total[1, :, a:b]], axis=1)
    dst_final = total[:, :, half : 2 * half].reshape(2, rows_out, QUARTERS, few)
    dst_final = dst_final.transpose(1, 2, 0, 3).reshape(rows_out, width)
    return (
        grad_mesh[None],
        joined(0, half),
        dst_final,
        joined(2 * half, total.shape[-1]),
    )


def solution(mesh):
    fine = Mesh(mesh.devices.reshape(2, 4, 4, 4, 2), ("zh", "x", "y", "zl", "c"))
    everywhere = ENS + SPACE
    in_specs = (
        P(ENS, SPACE, None),
        P(SPACE, None),
        P(),
        P(),
        P(),
        P(SPACE, None),
        P(SPACE),
        P(),
        P(SPACE, None),
        P(SPACE, None),
    )
    out_specs = (
        P(ENS, SPACE, None),
        P(everywhere, None),
        P(everywhere, None),
        P(everywhere, None),
    )
    return jax.shard_map(body, mesh=fine, in_specs=in_specs, out_specs=out_specs, check_vma=False)
```

```python
import functools
import jax
import jax.numpy as jnp
from jax import lax
from jax.experimental import pallas as pl
from jax.experimental.pallas import tpu as pltpu
from jax.sharding import Mesh, PartitionSpec as P

loss_scale = 8.0
smooth_sq = 0.01
TILE = 64
NCOL = 256
ROWS = 32
GROUP = 4
VMEM_LIMIT = 56 * 1024 * 1024
BACK = 2
GROUPS = 2
QUARTERS = 4
f32 = jnp.float32
bf16 = jnp.bfloat16
SPACE = ("y", "zl", "c")
ENS = ("zh", "x")
FIRST = ("x", "y")
SECOND = ("zh", "zl", "c")


def shifted(block, axes, distance):
    count = lax.axis_size(axes)
    return lax.ppermute(block, axes, [(i, (i + distance) % count) for i in range(count)])


def smooth_grad(diff):
    return diff * lax.rsqrt(diff * diff + smooth_sq)


def gelu_parts(v):
    c0 = 0.7978845608
    c1 = c0 * 0.044715
    sq = v * v
    t = jnp.tanh(v * (c0 + c1 * sq))
    u = 1.0 + t
    slope = v * (c0 + (3.0 * c1) * sq)
    return v * u, u * (1.0 + (1.0 - t) * slope)


def whole(array):
    zeros = (0,) * len(array.shape)
    return pl.BlockSpec(array.shape, lambda *_: zeros)


def landed():
    return pl.BlockSpec(memory_space=pltpu.VMEM)


def kept_near(array):
    return pltpu.with_memory_space_constraint(array, pltpu.VMEM)


def params():
    return pltpu.CompilerParams(vmem_limit_bytes=VMEM_LIMIT)


def give(ref, columns, values):
    chunks, rows = ref.shape[0], ref.shape[1] // GROUPS
    for zh in range(GROUPS):
        some = values[zh * chunks * rows : (zh + 1) * chunks * rows, :].astype(ref.dtype)
        ref[:, zh * rows : (zh + 1) * rows, columns] = some.reshape(chunks, rows, some.shape[1])


def scale_column(idx_ref):
    used = jnp.sum(jnp.where(idx_ref[...] >= 0, 1.0, 0.0), axis=0, keepdims=True)
    return jnp.broadcast_to(0.5 / used, (8, used.shape[1])).T[:, :1]


def forward_kernel(
    slots,
    members,
    place_ref,
    below_ref,
    here_ref,
    above_ref,
    wsrc_ref,
    dst_ref,
    idxt_ref,
    wout_ref,
    gp_ref,
    agg_ref,
    pred_ref,
    sent_ref,
    *rest,
):
    piece_refs = rest[:QUARTERS]
    forward_steps(
        slots,
        members,
        place_ref[1],
        (below_ref, here_ref, above_ref),
        wsrc_ref,
        dst_ref,
        idxt_ref,
        wout_ref,
        gp_ref,
        agg_ref,
        pred_ref,
        sent_ref,
        piece_refs,
        *rest[QUARTERS:],
    )


def forward_steps(
    slots,
    members,
    along,
    feat_refs,
    wsrc_ref,
    dst_ref,
    idxt_ref,
    wout_ref,
    gp_ref,
    agg_ref,
    pred_ref,
    sent_ref,
    piece_refs,
    feats,
    rhs,
    hot,
    pre,
    idx_all,
    scale_all,
    sums,
):
    step = pl.program_id(0)
    nodes, width = feats.shape
    depth = rhs.shape[0]
    tile = depth - nodes
    block = feat_refs[0].shape[0]

    @pl.when(step == 0)
    def _():
        idx_all[...] = idxt_ref[...].astype(f32).T.astype(jnp.int32)
        scale_all[...] = scale_column(idxt_ref)
        for i, ref in enumerate(feat_refs):
            feats[i * block : (i + 1) * block, :] = ref[...]
        for n in range(width // NCOL):
            cols = slice(n * NCOL, (n + 1) * NCOL)
            rhs[:nodes, cols] = jnp.dot(
                feats[...], wsrc_ref[:, cols], preferred_element_type=f32
            ).astype(bf16)

    base = pl.multiple_of(step * tile, tile)
    rhs[nodes:, :] = dst_ref[...]
    lane = lax.broadcasted_iota(jnp.int32, (tile, depth), 1)
    row = lax.broadcasted_iota(jnp.int32, (tile, depth), 0)
    eye = lane == row + nodes
    idx = idx_all[pl.ds(base, tile), :]
    for k in range(slots):
        col = idx[:, k : k + 1]
        hit = (lane == col) | (eye & (col >= 0))
        hot[k * tile : (k + 1) * tile, :] = jnp.where(hit, 1.0, 0.0).astype(bf16)
    for n in range(width // NCOL):
        cols = slice(n * NCOL, (n + 1) * NCOL)
        pre[n % 2] = jnp.dot(hot[...], rhs[:, cols], preferred_element_type=f32).astype(bf16)
        for r in range(0, tile, ROWS):
            acc_g = jnp.zeros((ROWS, NCOL), f32)
            acc_s = jnp.zeros((ROWS, NCOL), f32)
            for k in range(slots):
                rows = slice(k * tile + r, k * tile + r + ROWS)
                value, grad = gelu_parts(pre[n % 2, rows, :])
                gp_ref[rows, cols] = grad
                if k % GROUP == 0:
                    some_g, some_s = value, grad
                else:
                    some_g, some_s = some_g + value, some_s + grad
                if k % GROUP == GROUP - 1:
                    acc_g = acc_g + some_g.astype(f32)
                    acc_s = acc_s + some_s.astype(f32)
            scale = scale_all[pl.ds(pl.multiple_of(base + r, ROWS), ROWS), :]
            agg_ref[pl.ds(pl.multiple_of(base + r, ROWS), ROWS), cols] = (acc_g * scale).astype(bf16)
            sums[n, r : r + ROWS, :] = (acc_s - (slots - 0.5 / scale)).astype(bf16)

    for d, ref in enumerate(piece_refs):
        ref[...] = sums[(along + d) % QUARTERS]

    @pl.when(step == pl.num_programs(0) - 1)
    def _():
        pred = lax.dot_general(
            wout_ref[...], agg_ref[...], (((1,), (1,)), ((), ())), preferred_element_type=f32
        )
        pred_ref[...] = pred
        for e in range(members):
            sent_ref[e] = pred.astype(bf16)


def forward(place, below, here, above, w_src, dst, idx_t, wout_t, members):
    grid_rows, width = dst.shape
    nodes = 3 * here.shape[0]
    slots = idx_t.shape[0]
    outs = wout_t.shape[0]
    step = lambda t, place: (t, 0)
    out_shape = [
        jax.ShapeDtypeStruct((grid_rows * slots, width), bf16),
        jax.ShapeDtypeStruct((grid_rows, width), bf16),
        jax.ShapeDtypeStruct((outs, grid_rows), f32),
        jax.ShapeDtypeStruct((members, outs, grid_rows), bf16),
    ] + [jax.ShapeDtypeStruct((grid_rows, NCOL), bf16)] * QUARTERS
    return pl.pallas_call(
        functools.partial(forward_kernel, slots, members),
        grid_spec=prefetched(
            grid_rows // TILE,
            [landed(), whole(here), landed(), whole(w_src)]
            + [pl.BlockSpec((TILE, width), step), whole(idx_t), whole(wout_t)],
            [pl.BlockSpec((TILE * slots, width), step)]
            + [whole(x) for x in out_shape[1:4]]
            + [pl.BlockSpec((TILE, NCOL), step)] * QUARTERS,
            [
                pltpu.VMEM((nodes, width), bf16),
                pltpu.VMEM((nodes + TILE, width), bf16),
                pltpu.VMEM((TILE * slots, nodes + TILE), bf16),
                pltpu.VMEM((2, TILE * slots, NCOL), bf16),
                pltpu.VMEM((grid_rows, slots), jnp.int32),
                pltpu.VMEM((grid_rows, 1), f32),
                pltpu.VMEM((QUARTERS, TILE, NCOL), bf16),
            ],
        ),
        out_shape=out_shape,
        compiler_params=params(),
        cost_estimate=pl.CostEstimate(
            flops=2 * grid_rows * slots * 256 * width,
            bytes_accessed=2 * grid_rows * slots * width,
            transcendentals=grid_rows * slots * width,
        ),
        name="forward",
    )(place, kept_near(below), here, kept_near(above), w_src, dst, idx_t, wout_t)


def middle_step(
    place_ref,
    every_ref,
    pred_ref,
    truth_ref,
    area_ref,
    var_ref,
    wout_ref,
    idxt_ref,
    sum_refs,
    agg_hbm,
    grid_hbm,
    lead_ref,
    own_ref,
    far_ref,
    agg_ref,
    grid_ref,
    ddst,
    part_ref,
    sems,
):
    loads = [
        pltpu.make_async_copy(agg_hbm, agg_ref, sems.at[0]),
        pltpu.make_async_copy(grid_hbm, grid_ref, sems.at[1]),
    ]
    for copy in loads:
        copy.start()
    width = wout_ref.shape[1]
    members = every_ref.shape[0]
    near, columns = QUARTERS, sum_refs[0].shape[1]
    core, x, zh = place_ref[0], place_ref[1], place_ref[2]
    weighting = loss_scale * area_ref[...] * var_ref[...]

    def dpred_of(pred):
        pair = -smooth_grad(pred - pred.astype(bf16).astype(f32))
        for e in range(members):
            pair = pair + smooth_grad(pred - every_ref[e].astype(f32))
        against = smooth_grad(pred - truth_ref[...]) / members
        return (weighting * (against - pair / (members * (members - 1)))).astype(bf16)

    scale = scale_column(idxt_ref)
    first = (((0,), (0,)), ((), ()))
    dpred = dpred_of(pred_ref[...])
    for n in range(width // NCOL):
        cols = slice(n * NCOL, (n + 1) * NCOL)
        dagg = lax.dot_general(dpred, wout_ref[:, cols], first, preferred_element_type=f32)
        lead_ref[:, cols] = (dagg * scale).astype(bf16)

    quarter = wout_ref[:, pl.ds(pl.multiple_of(x * columns, columns), columns)]
    total = jnp.zeros(sum_refs[0].shape, f32)
    for d, sum_ref in enumerate(sum_refs):
        other = dpred_of(every_ref[zh * near + (x + near - d) % near].astype(f32))
        dagg = lax.dot_general(other, quarter, first, preferred_element_type=f32)
        total = total + dagg * sum_ref[...].astype(f32)
    ddst[...] = (total * scale).astype(bf16)

    for copy in loads:
        copy.wait()
    part_ref[...] = jnp.dot(dpred, agg_ref[...], preferred_element_type=f32)
    chunks, rows, few = own_ref.shape
    outs = part_ref.shape[0] // 2
    rows = rows - outs
    for ref, which in ((far_ref, 1 - core), (own_ref, core)):
        product = lax.dot_general(
            grid_ref[...],
            ddst[:, pl.ds(pl.multiple_of(which * few, few), few)],
            first,
            preferred_element_type=f32,
        )
        ref[:, :rows, :] = product.astype(bf16).reshape(chunks, rows, few)
        at = pl.ds(pl.multiple_of(which * outs, outs), outs)
        for chunk in range(chunks):
            ref[chunk, rows:, :] = part_ref[at, chunk * few : (chunk + 1) * few].astype(bf16)


def prefetched(count, ins, outs, scratch):
    return pltpu.PrefetchScalarGridSpec(
        num_scalar_prefetch=1, grid=(count,), in_specs=ins, out_specs=outs, scratch_shapes=scratch
    )


def backward_kernel(
    slots,
    place_ref,
    every_ref,
    pred_ref,
    truth_ref,
    area_ref,
    var_ref,
    wout_ref,
    idxt_ref,
    sum0_ref,
    sum1_ref,
    sum2_ref,
    sum3_ref,
    agg_hbm,
    grid_hbm,
    gp_ref,
    lower_ref,
    centre_ref,
    upper_ref,
    own_ref,
    far_ref,
    dst_ref,
    dstfar_ref,
    lead,
    agg_ref,
    grid_ref,
    ddst,
    part_ref,
    sems,
    hot,
    prod,
    acc,
):
    step = pl.program_id(0)
    nodes, width = acc.shape

    @pl.when(step == 0)
    def _():
        middle_step(
            place_ref,
            every_ref,
            pred_ref,
            truth_ref,
            area_ref,
            var_ref,
            wout_ref,
            idxt_ref,
            (sum0_ref, sum1_ref, sum2_ref, sum3_ref),
            agg_hbm,
            grid_hbm,
            lead,
            dst_ref,
            dstfar_ref,
            agg_ref,
            grid_ref,
            ddst,
            part_ref,
            sems,
        )
        acc[...] = jnp.zeros_like(acc)

    wide = gp_ref.shape[0] // slots
    base = pl.multiple_of(step * wide, wide)
    node = lax.broadcasted_iota(jnp.int32, (nodes, wide), 0)
    idx = idxt_ref[:, pl.ds(base, wide)]
    for k in range(slots):
        hot[:, k * wide : (k + 1) * wide] = jnp.where(node == idx[k : k + 1, :], 1.0, 0.0).astype(bf16)
    for start in range(0, wide, TILE):
        some = lead[pl.ds(pl.multiple_of(base + start, TILE), TILE), :]
        for k in range(slots):
            at = start * slots + k * TILE
            to = k * wide + start
            prod[to : to + TILE, :] = gp_ref[at : at + TILE, :] * some
    for n in range(width // NCOL):
        here = slice(n * NCOL, (n + 1) * NCOL)
        acc[:, here] += jnp.dot(hot[...], prod[:, here], preferred_element_type=f32)

    @pl.when(step == pl.num_programs(0) - 1)
    def _():
        core = place_ref[0]
        half = own_ref.shape[1]
        block = lower_ref.shape[0]
        for i, ref in enumerate((lower_ref, centre_ref, upper_ref)):
            ref[...] = acc[i * block : (i + 1) * block, :].astype(bf16)
        own_ref[...] = acc[:, pl.ds(pl.multiple_of(core * half, half), half)].astype(bf16)
        far_ref[...] = acc[:, pl.ds(pl.multiple_of((1 - core) * half, half), half)].astype(bf16)


def backward(
    place, everyone, pred, truth_t, area, var, wout_t, idx_t, sums, agg, grid_embed, gp, nodes
):
    grid_rows, width = agg.shape
    slots = idx_t.shape[0]
    rows = BACK * TILE
    columns = sums[0].shape[1]
    chunks = GROUPS * QUARTERS
    product = (chunks, width // chunks + wout_t.shape[0] // 2, columns // 2)
    anywhere = pl.BlockSpec(memory_space=pl.ANY)
    out_shape = (
        [jax.ShapeDtypeStruct((nodes // 3, width), bf16)] * 3
        + [pltpu.VMEM((nodes, width // 2), bf16)] * 2
        + [pltpu.VMEM(product, bf16)] * 2
    )
    small = (pred, truth_t, area, var, wout_t, idx_t, sums[0])
    return pl.pallas_call(
        functools.partial(backward_kernel, slots),
        grid_spec=prefetched(
            grid_rows // rows,
            [landed()]
            + [whole(x) for x in small]
            + [landed()] * (len(sums) - 1)
            + [anywhere] * 2
            + [pl.BlockSpec((rows * slots, width), lambda t, place: (t, 0))],
            [whole(x) for x in out_shape[:3]] + [landed()] * 4,
            [
                pltpu.VMEM((grid_rows, width), bf16),
                pltpu.VMEM((grid_rows, width), bf16),
                pltpu.VMEM((grid_rows, width), bf16),
                pltpu.VMEM((grid_rows, columns), bf16),
                pltpu.VMEM(wout_t.shape, f32),
                pltpu.SemaphoreType.DMA((2,)),
                pltpu.VMEM((nodes, rows * slots), bf16),
                pltpu.VMEM((rows * slots, width), bf16),
                pltpu.VMEM((nodes, width), f32),
            ],
        ),
        out_shape=out_shape,
        compiler_params=params(),
        cost_estimate=pl.CostEstimate(flops=gp.size * 512, bytes_accessed=2 * gp.size, transcendentals=0),
        name="backward",
    )(place, kept_near(everyone), *small, *map(kept_near, sums[1:]), agg, grid_embed, gp)


def pack_kernel(
    place_ref, below_ref, here_ref, above_ref, edge_ref, own_ref, far_ref, dst_ref, dstfar_ref, total_ref
):
    low = place_ref[0] == 0
    below, here, above, edge = below_ref[...], here_ref[...], above_ref[...], edge_ref[...]
    first = (((0,), (0,)), ((), ()))
    half = own_ref.shape[1]
    mine = jnp.concatenate([below, here, above], axis=0)
    other = jnp.concatenate(
        [jnp.where(low, here, edge), jnp.where(low, above, below), jnp.where(low, edge, here)], axis=0
    )
    product = lax.dot_general(mine, own_ref[...], first, preferred_element_type=f32)
    product = product + lax.dot_general(other, far_ref[...], first, preferred_element_type=f32)
    chunks, rows, columns = total_ref.shape
    total_ref[:, :, :half] = product.astype(bf16).reshape(chunks, rows, half)
    per_zh = dst_ref.shape[0] // GROUPS
    at = pl.ds(pl.program_id(0) * per_zh, per_zh)
    both = dst_ref[at].astype(f32) + dstfar_ref[at].astype(f32)
    few = both.shape[2]
    outs = columns - half - few
    some = both[:, : both.shape[1] - outs].astype(bf16)
    total_ref[:, :, half : half + few] = some.reshape(chunks, rows, few)
    some = jnp.concatenate([both[i, both.shape[1] - outs :] for i in range(both.shape[0])], axis=1)
    total_ref[:, :, half + few :] = some.T.astype(bf16).reshape(chunks, rows, outs)


def pack(place, feats, edge, own, far, dst_own, dst_far, chunks):
    nodes, width = feats[0].shape
    outs = dst_own.shape[1] - width // dst_own.shape[0]
    columns = width // 2 + dst_own.shape[2] + outs
    rows = width // chunks
    feat = pl.BlockSpec((nodes, width // GROUPS), lambda t, place: (0, t))
    return pl.pallas_call(
        pack_kernel,
        grid_spec=prefetched(
            GROUPS,
            [feat] * 4 + [landed()] * 4,
            pl.BlockSpec((chunks, rows // GROUPS, columns), lambda t, place: (0, t, 0)),
            [],
        ),
        out_shape=jax.ShapeDtypeStruct((chunks, rows, columns), bf16),
        compiler_params=params(),
        cost_estimate=pl.CostEstimate(
            flops=4 * width * own.size, bytes_accessed=4 * width * width, transcendentals=0
        ),
        name="pack",
    )(place, *feats, edge, kept_near(own), kept_near(far), kept_near(dst_own), kept_near(dst_far))


def join_kernel(parts_ref, total_ref):
    half = total_ref.shape[2] - parts_ref.shape[2]
    half = half * QUARTERS // (QUARTERS - 1)
    few = half // QUARTERS
    each = parts_ref.shape[0] // QUARTERS
    pieces = []
    ends = 0.0
    for x in range(QUARTERS):
        some = parts_ref[x * each].astype(f32)
        for y in range(1, each):
            some = some + parts_ref[x * each + y].astype(f32)
        pieces.append(some[:, half : half + few])
        ends = ends + some
    total = jnp.concatenate([ends[:, :half]] + pieces + [ends[:, half + few :]], axis=1).astype(bf16)
    for i in range(total_ref.shape[0]):
        rows = total_ref.shape[1]
        total_ref[i] = total[i * rows : (i + 1) * rows, :]


def join(parts, rows_out, half):
    sources, rows, columns = parts.shape
    wide = columns - half // QUARTERS + half
    count = rows // rows_out
    return pl.pallas_call(
        join_kernel,
        grid=(GROUPS,),
        in_specs=[pl.BlockSpec((sources, rows // GROUPS, columns), lambda t: (0, t, 0))],
        out_specs=pl.BlockSpec((count // GROUPS, rows_out, wide), lambda t: (t, 0, 0)),
        out_shape=jax.ShapeDtypeStruct((count, rows_out, wide), bf16),
        compiler_params=params(),
        cost_estimate=pl.CostEstimate(flops=parts.size, bytes_accessed=2 * parts.size, transcendentals=0),
        name="join",
    )(parts)


def body(
    mesh_feats,
    grid_embed,
    w_src,
    w_dst,
    w_out,
    truth,
    area_weight,
    var_weight,
    neighbour,
    edge_mask,
):
    own = mesh_feats[0]
    node_rows, width = own.shape
    grid_rows, slots = neighbour.shape
    half = width // 2
    space_count = lax.axis_size(SPACE)
    block_id = lax.axis_index(SPACE)
    members = lax.axis_size(ENS)
    swap = [(0, 1), (1, 0)]
    here = [lax.axis_index(name) for name in ("c", "x", "zh", "y")]
    place = jnp.stack(here).astype(jnp.int32)

    below = shifted(own, SPACE, 1)
    above = shifted(own, SPACE, -1)

    dst = jnp.dot(grid_embed, w_dst, preferred_element_type=f32).astype(bf16)
    local = jnp.mod(neighbour.T - (block_id - 1) * node_rows, node_rows * space_count)
    idx_t = jnp.where(edge_mask.T > 0, local, -1)
    wout_t = w_out.T
    truth_t = truth.T
    var = var_weight[:, None]
    area = area_weight[None, :]
    dst, idx_t, place, below = lax.optimization_barrier((dst, idx_t, place, below))
    feats = (below, own, above)
    chunks = lax.axis_size(FIRST)
    gp, agg, pred, sent, kept, *pieces = forward(
        place, *feats, w_src, dst, idx_t, wout_t, members
    )
    sums = [kept] + [shifted(piece, "x", d + 1) for d, piece in enumerate(pieces)]
    everyone = lax.all_to_all(sent, ENS, 0, 0, tiled=True)
    low = place[0] == 0
    edge = lax.ppermute(jnp.where(low, below, above), "c", swap)
    everyone, edge = lax.optimization_barrier((everyone, edge))
    lower, centre, upper, wide_own, wide_far, dst_own, dst_far = backward(
        place,
        everyone,
        pred,
        truth_t,
        area,
        var,
        wout_t,
        idx_t,
        sums,
        agg,
        grid_embed,
        gp,
        3 * node_rows,
    )
    dst_far = lax.ppermute(dst_far, "c", swap)
    wide_far = lax.ppermute(wide_far, "c", swap)
    from_above = shifted(lower, SPACE, -1)
    from_below = shifted(upper, SPACE, 1)

    total = pack(place, feats, edge, wide_own, wide_far, dst_own, dst_far, chunks)
    parts = lax.all_to_all(total, FIRST, 0, 0, tiled=True)
    few = half // QUARTERS
    rows_out = width // lax.axis_size(ENS + SPACE)

    total = join(parts, rows_out, half)
    total, from_above, from_below = lax.optimization_barrier((total, from_above, from_below))
    parts = lax.all_to_all(total, SECOND, 0, 0, tiled=True)
    dproj = (centre.astype(f32) + from_above.astype(f32) + from_below.astype(f32)).astype(bf16)
    grad_mesh = lax.dot_general(
        dproj, w_src, (((1,), (1,)), ((), ())), preferred_element_type=f32
    ).astype(bf16)
    total = jnp.sum(parts.reshape(-1, 2, rows_out, parts.shape[2]).astype(f32), axis=0)
    joined = lambda a, b: jnp.concatenate([total[0, :, a:b], total[1, :, a:b]], axis=1)
    dst_final = total[:, :, half : 2 * half].reshape(2, rows_out, QUARTERS, few)
    dst_final = dst_final.transpose(1, 2, 0, 3).reshape(rows_out, width)
    return (
        grad_mesh[None],
        joined(0, half),
        dst_final,
        joined(2 * half, total.shape[-1]),
    )


def solution(mesh):
    fine = Mesh(mesh.devices.reshape(2, 4, 4, 4, 2), ("zh", "x", "y", "zl", "c"))
    everywhere = ENS + SPACE
    in_specs = (
        P(ENS, SPACE, None),
        P(SPACE, None),
        P(),
        P(),
        P(),
        P(SPACE, None),
        P(SPACE),
        P(),
        P(SPACE, None),
        P(SPACE, None),
    )
    out_specs = (
        P(ENS, SPACE, None),
        P(everywhere, None),
        P(everywhere, None),
        P(everywhere, None),
    )
    return jax.shard_map(body, mesh=fine, in_specs=in_specs, out_specs=out_specs, check_vma=False)
```

```python
import functools
import jax
import jax.numpy as jnp
from jax import lax
from jax.experimental import pallas as pl
from jax.experimental.pallas import tpu as pltpu
from jax.sharding import Mesh, PartitionSpec as P

loss_scale = 8.0
smooth_sq = 0.01
TILE = 64
NCOL = 256
ROWS = 32
GROUP = 4
VMEM_LIMIT = 56 * 1024 * 1024
BACK = 2
GROUPS = 2
QUARTERS = 4
f32 = jnp.float32
bf16 = jnp.bfloat16
SPACE = ("y", "zl", "c")
ENS = ("zh", "x")
FIRST = ("x", "y")
SECOND = ("zh", "zl", "c")


def shifted(block, axes, distance):
    count = lax.axis_size(axes)
    return lax.ppermute(block, axes, [(i, (i + distance) % count) for i in range(count)])


def smooth_grad(diff):
    return diff * lax.rsqrt(diff * diff + smooth_sq)


def gelu_parts(v):
    c0 = 0.7978845608
    c1 = c0 * 0.044715
    sq = v * v
    t = jnp.tanh(v * (c0 + c1 * sq))
    u = 1.0 + t
    slope = v * (c0 + (3.0 * c1) * sq)
    return v * u, u * (1.0 + (1.0 - t) * slope)


def whole(array):
    zeros = (0,) * len(array.shape)
    return pl.BlockSpec(array.shape, lambda *_: zeros)


def landed():
    return pl.BlockSpec(memory_space=pltpu.VMEM)


def kept_near(array):
    return pltpu.with_memory_space_constraint(array, pltpu.VMEM)


def params():
    return pltpu.CompilerParams(vmem_limit_bytes=VMEM_LIMIT)


def give(ref, columns, values):
    chunks, rows = ref.shape[0], ref.shape[1] // GROUPS
    for zh in range(GROUPS):
        some = values[zh * chunks * rows : (zh + 1) * chunks * rows, :].astype(ref.dtype)
        ref[:, zh * rows : (zh + 1) * rows, columns] = some.reshape(chunks, rows, some.shape[1])


def scale_column(idx_ref):
    used = jnp.sum(jnp.where(idx_ref[...] >= 0, 1.0, 0.0), axis=0, keepdims=True)
    return jnp.broadcast_to(0.5 / used, (8, used.shape[1])).T[:, :1]


def forward_kernel(
    slots,
    members,
    place_ref,
    below_ref,
    here_ref,
    above_ref,
    wsrc_ref,
    dst_ref,
    idxt_ref,
    wout_ref,
    gp_ref,
    agg_ref,
    pred_ref,
    sent_ref,
    *rest,
):
    piece_refs = rest[:QUARTERS]
    forward_steps(
        slots,
        members,
        place_ref[1],
        (below_ref, here_ref, above_ref),
        wsrc_ref,
        dst_ref,
        idxt_ref,
        wout_ref,
        gp_ref,
        agg_ref,
        pred_ref,
        sent_ref,
        piece_refs,
        *rest[QUARTERS:],
    )


def forward_steps(
    slots,
    members,
    along,
    feat_refs,
    wsrc_ref,
    dst_ref,
    idxt_ref,
    wout_ref,
    gp_ref,
    agg_ref,
    pred_ref,
    sent_ref,
    piece_refs,
    feats,
    rhs,
    hot,
    pre,
    idx_all,
    scale_all,
    sums,
):
    step = pl.program_id(0)
    nodes, width = feats.shape
    depth = rhs.shape[0]
    tile = depth - nodes
    block = feat_refs[0].shape[0]

    @pl.when(step == 0)
    def _():
        idx_all[...] = idxt_ref[...].astype(f32).T.astype(jnp.int32)
        scale_all[...] = scale_column(idxt_ref)
        for i, ref in enumerate(feat_refs):
            feats[i * block : (i + 1) * block, :] = ref[...]
        for n in range(width // NCOL):
            cols = slice(n * NCOL, (n + 1) * NCOL)
            rhs[:nodes, cols] = jnp.dot(
                feats[...], wsrc_ref[:, cols], preferred_element_type=f32
            ).astype(bf16)

    base = pl.multiple_of(step * tile, tile)
    rhs[nodes:, :] = dst_ref[...]
    lane = lax.broadcasted_iota(jnp.int32, (tile, depth), 1)
    row = lax.broadcasted_iota(jnp.int32, (tile, depth), 0)
    eye = lane == row + nodes
    idx = idx_all[pl.ds(base, tile), :]
    for k in range(slots):
        col = idx[:, k : k + 1]
        hit = (lane == col) | (eye & (col >= 0))
        hot[k * tile : (k + 1) * tile, :] = jnp.where(hit, 1.0, 0.0).astype(bf16)
    for n in range(width // NCOL):
        cols = slice(n * NCOL, (n + 1) * NCOL)
        pre[n % 2] = jnp.dot(hot[...], rhs[:, cols], preferred_element_type=f32).astype(bf16)
        for r in range(0, tile, ROWS):
            acc_g = jnp.zeros((ROWS, NCOL), f32)
            acc_s = jnp.zeros((ROWS, NCOL), f32)
            for k in range(slots):
                rows = slice(k * tile + r, k * tile + r + ROWS)
                value, grad = gelu_parts(pre[n % 2, rows, :])
                gp_ref[rows, cols] = grad
                if k % GROUP == 0:
                    some_g, some_s = value, grad
                else:
                    some_g, some_s = some_g + value, some_s + grad
                if k % GROUP == GROUP - 1:
                    acc_g = acc_g + some_g.astype(f32)
                    acc_s = acc_s + some_s.astype(f32)
            scale = scale_all[pl.ds(pl.multiple_of(base + r, ROWS), ROWS), :]
            agg_ref[pl.ds(pl.multiple_of(base + r, ROWS), ROWS), cols] = (acc_g * scale).astype(bf16)
            part = (acc_s - (slots - 0.5 / scale)).astype(bf16)
            few = NCOL // 2
            for j in range(2):
                half, x = divmod(2 * n + j, QUARTERS)
                sums[x, r : r + ROWS, half * few : (half + 1) * few] = part[:, j * few : (j + 1) * few]

    for d, ref in enumerate(piece_refs):
        ref[...] = sums[(along + d) % QUARTERS]

    @pl.when(step == pl.num_programs(0) - 1)
    def _():
        pred = lax.dot_general(
            wout_ref[...], agg_ref[...], (((1,), (1,)), ((), ())), preferred_element_type=f32
        )
        pred_ref[...] = pred
        for e in range(members):
            sent_ref[e] = pred.astype(bf16)


def forward(place, below, here, above, w_src, dst, idx_t, wout_t, members):
    grid_rows, width = dst.shape
    nodes = 3 * here.shape[0]
    slots = idx_t.shape[0]
    outs = wout_t.shape[0]
    step = lambda t, place: (t, 0)
    out_shape = [
        jax.ShapeDtypeStruct((grid_rows * slots, width), bf16),
        jax.ShapeDtypeStruct((grid_rows, width), bf16),
        jax.ShapeDtypeStruct((outs, grid_rows), f32),
        jax.ShapeDtypeStruct((members, outs, grid_rows), bf16),
    ] + [jax.ShapeDtypeStruct((grid_rows, NCOL), bf16)] * QUARTERS
    return pl.pallas_call(
        functools.partial(forward_kernel, slots, members),
        grid_spec=prefetched(
            grid_rows // TILE,
            [landed(), whole(here), landed(), landed()]
            + [pl.BlockSpec((TILE, width), step), whole(idx_t), whole(wout_t)],
            [pl.BlockSpec((TILE * slots, width), step)]
            + [whole(x) for x in out_shape[1:4]]
            + [pl.BlockSpec((TILE, NCOL), step)] * QUARTERS,
            [
                pltpu.VMEM((nodes, width), bf16),
                pltpu.VMEM((nodes + TILE, width), bf16),
                pltpu.VMEM((TILE * slots, nodes + TILE), bf16),
                pltpu.VMEM((2, TILE * slots, NCOL), bf16),
                pltpu.VMEM((grid_rows, slots), jnp.int32),
                pltpu.VMEM((grid_rows, 1), f32),
                pltpu.VMEM((QUARTERS, TILE, NCOL), bf16),
            ],
        ),
        out_shape=out_shape,
        compiler_params=params(),
        cost_estimate=pl.CostEstimate(
            flops=2 * grid_rows * slots * 256 * width,
            bytes_accessed=2 * grid_rows * slots * width,
            transcendentals=grid_rows * slots * width,
        ),
        name="forward",
    )(place, kept_near(below), here, kept_near(above), kept_near(w_src), dst, idx_t, wout_t)


def middle_step(
    place_ref,
    every_ref,
    pred_ref,
    truth_ref,
    area_ref,
    var_ref,
    wout_ref,
    idxt_ref,
    sum_refs,
    agg_hbm,
    grid_hbm,
    lead_ref,
    own_ref,
    far_ref,
    agg_ref,
    grid_ref,
    ddst,
    part_ref,
    sems,
):
    loads = [
        pltpu.make_async_copy(agg_hbm, agg_ref, sems.at[0]),
        pltpu.make_async_copy(grid_hbm, grid_ref, sems.at[1]),
    ]
    for copy in loads:
        copy.start()
    width = wout_ref.shape[1]
    members = every_ref.shape[0]
    near, columns = QUARTERS, sum_refs[0].shape[1]
    core, x, zh = place_ref[0], place_ref[1], place_ref[2]
    weighting = loss_scale * area_ref[...] * var_ref[...]

    def dpred_of(pred):
        pair = -smooth_grad(pred - pred.astype(bf16).astype(f32))
        for e in range(members):
            pair = pair + smooth_grad(pred - every_ref[e].astype(f32))
        against = smooth_grad(pred - truth_ref[...]) / members
        return (weighting * (against - pair / (members * (members - 1)))).astype(bf16)

    scale = scale_column(idxt_ref)
    first = (((0,), (0,)), ((), ()))
    dpred = dpred_of(pred_ref[...])
    for n in range(width // NCOL):
        cols = slice(n * NCOL, (n + 1) * NCOL)
        dagg = lax.dot_general(dpred, wout_ref[:, cols], first, preferred_element_type=f32)
        lead_ref[:, cols] = (dagg * scale).astype(bf16)

    few = columns // 2
    quarter = jnp.concatenate(
        [
            wout_ref[:, pl.ds(pl.multiple_of(x * few + at, few), few)]
            for at in range(0, width, width // 2)
        ],
        axis=1,
    )
    total = jnp.zeros(sum_refs[0].shape, f32)
    for d, sum_ref in enumerate(sum_refs):
        other = dpred_of(every_ref[zh * near + (x + near - d) % near].astype(f32))
        dagg = lax.dot_general(other, quarter, first, preferred_element_type=f32)
        total = total + dagg * sum_ref[...].astype(f32)
    ddst[...] = (total * scale).astype(bf16)

    for copy in loads:
        copy.wait()
    part_ref[...] = jnp.dot(dpred, agg_ref[...], preferred_element_type=f32)
    chunks, rows, few = own_ref.shape
    outs = part_ref.shape[0] // 2
    rows = rows - outs
    for ref, which in ((far_ref, 1 - core), (own_ref, core)):
        product = lax.dot_general(
            grid_ref[...],
            ddst[:, pl.ds(pl.multiple_of(which * few, few), few)],
            first,
            preferred_element_type=f32,
        )
        ref[:, :rows, :] = product.astype(bf16).reshape(chunks, rows, few)
        at = pl.ds(pl.multiple_of(which * outs, outs), outs)
        for chunk in range(chunks):
            ref[chunk, rows:, :] = part_ref[at, chunk * few : (chunk + 1) * few].astype(bf16)


def prefetched(count, ins, outs, scratch):
    return pltpu.PrefetchScalarGridSpec(
        num_scalar_prefetch=1, grid=(count,), in_specs=ins, out_specs=outs, scratch_shapes=scratch
    )


def backward_kernel(
    slots,
    place_ref,
    every_ref,
    pred_ref,
    truth_ref,
    area_ref,
    var_ref,
    wout_ref,
    idxt_ref,
    sum0_ref,
    sum1_ref,
    sum2_ref,
    sum3_ref,
    agg_hbm,
    grid_hbm,
    gp_hbm,
    lower_ref,
    centre_ref,
    upper_ref,
    own_ref,
    far_ref,
    dst_ref,
    dstfar_ref,
    lead,
    agg_ref,
    grid_ref,
    ddst,
    part_ref,
    sems,
    hot,
    prod,
    acc,
    blocks,
    arrived,
):
    step = pl.program_id(0)
    nodes, width = acc.shape
    count, size, _ = blocks.shape

    def block_copy(t):
        rows = pl.ds(pl.multiple_of(t * size, size), size)
        return pltpu.make_async_copy(gp_hbm.at[rows], blocks.at[t], arrived.at[t])

    @pl.when(step == 0)
    def _():
        for t in range(count):
            block_copy(t).start()
        middle_step(
            place_ref,
            every_ref,
            pred_ref,
            truth_ref,
            area_ref,
            var_ref,
            wout_ref,
            idxt_ref,
            (sum0_ref, sum1_ref, sum2_ref, sum3_ref),
            agg_hbm,
            grid_hbm,
            lead,
            dst_ref,
            dstfar_ref,
            agg_ref,
            grid_ref,
            ddst,
            part_ref,
            sems,
        )
        acc[...] = jnp.zeros_like(acc)

    block_copy(step).wait()
    wide = size // slots
    base = pl.multiple_of(step * wide, wide)
    node = lax.broadcasted_iota(jnp.int32, (nodes, wide), 0)
    idx = idxt_ref[:, pl.ds(base, wide)]
    for k in range(slots):
        hot[:, k * wide : (k + 1) * wide] = jnp.where(node == idx[k : k + 1, :], 1.0, 0.0).astype(bf16)
    for start in range(0, wide, TILE):
        some = lead[pl.ds(pl.multiple_of(base + start, TILE), TILE), :]
        for k in range(slots):
            at = start * slots + k * TILE
            to = k * wide + start
            prod[to : to + TILE, :] = blocks[step, at : at + TILE, :] * some
    for n in range(width // NCOL):
        here = slice(n * NCOL, (n + 1) * NCOL)
        acc[:, here] += jnp.dot(hot[...], prod[:, here], preferred_element_type=f32)

    @pl.when(step == pl.num_programs(0) - 1)
    def _():
        core = place_ref[0]
        half = own_ref.shape[1]
        block = lower_ref.shape[0]
        for i, ref in enumerate((lower_ref, centre_ref, upper_ref)):
            ref[...] = acc[i * block : (i + 1) * block, :].astype(bf16)
        own_ref[...] = acc[:, pl.ds(pl.multiple_of(core * half, half), half)].astype(bf16)
        far_ref[...] = acc[:, pl.ds(pl.multiple_of((1 - core) * half, half), half)].astype(bf16)


def backward(
    place, everyone, pred, truth_t, area, var, wout_t, idx_t, sums, agg, grid_embed, gp, nodes
):
    grid_rows, width = agg.shape
    slots = idx_t.shape[0]
    rows = BACK * TILE
    columns = sums[0].shape[1]
    chunks = GROUPS * QUARTERS
    product = (chunks, width // chunks + wout_t.shape[0] // 2, columns // 2)
    anywhere = pl.BlockSpec(memory_space=pl.ANY)
    out_shape = (
        [jax.ShapeDtypeStruct((nodes // 3, width), bf16)] * 3
        + [pltpu.VMEM((nodes, width // 2), bf16)] * 2
        + [pltpu.VMEM(product, bf16)] * 2
    )
    small = (pred, truth_t, area, var, wout_t, idx_t, sums[0])
    return pl.pallas_call(
        functools.partial(backward_kernel, slots),
        grid_spec=prefetched(
            grid_rows // rows,
            [landed()]
            + [whole(x) for x in small]
            + [landed()] * (len(sums) - 1)
            + [anywhere] * 3,
            [whole(x) for x in out_shape[:3]] + [landed()] * 4,
            [
                pltpu.VMEM((grid_rows, width), bf16),
                pltpu.VMEM((grid_rows, width), bf16),
                pltpu.VMEM((grid_rows, width), bf16),
                pltpu.VMEM((grid_rows, columns), bf16),
                pltpu.VMEM(wout_t.shape, f32),
                pltpu.SemaphoreType.DMA((2,)),
                pltpu.VMEM((nodes, rows * slots), bf16),
                pltpu.VMEM((rows * slots, width), bf16),
                pltpu.VMEM((nodes, width), f32),
                pltpu.VMEM((grid_rows // rows, rows * slots, width), bf16),
                pltpu.SemaphoreType.DMA((grid_rows // rows,)),
            ],
        ),
        out_shape=out_shape,
        compiler_params=params(),
        cost_estimate=pl.CostEstimate(flops=gp.size * 512, bytes_accessed=2 * gp.size, transcendentals=0),
        name="backward",
    )(place, kept_near(everyone), *small, *map(kept_near, sums[1:]), agg, grid_embed, gp)


def pack_kernel(
    place_ref, below_ref, here_ref, above_ref, edge_ref, own_ref, far_ref, dst_ref, dstfar_ref, total_ref
):
    low = place_ref[0] == 0
    below, here, above, edge = below_ref[...], here_ref[...], above_ref[...], edge_ref[...]
    first = (((0,), (0,)), ((), ()))
    half = own_ref.shape[1]
    mine = jnp.concatenate([below, here, above], axis=0)
    other = jnp.concatenate(
        [jnp.where(low, here, edge), jnp.where(low, above, below), jnp.where(low, edge, here)], axis=0
    )
    product = lax.dot_general(mine, own_ref[...], first, preferred_element_type=f32)
    product = product + lax.dot_general(other, far_ref[...], first, preferred_element_type=f32)
    chunks, rows, columns = total_ref.shape
    total_ref[:, :, :half] = product.astype(bf16).reshape(chunks, rows, half)
    per_zh = dst_ref.shape[0] // GROUPS
    at = pl.ds(pl.program_id(0) * per_zh, per_zh)
    both = dst_ref[at].astype(f32) + dstfar_ref[at].astype(f32)
    few = both.shape[2]
    outs = columns - half - few
    some = both[:, : both.shape[1] - outs].astype(bf16)
    total_ref[:, :, half : half + few] = some.reshape(chunks, rows, few)
    some = jnp.concatenate([both[i, both.shape[1] - outs :] for i in range(both.shape[0])], axis=1)
    total_ref[:, :, half + few :] = some.T.astype(bf16).reshape(chunks, rows, outs)


def pack(place, feats, edge, own, far, dst_own, dst_far, chunks):
    nodes, width = feats[0].shape
    outs = dst_own.shape[1] - width // dst_own.shape[0]
    columns = width // 2 + dst_own.shape[2] + outs
    rows = width // chunks
    feat = pl.BlockSpec((nodes, width // GROUPS), lambda t, place: (0, t))
    return pl.pallas_call(
        pack_kernel,
        grid_spec=prefetched(
            GROUPS,
            [feat] * 4 + [landed()] * 4,
            pl.BlockSpec((chunks, rows // GROUPS, columns), lambda t, place: (0, t, 0)),
            [],
        ),
        out_shape=jax.ShapeDtypeStruct((chunks, rows, columns), bf16),
        compiler_params=params(),
        cost_estimate=pl.CostEstimate(
            flops=4 * width * own.size, bytes_accessed=4 * width * width, transcendentals=0
        ),
        name="pack",
    )(place, *feats, edge, kept_near(own), kept_near(far), kept_near(dst_own), kept_near(dst_far))


def join_kernel(parts_ref, total_ref):
    half = total_ref.shape[2] - parts_ref.shape[2]
    half = half * QUARTERS // (QUARTERS - 1)
    few = half // QUARTERS
    each = parts_ref.shape[0] // QUARTERS
    pieces = []
    ends = 0.0
    for x in range(QUARTERS):
        some = parts_ref[x * each].astype(f32)
        for y in range(1, each):
            some = some + parts_ref[x * each + y].astype(f32)
        pieces.append(some[:, half : half + few])
        ends = ends + some
    total = jnp.concatenate([ends[:, :half]] + pieces + [ends[:, half + few :]], axis=1).astype(bf16)
    for i in range(total_ref.shape[0]):
        rows = total_ref.shape[1]
        total_ref[i] = total[i * rows : (i + 1) * rows, :]


def join(parts, rows_out, half):
    sources, rows, columns = parts.shape
    wide = columns - half // QUARTERS + half
    count = rows // rows_out
    return pl.pallas_call(
        join_kernel,
        grid=(GROUPS,),
        in_specs=[pl.BlockSpec((sources, rows // GROUPS, columns), lambda t: (0, t, 0))],
        out_specs=pl.BlockSpec((count // GROUPS, rows_out, wide), lambda t: (t, 0, 0)),
        out_shape=jax.ShapeDtypeStruct((count, rows_out, wide), bf16),
        compiler_params=params(),
        cost_estimate=pl.CostEstimate(flops=parts.size, bytes_accessed=2 * parts.size, transcendentals=0),
        name="join",
    )(parts)


def body(
    mesh_feats,
    grid_embed,
    w_src,
    w_dst,
    w_out,
    truth,
    area_weight,
    var_weight,
    neighbour,
    edge_mask,
):
    own = mesh_feats[0]
    node_rows, width = own.shape
    grid_rows, slots = neighbour.shape
    half = width // 2
    space_count = lax.axis_size(SPACE)
    block_id = lax.axis_index(SPACE)
    members = lax.axis_size(ENS)
    swap = [(0, 1), (1, 0)]
    here = [lax.axis_index(name) for name in ("c", "x", "zh", "y")]
    place = jnp.stack(here).astype(jnp.int32)

    below = shifted(own, SPACE, 1)
    above = shifted(own, SPACE, -1)

    dst = jnp.dot(grid_embed, w_dst, preferred_element_type=f32).astype(bf16)
    local = jnp.mod(neighbour.T - (block_id - 1) * node_rows, node_rows * space_count)
    idx_t = jnp.where(edge_mask.T > 0, local, -1)
    wout_t = w_out.T
    truth_t = truth.T
    var = var_weight[:, None]
    area = area_weight[None, :]
    dst, idx_t, place, below = lax.optimization_barrier((dst, idx_t, place, below))
    feats = (below, own, above)
    chunks = lax.axis_size(FIRST)
    gp, agg, pred, sent, kept, *pieces = forward(
        place, *feats, w_src, dst, idx_t, wout_t, members
    )
    sums = [kept] + [shifted(piece, "x", d + 1) for d, piece in enumerate(pieces)]
    everyone = lax.all_to_all(sent, ENS, 0, 0, tiled=True)
    low = place[0] == 0
    edge = lax.ppermute(jnp.where(low, below, above), "c", swap)
    everyone, edge = lax.optimization_barrier((everyone, edge))
    lower, centre, upper, wide_own, wide_far, dst_own, dst_far = backward(
        place,
        everyone,
        pred,
        truth_t,
        area,
        var,
        wout_t,
        idx_t,
        sums,
        agg,
        grid_embed,
        gp,
        3 * node_rows,
    )
    dst_far = lax.ppermute(dst_far, "c", swap)
    wide_far = lax.ppermute(wide_far, "c", swap)
    from_above = shifted(lower, SPACE, -1)
    from_below = shifted(upper, SPACE, 1)

    total = pack(place, feats, edge, wide_own, wide_far, dst_own, dst_far, chunks)
    parts = lax.all_to_all(total, FIRST, 0, 0, tiled=True)
    rows_out = width // lax.axis_size(ENS + SPACE)

    total = join(parts, rows_out, half)
    total, from_above, from_below = lax.optimization_barrier((total, from_above, from_below))
    parts = lax.all_to_all(total, SECOND, 0, 0, tiled=True)
    dproj = (centre.astype(f32) + from_above.astype(f32) + from_below.astype(f32)).astype(bf16)
    grad_mesh = lax.dot_general(
        dproj, w_src, (((1,), (1,)), ((), ())), preferred_element_type=f32
    ).astype(bf16)
    total = jnp.sum(parts.reshape(-1, 2, rows_out, parts.shape[2]).astype(f32), axis=0)
    joined = lambda a, b: jnp.concatenate([total[0, :, a:b], total[1, :, a:b]], axis=1)
    return (
        grad_mesh[None],
        joined(0, half),
        joined(half, 2 * half),
        joined(2 * half, total.shape[-1]),
    )


def solution(mesh):
    fine = Mesh(mesh.devices.reshape(2, 4, 4, 4, 2), ("zh", "x", "y", "zl", "c"))
    everywhere = ENS + SPACE
    in_specs = (
        P(ENS, SPACE, None),
        P(SPACE, None),
        P(),
        P(),
        P(),
        P(SPACE, None),
        P(SPACE),
        P(),
        P(SPACE, None),
        P(SPACE, None),
    )
    out_specs = (
        P(ENS, SPACE, None),
        P(everywhere, None),
        P(everywhere, None),
        P(everywhere, None),
    )
    return jax.shard_map(body, mesh=fine, in_specs=in_specs, out_specs=out_specs, check_vma=False)
```

```python
import functools
import jax
import jax.numpy as jnp
from jax import lax
from jax.experimental import pallas as pl
from jax.experimental.pallas import tpu as pltpu
from jax.sharding import Mesh, PartitionSpec as P

loss_scale = 8.0
smooth_sq = 0.01
TILE = 64
NCOL = 256
ROWS = 32
GROUP = 4
VMEM_LIMIT = 56 * 1024 * 1024
BACK = 2
GROUPS = 2
QUARTERS = 4
f32 = jnp.float32
bf16 = jnp.bfloat16
SPACE = ("y", "zl", "c")
ENS = ("zh", "x")
FIRST = ("x", "y")
SECOND = ("zh", "zl", "c")


def shifted(block, axes, distance):
    count = lax.axis_size(axes)
    return lax.ppermute(block, axes, [(i, (i + distance) % count) for i in range(count)])


def smooth_grad(diff):
    return diff * lax.rsqrt(diff * diff + smooth_sq)


def gelu_parts(v):
    c0 = 0.7978845608
    c1 = c0 * 0.044715
    sq = v * v
    t = jnp.tanh(v * (c0 + c1 * sq))
    u = 1.0 + t
    slope = v * (c0 + (3.0 * c1) * sq)
    return v * u, u * (1.0 + (1.0 - t) * slope)


def whole(array):
    zeros = (0,) * len(array.shape)
    return pl.BlockSpec(array.shape, lambda *_: zeros)


def landed():
    return pl.BlockSpec(memory_space=pltpu.VMEM)


def kept_near(array):
    return pltpu.with_memory_space_constraint(array, pltpu.VMEM)


def params():
    return pltpu.CompilerParams(vmem_limit_bytes=VMEM_LIMIT)


def give(ref, columns, values):
    chunks, rows = ref.shape[0], ref.shape[1] // GROUPS
    for zh in range(GROUPS):
        some = values[zh * chunks * rows : (zh + 1) * chunks * rows, :].astype(ref.dtype)
        ref[:, zh * rows : (zh + 1) * rows, columns] = some.reshape(chunks, rows, some.shape[1])


def scale_column(idx_ref):
    used = jnp.sum(jnp.where(idx_ref[...] >= 0, 1.0, 0.0), axis=0, keepdims=True)
    return jnp.broadcast_to(0.5 / used, (8, used.shape[1])).T[:, :1]


def forward_kernel(
    slots,
    members,
    place_ref,
    below_ref,
    here_ref,
    above_ref,
    wsrc_ref,
    dst_ref,
    idxt_ref,
    wout_ref,
    gp_ref,
    agg_ref,
    pred_ref,
    sent_ref,
    *rest,
):
    piece_refs = rest[:QUARTERS]
    forward_steps(
        slots,
        members,
        place_ref[1],
        (below_ref, here_ref, above_ref),
        wsrc_ref,
        dst_ref,
        idxt_ref,
        wout_ref,
        gp_ref,
        agg_ref,
        pred_ref,
        sent_ref,
        piece_refs,
        *rest[QUARTERS:],
    )


def forward_steps(
    slots,
    members,
    along,
    feat_refs,
    wsrc_ref,
    dst_ref,
    idxt_ref,
    wout_ref,
    gp_ref,
    agg_ref,
    pred_ref,
    sent_ref,
    piece_refs,
    feats,
    rhs,
    hot,
    pre,
    idx_all,
    scale_all,
    sums,
    wsrc,
    sems,
):
    step = pl.program_id(0)
    nodes, width = feats.shape
    depth = rhs.shape[0]
    tile = depth - nodes
    block = feat_refs[0].shape[0]

    @pl.when(step == 0)
    def _():
        parts = [slice(n * NCOL, (n + 1) * NCOL) for n in range(width // NCOL)]
        copies = [
            pltpu.make_async_copy(wsrc_ref.at[:, cols], wsrc.at[:, cols], sems.at[n])
            for n, cols in enumerate(parts)
        ]
        for copy in copies:
            copy.start()
        idx_all[...] = idxt_ref[...].astype(f32).T.astype(jnp.int32)
        scale_all[...] = scale_column(idxt_ref)
        for i, ref in enumerate(feat_refs):
            feats[i * block : (i + 1) * block, :] = ref[...]
        for copy, cols in zip(copies, parts):
            copy.wait()
            rhs[:nodes, cols] = jnp.dot(
                feats[...], wsrc[:, cols], preferred_element_type=f32
            ).astype(bf16)

    base = pl.multiple_of(step * tile, tile)
    rhs[nodes:, :] = dst_ref[...]
    lane = lax.broadcasted_iota(jnp.int32, (tile, depth), 1)
    row = lax.broadcasted_iota(jnp.int32, (tile, depth), 0)
    eye = lane == row + nodes
    idx = idx_all[pl.ds(base, tile), :]
    for k in range(slots):
        col = idx[:, k : k + 1]
        hit = (lane == col) | (eye & (col >= 0))
        hot[k * tile : (k + 1) * tile, :] = jnp.where(hit, 1.0, 0.0).astype(bf16)
    for n in range(width // NCOL):
        cols = slice(n * NCOL, (n + 1) * NCOL)
        pre[n % 2] = jnp.dot(hot[...], rhs[:, cols], preferred_element_type=f32).astype(bf16)
        for r in range(0, tile, ROWS):
            acc_g = jnp.zeros((ROWS, NCOL), f32)
            acc_s = jnp.zeros((ROWS, NCOL), f32)
            for k in range(slots):
                rows = slice(k * tile + r, k * tile + r + ROWS)
                value, grad = gelu_parts(pre[n % 2, rows, :])
                gp_ref[rows, cols] = grad
                if k % GROUP == 0:
                    some_g, some_s = value, grad
                else:
                    some_g, some_s = some_g + value, some_s + grad
                if k % GROUP == GROUP - 1:
                    acc_g = acc_g + some_g.astype(f32)
                    acc_s = acc_s + some_s.astype(f32)
            scale = scale_all[pl.ds(pl.multiple_of(base + r, ROWS), ROWS), :]
            agg_ref[pl.ds(pl.multiple_of(base + r, ROWS), ROWS), cols] = (acc_g * scale).astype(bf16)
            part = (acc_s - (slots - 0.5 / scale)).astype(bf16)
            few = NCOL // 2
            for j in range(2):
                half, x = divmod(2 * n + j, QUARTERS)
                sums[x, r : r + ROWS, half * few : (half + 1) * few] = part[:, j * few : (j + 1) * few]

    for d, ref in enumerate(piece_refs):
        ref[...] = sums[(along + d) % QUARTERS]

    @pl.when(step == pl.num_programs(0) - 1)
    def _():
        pred = lax.dot_general(
            wout_ref[...], agg_ref[...], (((1,), (1,)), ((), ())), preferred_element_type=f32
        )
        pred_ref[...] = pred
        for e in range(members):
            sent_ref[e] = pred.astype(bf16)


def forward(place, below, here, above, w_src, dst, idx_t, wout_t, members):
    grid_rows, width = dst.shape
    nodes = 3 * here.shape[0]
    slots = idx_t.shape[0]
    outs = wout_t.shape[0]
    step = lambda t, place: (t, 0)
    out_shape = [
        jax.ShapeDtypeStruct((grid_rows * slots, width), bf16),
        jax.ShapeDtypeStruct((grid_rows, width), bf16),
        jax.ShapeDtypeStruct((outs, grid_rows), f32),
        jax.ShapeDtypeStruct((members, outs, grid_rows), bf16),
    ] + [jax.ShapeDtypeStruct((grid_rows, NCOL), bf16)] * QUARTERS
    return pl.pallas_call(
        functools.partial(forward_kernel, slots, members),
        grid_spec=prefetched(
            grid_rows // TILE,
            [landed(), whole(here), landed(), pl.BlockSpec(memory_space=pl.ANY)]
            + [pl.BlockSpec((TILE, width), step), whole(idx_t), whole(wout_t)],
            [pl.BlockSpec((TILE * slots, width), step)]
            + [whole(x) for x in out_shape[1:4]]
            + [pl.BlockSpec((TILE, NCOL), step)] * QUARTERS,
            [
                pltpu.VMEM((nodes, width), bf16),
                pltpu.VMEM((nodes + TILE, width), bf16),
                pltpu.VMEM((TILE * slots, nodes + TILE), bf16),
                pltpu.VMEM((2, TILE * slots, NCOL), bf16),
                pltpu.VMEM((grid_rows, slots), jnp.int32),
                pltpu.VMEM((grid_rows, 1), f32),
                pltpu.VMEM((QUARTERS, TILE, NCOL), bf16),
                pltpu.VMEM(w_src.shape, bf16),
                pltpu.SemaphoreType.DMA((width // NCOL,)),
            ],
        ),
        out_shape=out_shape,
        compiler_params=params(),
        cost_estimate=pl.CostEstimate(
            flops=2 * grid_rows * slots * 256 * width,
            bytes_accessed=2 * grid_rows * slots * width,
            transcendentals=grid_rows * slots * width,
        ),
        name="forward",
    )(place, kept_near(below), here, kept_near(above), w_src, dst, idx_t, wout_t)


def middle_step(
    later,
    place_ref,
    every_ref,
    pred_ref,
    truth_ref,
    area_ref,
    var_ref,
    wout_ref,
    idxt_ref,
    sum_refs,
    agg_hbm,
    grid_hbm,
    lead_ref,
    own_ref,
    far_ref,
    agg_ref,
    grid_ref,
    ddst,
    part_ref,
    sems,
):
    loads = [
        pltpu.make_async_copy(agg_hbm, agg_ref, sems.at[0]),
        pltpu.make_async_copy(grid_hbm, grid_ref, sems.at[1]),
    ]
    for copy in loads + later:
        copy.start()
    width = wout_ref.shape[1]
    members = every_ref.shape[0]
    near, columns = QUARTERS, sum_refs[0].shape[1]
    core, x, zh = place_ref[0], place_ref[1], place_ref[2]
    weighting = loss_scale * area_ref[...] * var_ref[...]

    def dpred_of(pred):
        pair = -smooth_grad(pred - pred.astype(bf16).astype(f32))
        for e in range(members):
            pair = pair + smooth_grad(pred - every_ref[e].astype(f32))
        against = smooth_grad(pred - truth_ref[...]) / members
        return (weighting * (against - pair / (members * (members - 1)))).astype(bf16)

    scale = scale_column(idxt_ref)
    first = (((0,), (0,)), ((), ()))
    dpred = dpred_of(pred_ref[...])
    for n in range(width // NCOL):
        cols = slice(n * NCOL, (n + 1) * NCOL)
        dagg = lax.dot_general(dpred, wout_ref[:, cols], first, preferred_element_type=f32)
        lead_ref[:, cols] = (dagg * scale).astype(bf16)

    few = columns // 2
    quarter = jnp.concatenate(
        [
            wout_ref[:, pl.ds(pl.multiple_of(x * few + at, few), few)]
            for at in range(0, width, width // 2)
        ],
        axis=1,
    )
    total = jnp.zeros(sum_refs[0].shape, f32)
    for d, sum_ref in enumerate(sum_refs):
        other = dpred_of(every_ref[zh * near + (x + near - d) % near].astype(f32))
        dagg = lax.dot_general(other, quarter, first, preferred_element_type=f32)
        total = total + dagg * sum_ref[...].astype(f32)
    ddst[...] = (total * scale).astype(bf16)

    for copy in loads:
        copy.wait()
    part_ref[...] = jnp.dot(dpred, agg_ref[...], preferred_element_type=f32)
    chunks, rows, few = own_ref.shape
    outs = part_ref.shape[0] // 2
    rows = rows - outs
    for ref, which in ((far_ref, 1 - core), (own_ref, core)):
        product = lax.dot_general(
            grid_ref[...],
            ddst[:, pl.ds(pl.multiple_of(which * few, few), few)],
            first,
            preferred_element_type=f32,
        )
        ref[:, :rows, :] = product.astype(bf16).reshape(chunks, rows, few)
        at = pl.ds(pl.multiple_of(which * outs, outs), outs)
        for chunk in range(chunks):
            ref[chunk, rows:, :] = part_ref[at, chunk * few : (chunk + 1) * few].astype(bf16)


def prefetched(count, ins, outs, scratch):
    return pltpu.PrefetchScalarGridSpec(
        num_scalar_prefetch=1, grid=(count,), in_specs=ins, out_specs=outs, scratch_shapes=scratch
    )


def backward_kernel(
    slots,
    place_ref,
    every_ref,
    pred_ref,
    truth_ref,
    area_ref,
    var_ref,
    wout_ref,
    idxt_ref,
    sum0_ref,
    sum1_ref,
    sum2_ref,
    sum3_ref,
    agg_hbm,
    grid_hbm,
    gp_hbm,
    lower_ref,
    centre_ref,
    upper_ref,
    own_ref,
    far_ref,
    dst_ref,
    dstfar_ref,
    lead,
    agg_ref,
    grid_ref,
    ddst,
    part_ref,
    sems,
    hot,
    prod,
    acc,
    blocks,
    arrived,
):
    step = pl.program_id(0)
    nodes, width = acc.shape
    count, size, _ = blocks.shape

    def block_copy(t):
        rows = pl.ds(pl.multiple_of(t * size, size), size)
        return pltpu.make_async_copy(gp_hbm.at[rows], blocks.at[t], arrived.at[t])

    @pl.when(step == 0)
    def _():
        middle_step(
            [block_copy(t) for t in range(count)],
            place_ref,
            every_ref,
            pred_ref,
            truth_ref,
            area_ref,
            var_ref,
            wout_ref,
            idxt_ref,
            (sum0_ref, sum1_ref, sum2_ref, sum3_ref),
            agg_hbm,
            grid_hbm,
            lead,
            dst_ref,
            dstfar_ref,
            agg_ref,
            grid_ref,
            ddst,
            part_ref,
            sems,
        )
        acc[...] = jnp.zeros_like(acc)

    block_copy(step).wait()
    wide = size // slots
    base = pl.multiple_of(step * wide, wide)
    node = lax.broadcasted_iota(jnp.int32, (nodes, wide), 0)
    idx = idxt_ref[:, pl.ds(base, wide)]
    for k in range(slots):
        hot[:, k * wide : (k + 1) * wide] = jnp.where(node == idx[k : k + 1, :], 1.0, 0.0).astype(bf16)
    for start in range(0, wide, TILE):
        some = lead[pl.ds(pl.multiple_of(base + start, TILE), TILE), :]
        for k in range(slots):
            at = start * slots + k * TILE
            to = k * wide + start
            prod[to : to + TILE, :] = blocks[step, at : at + TILE, :] * some
    for n in range(width // NCOL):
        here = slice(n * NCOL, (n + 1) * NCOL)
        acc[:, here] += jnp.dot(hot[...], prod[:, here], preferred_element_type=f32)

    @pl.when(step == pl.num_programs(0) - 1)
    def _():
        core = place_ref[0]
        half = own_ref.shape[1]
        block = lower_ref.shape[0]
        for i, ref in enumerate((lower_ref, centre_ref, upper_ref)):
            ref[...] = acc[i * block : (i + 1) * block, :].astype(bf16)
        own_ref[...] = acc[:, pl.ds(pl.multiple_of(core * half, half), half)].astype(bf16)
        far_ref[...] = acc[:, pl.ds(pl.multiple_of((1 - core) * half, half), half)].astype(bf16)


def backward(
    place, everyone, pred, truth_t, area, var, wout_t, idx_t, sums, agg, grid_embed, gp, nodes
):
    grid_rows, width = agg.shape
    slots = idx_t.shape[0]
    rows = BACK * TILE
    columns = sums[0].shape[1]
    chunks = GROUPS * QUARTERS
    product = (chunks, width // chunks + wout_t.shape[0] // 2, columns // 2)
    anywhere = pl.BlockSpec(memory_space=pl.ANY)
    out_shape = (
        [jax.ShapeDtypeStruct((nodes // 3, width), bf16)] * 3
        + [pltpu.VMEM((nodes, width // 2), bf16)] * 2
        + [pltpu.VMEM(product, bf16)] * 2
    )
    small = (pred, truth_t, area, var, wout_t, idx_t, sums[0])
    return pl.pallas_call(
        functools.partial(backward_kernel, slots),
        grid_spec=prefetched(
            grid_rows // rows,
            [landed()]
            + [whole(x) for x in small]
            + [landed()] * (len(sums) - 1)
            + [anywhere] * 3,
            [whole(x) for x in out_shape[:3]] + [landed()] * 4,
            [
                pltpu.VMEM((grid_rows, width), bf16),
                pltpu.VMEM((grid_rows, width), bf16),
                pltpu.VMEM((grid_rows, width), bf16),
                pltpu.VMEM((grid_rows, columns), bf16),
                pltpu.VMEM(wout_t.shape, f32),
                pltpu.SemaphoreType.DMA((2,)),
                pltpu.VMEM((nodes, rows * slots), bf16),
                pltpu.VMEM((rows * slots, width), bf16),
                pltpu.VMEM((nodes, width), f32),
                pltpu.VMEM((grid_rows // rows, rows * slots, width), bf16),
                pltpu.SemaphoreType.DMA((grid_rows // rows,)),
            ],
        ),
        out_shape=out_shape,
        compiler_params=params(),
        cost_estimate=pl.CostEstimate(flops=gp.size * 512, bytes_accessed=2 * gp.size, transcendentals=0),
        name="backward",
    )(place, kept_near(everyone), *small, *map(kept_near, sums[1:]), agg, grid_embed, gp)


def pack_kernel(
    place_ref, below_ref, here_ref, above_ref, edge_ref, own_ref, far_ref, dst_ref, dstfar_ref, total_ref
):
    low = place_ref[0] == 0
    below, here, above, edge = below_ref[...], here_ref[...], above_ref[...], edge_ref[...]
    first = (((0,), (0,)), ((), ()))
    half = own_ref.shape[1]
    mine = jnp.concatenate([below, here, above], axis=0)
    other = jnp.concatenate(
        [jnp.where(low, here, edge), jnp.where(low, above, below), jnp.where(low, edge, here)], axis=0
    )
    product = lax.dot_general(mine, own_ref[...], first, preferred_element_type=f32)
    product = product + lax.dot_general(other, far_ref[...], first, preferred_element_type=f32)
    chunks, rows, columns = total_ref.shape
    total_ref[:, :, :half] = product.astype(bf16).reshape(chunks, rows, half)
    per_zh = dst_ref.shape[0] // GROUPS
    at = pl.ds(pl.program_id(0) * per_zh, per_zh)
    both = dst_ref[at].astype(f32) + dstfar_ref[at].astype(f32)
    few = both.shape[2]
    outs = columns - half - few
    some = both[:, : both.shape[1] - outs].astype(bf16)
    total_ref[:, :, half : half + few] = some.reshape(chunks, rows, few)
    some = jnp.concatenate([both[i, both.shape[1] - outs :] for i in range(both.shape[0])], axis=1)
    total_ref[:, :, half + few :] = some.T.astype(bf16).reshape(chunks, rows, outs)


def pack(place, feats, edge, own, far, dst_own, dst_far, chunks):
    nodes, width = feats[0].shape
    outs = dst_own.shape[1] - width // dst_own.shape[0]
    columns = width // 2 + dst_own.shape[2] + outs
    rows = width // chunks
    feat = pl.BlockSpec((nodes, width // GROUPS), lambda t, place: (0, t))
    return pl.pallas_call(
        pack_kernel,
        grid_spec=prefetched(
            GROUPS,
            [feat] * 4 + [landed()] * 4,
            pl.BlockSpec((chunks, rows // GROUPS, columns), lambda t, place: (0, t, 0)),
            [],
        ),
        out_shape=jax.ShapeDtypeStruct((chunks, rows, columns), bf16),
        compiler_params=params(),
        cost_estimate=pl.CostEstimate(
            flops=4 * width * own.size, bytes_accessed=4 * width * width, transcendentals=0
        ),
        name="pack",
    )(place, *feats, edge, kept_near(own), kept_near(far), kept_near(dst_own), kept_near(dst_far))


def join_kernel(parts_ref, total_ref):
    half = total_ref.shape[2] - parts_ref.shape[2]
    half = half * QUARTERS // (QUARTERS - 1)
    few = half // QUARTERS
    each = parts_ref.shape[0] // QUARTERS
    pieces = []
    ends = 0.0
    for x in range(QUARTERS):
        some = parts_ref[x * each].astype(f32)
        for y in range(1, each):
            some = some + parts_ref[x * each + y].astype(f32)
        pieces.append(some[:, half : half + few])
        ends = ends + some
    total = jnp.concatenate([ends[:, :half]] + pieces + [ends[:, half + few :]], axis=1).astype(bf16)
    for i in range(total_ref.shape[0]):
        rows = total_ref.shape[1]
        total_ref[i] = total[i * rows : (i + 1) * rows, :]


def join(parts, rows_out, half):
    sources, rows, columns = parts.shape
    wide = columns - half // QUARTERS + half
    count = rows // rows_out
    return pl.pallas_call(
        join_kernel,
        grid=(GROUPS,),
        in_specs=[pl.BlockSpec((sources, rows // GROUPS, columns), lambda t: (0, t, 0))],
        out_specs=pl.BlockSpec((count // GROUPS, rows_out, wide), lambda t: (t, 0, 0)),
        out_shape=jax.ShapeDtypeStruct((count, rows_out, wide), bf16),
        compiler_params=params(),
        cost_estimate=pl.CostEstimate(flops=parts.size, bytes_accessed=2 * parts.size, transcendentals=0),
        name="join",
    )(parts)


def body(
    mesh_feats,
    grid_embed,
    w_src,
    w_dst,
    w_out,
    truth,
    area_weight,
    var_weight,
    neighbour,
    edge_mask,
):
    own = mesh_feats[0]
    node_rows, width = own.shape
    grid_rows, slots = neighbour.shape
    half = width // 2
    space_count = lax.axis_size(SPACE)
    block_id = lax.axis_index(SPACE)
    members = lax.axis_size(ENS)
    swap = [(0, 1), (1, 0)]
    here = [lax.axis_index(name) for name in ("c", "x", "zh", "y")]
    place = jnp.stack(here).astype(jnp.int32)

    below = shifted(own, SPACE, 1)
    above = shifted(own, SPACE, -1)

    dst = jnp.dot(grid_embed, w_dst, preferred_element_type=f32).astype(bf16)
    local = jnp.mod(neighbour.T - (block_id - 1) * node_rows, node_rows * space_count)
    idx_t = jnp.where(edge_mask.T > 0, local, -1)
    wout_t = w_out.T
    truth_t = truth.T
    var = var_weight[:, None]
    area = area_weight[None, :]
    dst, idx_t, place, below = lax.optimization_barrier((dst, idx_t, place, below))
    feats = (below, own, above)
    chunks = lax.axis_size(FIRST)
    gp, agg, pred, sent, kept, *pieces = forward(
        place, *feats, w_src, dst, idx_t, wout_t, members
    )
    sums = [kept] + [shifted(piece, "x", d + 1) for d, piece in enumerate(pieces)]
    everyone = lax.all_to_all(sent, ENS, 0, 0, tiled=True)
    low = place[0] == 0
    edge = lax.ppermute(jnp.where(low, below, above), "c", swap)
    everyone, edge = lax.optimization_barrier((everyone, edge))
    lower, centre, upper, wide_own, wide_far, dst_own, dst_far = backward(
        place,
        everyone,
        pred,
        truth_t,
        area,
        var,
        wout_t,
        idx_t,
        sums,
        agg,
        grid_embed,
        gp,
        3 * node_rows,
    )
    dst_far = lax.ppermute(dst_far, "c", swap)
    wide_far = lax.ppermute(wide_far, "c", swap)
    from_above = shifted(lower, SPACE, -1)
    from_below = shifted(upper, SPACE, 1)

    total = pack(place, feats, edge, wide_own, wide_far, dst_own, dst_far, chunks)
    parts = lax.all_to_all(total, FIRST, 0, 0, tiled=True)
    rows_out = width // lax.axis_size(ENS + SPACE)

    total = join(parts, rows_out, half)
    total, from_above, from_below = lax.optimization_barrier((total, from_above, from_below))
    parts = lax.all_to_all(total, SECOND, 0, 0, tiled=True)
    dproj = (centre.astype(f32) + from_above.astype(f32) + from_below.astype(f32)).astype(bf16)
    grad_mesh = lax.dot_general(
        dproj, w_src, (((1,), (1,)), ((), ())), preferred_element_type=f32
    ).astype(bf16)
    total = jnp.sum(parts.reshape(-1, 2, rows_out, parts.shape[2]).astype(f32), axis=0)
    joined = lambda a, b: jnp.concatenate([total[0, :, a:b], total[1, :, a:b]], axis=1)
    return (
        grad_mesh[None],
        joined(0, half),
        joined(half, 2 * half),
        joined(2 * half, total.shape[-1]),
    )


def solution(mesh):
    fine = Mesh(mesh.devices.reshape(2, 4, 4, 4, 2), ("zh", "x", "y", "zl", "c"))
    everywhere = ENS + SPACE
    in_specs = (
        P(ENS, SPACE, None),
        P(SPACE, None),
        P(),
        P(),
        P(),
        P(SPACE, None),
        P(SPACE),
        P(),
        P(SPACE, None),
        P(SPACE, None),
    )
    out_specs = (
        P(ENS, SPACE, None),
        P(everywhere, None),
        P(everywhere, None),
        P(everywhere, None),
    )
    return jax.shard_map(body, mesh=fine, in_specs=in_specs, out_specs=out_specs, check_vma=False)
```

```python
import functools
import jax
import jax.numpy as jnp
from jax import lax
from jax.experimental import pallas as pl
from jax.experimental.pallas import tpu as pltpu
from jax.sharding import Mesh, PartitionSpec as P

loss_scale = 8.0
smooth_sq = 0.01
TILE = 64
NCOL = 256
ROWS = 32
GROUP = 4
VMEM_LIMIT = 56 * 1024 * 1024
BACK = 2
GROUPS = 2
QUARTERS = 4
f32 = jnp.float32
bf16 = jnp.bfloat16
SPACE = ("y", "zl", "c")
ENS = ("zh", "x")
FIRST = ("x", "y")
SECOND = ("zh", "zl", "c")


def shifted(block, axes, distance):
    count = lax.axis_size(axes)
    return lax.ppermute(block, axes, [(i, (i + distance) % count) for i in range(count)])


def smooth_grad(diff):
    return diff * lax.rsqrt(diff * diff + smooth_sq)


def gelu_parts(v):
    c0 = 0.7978845608
    c1 = c0 * 0.044715
    sq = v * v
    t = jnp.tanh(v * (c0 + c1 * sq))
    u = 1.0 + t
    slope = v * (c0 + (3.0 * c1) * sq)
    return v * u, u * (1.0 + (1.0 - t) * slope)


def whole(array):
    zeros = (0,) * len(array.shape)
    return pl.BlockSpec(array.shape, lambda *_: zeros)


def landed():
    return pl.BlockSpec(memory_space=pltpu.VMEM)


def kept_near(array):
    return pltpu.with_memory_space_constraint(array, pltpu.VMEM)


def params():
    return pltpu.CompilerParams(vmem_limit_bytes=VMEM_LIMIT)


def give(ref, columns, values):
    chunks, rows = ref.shape[0], ref.shape[1] // GROUPS
    for zh in range(GROUPS):
        some = values[zh * chunks * rows : (zh + 1) * chunks * rows, :].astype(ref.dtype)
        ref[:, zh * rows : (zh + 1) * rows, columns] = some.reshape(chunks, rows, some.shape[1])


def scale_column(idx_ref):
    used = jnp.sum(jnp.where(idx_ref[...] >= 0, 1.0, 0.0), axis=0, keepdims=True)
    return jnp.broadcast_to(0.5 / used, (8, used.shape[1])).T[:, :1]


def forward_kernel(
    slots,
    members,
    place_ref,
    below_ref,
    here_ref,
    above_ref,
    wsrc_ref,
    dst_ref,
    idxt_ref,
    wout_ref,
    gp_ref,
    agg_ref,
    pred_ref,
    sent_ref,
    *rest,
):
    piece_refs = rest[:QUARTERS]
    forward_steps(
        slots,
        members,
        place_ref[1],
        (below_ref, here_ref, above_ref),
        wsrc_ref,
        dst_ref,
        idxt_ref,
        wout_ref,
        gp_ref,
        agg_ref,
        pred_ref,
        sent_ref,
        piece_refs,
        *rest[QUARTERS:],
    )


def forward_steps(
    slots,
    members,
    along,
    feat_refs,
    wsrc_ref,
    dst_ref,
    idxt_ref,
    wout_ref,
    gp_ref,
    agg_ref,
    pred_ref,
    sent_ref,
    piece_refs,
    feats,
    rhs,
    hot,
    pre,
    idx_all,
    scale_all,
    sums,
):
    step = pl.program_id(0)
    nodes, width = feats.shape
    depth = rhs.shape[0]
    tile = depth - nodes
    block = feat_refs[0].shape[0]

    @pl.when(step == 0)
    def _():
        idx_all[...] = idxt_ref[...].astype(f32).T.astype(bf16)
        scale_all[...] = scale_column(idxt_ref)
        for i, ref in enumerate(feat_refs):
            feats[i * block : (i + 1) * block, :] = ref[...]
        for n in range(width // NCOL):
            cols = slice(n * NCOL, (n + 1) * NCOL)
            rhs[:nodes, cols] = jnp.dot(
                feats[...], wsrc_ref[:, cols], preferred_element_type=f32
            ).astype(bf16)

    base = pl.multiple_of(step * tile, tile)
    rhs[nodes:, :] = dst_ref[...]
    lane = lax.broadcasted_iota(jnp.int32, (tile, depth), 1)
    row = lax.broadcasted_iota(jnp.int32, (tile, depth), 0)
    eye = jnp.where(lane == row + nodes, 1.0, 0.0).astype(bf16)
    lane = lane.astype(f32).astype(bf16)
    idx = idx_all[pl.ds(base, tile), :]
    for k in range(slots):
        col = idx[:, k : k + 1]
        used = eye * jnp.where(col >= 0, 1.0, 0.0).astype(bf16)
        hot[k * tile : (k + 1) * tile, :] = jnp.where(lane == col, jnp.ones_like(used), used)
    for n in range(width // NCOL):
        cols = slice(n * NCOL, (n + 1) * NCOL)
        pre[n % 2] = jnp.dot(hot[...], rhs[:, cols], preferred_element_type=f32).astype(bf16)
        for r in range(0, tile, ROWS):
            acc_g = jnp.zeros((ROWS, NCOL), f32)
            acc_s = jnp.zeros((ROWS, NCOL), f32)
            for k in range(slots):
                rows = slice(k * tile + r, k * tile + r + ROWS)
                value, grad = gelu_parts(pre[n % 2, rows, :])
                gp_ref[rows, cols] = grad
                if k % GROUP == 0:
                    some_g, some_s = value, grad
                else:
                    some_g, some_s = some_g + value, some_s + grad
                if k % GROUP == GROUP - 1:
                    acc_g = acc_g + some_g.astype(f32)
                    acc_s = acc_s + some_s.astype(f32)
            scale = scale_all[pl.ds(pl.multiple_of(base + r, ROWS), ROWS), :]
            agg_ref[pl.ds(pl.multiple_of(base + r, ROWS), ROWS), cols] = (acc_g * scale).astype(bf16)
            part = (acc_s - (slots - 0.5 / scale)).astype(bf16)
            few = NCOL // 2
            for j in range(2):
                half, x = divmod(2 * n + j, QUARTERS)
                sums[x, r : r + ROWS, half * few : (half + 1) * few] = part[:, j * few : (j + 1) * few]

    for d, ref in enumerate(piece_refs):
        ref[...] = sums[(along + d) % QUARTERS]

    @pl.when(step == pl.num_programs(0) - 1)
    def _():
        pred = lax.dot_general(
            wout_ref[...], agg_ref[...], (((1,), (1,)), ((), ())), preferred_element_type=f32
        )
        pred_ref[...] = pred
        for e in range(members):
            sent_ref[e] = pred.astype(bf16)


def forward(place, below, here, above, w_src, dst, idx_t, wout_t, members):
    grid_rows, width = dst.shape
    nodes = 3 * here.shape[0]
    slots = idx_t.shape[0]
    outs = wout_t.shape[0]
    step = lambda t, place: (t, 0)
    out_shape = [
        jax.ShapeDtypeStruct((grid_rows * slots, width), bf16),
        jax.ShapeDtypeStruct((grid_rows, width), bf16),
        jax.ShapeDtypeStruct((outs, grid_rows), f32),
        jax.ShapeDtypeStruct((members, outs, grid_rows), bf16),
    ] + [jax.ShapeDtypeStruct((grid_rows, NCOL), bf16)] * QUARTERS
    return pl.pallas_call(
        functools.partial(forward_kernel, slots, members),
        grid_spec=prefetched(
            grid_rows // TILE,
            [landed(), whole(here), landed(), whole(w_src)]
            + [pl.BlockSpec((TILE, width), step), whole(idx_t), whole(wout_t)],
            [pl.BlockSpec((TILE * slots, width), step)]
            + [whole(x) for x in out_shape[1:4]]
            + [pl.BlockSpec((TILE, NCOL), step)] * QUARTERS,
            [
                pltpu.VMEM((nodes, width), bf16),
                pltpu.VMEM((nodes + TILE, width), bf16),
                pltpu.VMEM((TILE * slots, nodes + TILE), bf16),
                pltpu.VMEM((2, TILE * slots, NCOL), bf16),
                pltpu.VMEM((grid_rows, slots), bf16),
                pltpu.VMEM((grid_rows, 1), f32),
                pltpu.VMEM((QUARTERS, TILE, NCOL), bf16),
            ],
        ),
        out_shape=out_shape,
        compiler_params=params(),
        cost_estimate=pl.CostEstimate(
            flops=2 * grid_rows * slots * 256 * width,
            bytes_accessed=2 * grid_rows * slots * width,
            transcendentals=grid_rows * slots * width,
        ),
        name="forward",
    )(place, kept_near(below), here, kept_near(above), w_src, dst, idx_t, wout_t)


def middle_step(
    later,
    place_ref,
    every_ref,
    pred_ref,
    truth_ref,
    area_ref,
    var_ref,
    wout_ref,
    idxt_ref,
    sum_refs,
    agg_hbm,
    grid_hbm,
    lead_ref,
    own_ref,
    far_ref,
    agg_ref,
    grid_ref,
    ddst,
    part_ref,
    sems,
):
    loads = [
        pltpu.make_async_copy(agg_hbm, agg_ref, sems.at[0]),
        pltpu.make_async_copy(grid_hbm, grid_ref, sems.at[1]),
    ]
    for copy in loads + later:
        copy.start()
    width = wout_ref.shape[1]
    members = every_ref.shape[0]
    near, columns = QUARTERS, sum_refs[0].shape[1]
    core, x, zh = place_ref[0], place_ref[1], place_ref[2]
    weighting = loss_scale * area_ref[...] * var_ref[...]

    def dpred_of(pred):
        pair = -smooth_grad(pred - pred.astype(bf16).astype(f32))
        for e in range(members):
            pair = pair + smooth_grad(pred - every_ref[e].astype(f32))
        against = smooth_grad(pred - truth_ref[...]) / members
        return (weighting * (against - pair / (members * (members - 1)))).astype(bf16)

    scale = scale_column(idxt_ref)
    first = (((0,), (0,)), ((), ()))
    dpred = dpred_of(pred_ref[...])
    for n in range(width // NCOL):
        cols = slice(n * NCOL, (n + 1) * NCOL)
        dagg = lax.dot_general(dpred, wout_ref[:, cols], first, preferred_element_type=f32)
        lead_ref[:, cols] = (dagg * scale).astype(bf16)

    few = columns // 2
    quarter = jnp.concatenate(
        [
            wout_ref[:, pl.ds(pl.multiple_of(x * few + at, few), few)]
            for at in range(0, width, width // 2)
        ],
        axis=1,
    )
    total = jnp.zeros(sum_refs[0].shape, f32)
    for d, sum_ref in enumerate(sum_refs):
        other = dpred_of(every_ref[zh * near + (x + near - d) % near].astype(f32))
        dagg = lax.dot_general(other, quarter, first, preferred_element_type=f32)
        total = total + dagg * sum_ref[...].astype(f32)
    ddst[...] = (total * scale).astype(bf16)

    for copy in loads:
        copy.wait()
    part_ref[...] = jnp.dot(dpred, agg_ref[...], preferred_element_type=f32)
    chunks, rows, few = own_ref.shape
    outs = part_ref.shape[0] // 2
    rows = rows - outs
    for ref, which in ((far_ref, 1 - core), (own_ref, core)):
        product = lax.dot_general(
            grid_ref[...],
            ddst[:, pl.ds(pl.multiple_of(which * few, few), few)],
            first,
            preferred_element_type=f32,
        )
        ref[:, :rows, :] = product.astype(bf16).reshape(chunks, rows, few)
        at = pl.ds(pl.multiple_of(which * outs, outs), outs)
        for chunk in range(chunks):
            ref[chunk, rows:, :] = part_ref[at, chunk * few : (chunk + 1) * few].astype(bf16)


def prefetched(count, ins, outs, scratch):
    return pltpu.PrefetchScalarGridSpec(
        num_scalar_prefetch=1, grid=(count,), in_specs=ins, out_specs=outs, scratch_shapes=scratch
    )


def backward_kernel(
    slots,
    place_ref,
    every_ref,
    pred_ref,
    truth_ref,
    area_ref,
    var_ref,
    wout_ref,
    idxt_ref,
    sum0_ref,
    sum1_ref,
    sum2_ref,
    sum3_ref,
    agg_hbm,
    grid_hbm,
    gp_hbm,
    lower_ref,
    centre_ref,
    upper_ref,
    own_ref,
    far_ref,
    dst_ref,
    dstfar_ref,
    lead,
    agg_ref,
    grid_ref,
    ddst,
    part_ref,
    sems,
    hot,
    prod,
    acc,
    blocks,
    arrived,
):
    step = pl.program_id(0)
    nodes, width = acc.shape
    count, size, _ = blocks.shape

    def block_copy(t):
        rows = pl.ds(pl.multiple_of(t * size, size), size)
        return pltpu.make_async_copy(gp_hbm.at[rows], blocks.at[t], arrived.at[t])

    @pl.when(step == 0)
    def _():
        middle_step(
            [block_copy(t) for t in range(count)],
            place_ref,
            every_ref,
            pred_ref,
            truth_ref,
            area_ref,
            var_ref,
            wout_ref,
            idxt_ref,
            (sum0_ref, sum1_ref, sum2_ref, sum3_ref),
            agg_hbm,
            grid_hbm,
            lead,
            dst_ref,
            dstfar_ref,
            agg_ref,
            grid_ref,
            ddst,
            part_ref,
            sems,
        )
        acc[...] = jnp.zeros_like(acc)

    block_copy(step).wait()
    wide = size // slots
    base = pl.multiple_of(step * wide, wide)
    node = lax.broadcasted_iota(jnp.int32, (nodes, wide), 0)
    idx = idxt_ref[:, pl.ds(base, wide)]
    for k in range(slots):
        hot[:, k * wide : (k + 1) * wide] = jnp.where(node == idx[k : k + 1, :], 1.0, 0.0).astype(bf16)
    for start in range(0, wide, TILE):
        some = lead[pl.ds(pl.multiple_of(base + start, TILE), TILE), :]
        for k in range(slots):
            at = start * slots + k * TILE
            to = k * wide + start
            prod[to : to + TILE, :] = blocks[step, at : at + TILE, :] * some
    for n in range(width // NCOL):
        here = slice(n * NCOL, (n + 1) * NCOL)
        acc[:, here] += jnp.dot(hot[...], prod[:, here], preferred_element_type=f32)

    @pl.when(step == pl.num_programs(0) - 1)
    def _():
        core = place_ref[0]
        half = own_ref.shape[1]
        block = lower_ref.shape[0]
        for i, ref in enumerate((lower_ref, centre_ref, upper_ref)):
            ref[...] = acc[i * block : (i + 1) * block, :].astype(bf16)
        own_ref[...] = acc[:, pl.ds(pl.multiple_of(core * half, half), half)].astype(bf16)
        far_ref[...] = acc[:, pl.ds(pl.multiple_of((1 - core) * half, half), half)].astype(bf16)


def backward(
    place, everyone, pred, truth_t, area, var, wout_t, idx_t, sums, agg, grid_embed, gp, nodes
):
    grid_rows, width = agg.shape
    slots = idx_t.shape[0]
    rows = BACK * TILE
    columns = sums[0].shape[1]
    chunks = GROUPS * QUARTERS
    product = (chunks, width // chunks + wout_t.shape[0] // 2, columns // 2)
    anywhere = pl.BlockSpec(memory_space=pl.ANY)
    out_shape = (
        [jax.ShapeDtypeStruct((nodes // 3, width), bf16)] * 3
        + [pltpu.VMEM((nodes, width // 2), bf16)] * 2
        + [pltpu.VMEM(product, bf16)] * 2
    )
    small = (pred, truth_t, area, var, wout_t, idx_t, sums[0])
    return pl.pallas_call(
        functools.partial(backward_kernel, slots),
        grid_spec=prefetched(
            grid_rows // rows,
            [landed()]
            + [whole(x) for x in small]
            + [landed()] * (len(sums) - 1)
            + [anywhere] * 3,
            [whole(x) for x in out_shape[:3]] + [landed()] * 4,
            [
                pltpu.VMEM((grid_rows, width), bf16),
                pltpu.VMEM((grid_rows, width), bf16),
                pltpu.VMEM((grid_rows, width), bf16),
                pltpu.VMEM((grid_rows, columns), bf16),
                pltpu.VMEM(wout_t.shape, f32),
                pltpu.SemaphoreType.DMA((2,)),
                pltpu.VMEM((nodes, rows * slots), bf16),
                pltpu.VMEM((rows * slots, width), bf16),
                pltpu.VMEM((nodes, width), f32),
                pltpu.VMEM((grid_rows // rows, rows * slots, width), bf16),
                pltpu.SemaphoreType.DMA((grid_rows // rows,)),
            ],
        ),
        out_shape=out_shape,
        compiler_params=params(),
        cost_estimate=pl.CostEstimate(flops=gp.size * 512, bytes_accessed=2 * gp.size, transcendentals=0),
        name="backward",
    )(place, kept_near(everyone), *small, *map(kept_near, sums[1:]), agg, grid_embed, gp)


def pack_kernel(
    place_ref, below_ref, here_ref, above_ref, edge_ref, own_ref, far_ref, dst_ref, dstfar_ref, total_ref
):
    low = place_ref[0] == 0
    below, here, above, edge = below_ref[...], here_ref[...], above_ref[...], edge_ref[...]
    first = (((0,), (0,)), ((), ()))
    half = own_ref.shape[1]
    mine = jnp.concatenate([below, here, above], axis=0)
    other = jnp.concatenate(
        [jnp.where(low, here, edge), jnp.where(low, above, below), jnp.where(low, edge, here)], axis=0
    )
    product = lax.dot_general(mine, own_ref[...], first, preferred_element_type=f32)
    product = product + lax.dot_general(other, far_ref[...], first, preferred_element_type=f32)
    chunks, rows, columns = total_ref.shape
    total_ref[:, :, :half] = product.astype(bf16).reshape(chunks, rows, half)
    per_zh = dst_ref.shape[0] // GROUPS
    at = pl.ds(pl.program_id(0) * per_zh, per_zh)
    both = dst_ref[at].astype(f32) + dstfar_ref[at].astype(f32)
    few = both.shape[2]
    outs = columns - half - few
    some = both[:, : both.shape[1] - outs].astype(bf16)
    total_ref[:, :, half : half + few] = some.reshape(chunks, rows, few)
    some = jnp.concatenate([both[i, both.shape[1] - outs :] for i in range(both.shape[0])], axis=1)
    total_ref[:, :, half + few :] = some.T.astype(bf16).reshape(chunks, rows, outs)


def pack(place, feats, edge, own, far, dst_own, dst_far, chunks):
    nodes, width = feats[0].shape
    outs = dst_own.shape[1] - width // dst_own.shape[0]
    columns = width // 2 + dst_own.shape[2] + outs
    rows = width // chunks
    feat = pl.BlockSpec((nodes, width // GROUPS), lambda t, place: (0, t))
    return pl.pallas_call(
        pack_kernel,
        grid_spec=prefetched(
            GROUPS,
            [feat] * 4 + [landed()] * 4,
            pl.BlockSpec((chunks, rows // GROUPS, columns), lambda t, place: (0, t, 0)),
            [],
        ),
        out_shape=jax.ShapeDtypeStruct((chunks, rows, columns), bf16),
        compiler_params=params(),
        cost_estimate=pl.CostEstimate(
            flops=4 * width * own.size, bytes_accessed=4 * width * width, transcendentals=0
        ),
        name="pack",
    )(place, *feats, edge, kept_near(own), kept_near(far), kept_near(dst_own), kept_near(dst_far))


def join_kernel(parts_ref, total_ref):
    half = total_ref.shape[2] - parts_ref.shape[2]
    half = half * QUARTERS // (QUARTERS - 1)
    few = half // QUARTERS
    each = parts_ref.shape[0] // QUARTERS
    pieces = []
    ends = 0.0
    for x in range(QUARTERS):
        some = parts_ref[x * each].astype(f32)
        for y in range(1, each):
            some = some + parts_ref[x * each + y].astype(f32)
        pieces.append(some[:, half : half + few])
        ends = ends + some
    total = jnp.concatenate([ends[:, :half]] + pieces + [ends[:, half + few :]], axis=1).astype(bf16)
    for i in range(total_ref.shape[0]):
        rows = total_ref.shape[1]
        total_ref[i] = total[i * rows : (i + 1) * rows, :]


def join(parts, rows_out, half):
    sources, rows, columns = parts.shape
    wide = columns - half // QUARTERS + half
    count = rows // rows_out
    return pl.pallas_call(
        join_kernel,
        grid=(GROUPS,),
        in_specs=[pl.BlockSpec((sources, rows // GROUPS, columns), lambda t: (0, t, 0))],
        out_specs=pl.BlockSpec((count // GROUPS, rows_out, wide), lambda t: (t, 0, 0)),
        out_shape=jax.ShapeDtypeStruct((count, rows_out, wide), bf16),
        compiler_params=params(),
        cost_estimate=pl.CostEstimate(flops=parts.size, bytes_accessed=2 * parts.size, transcendentals=0),
        name="join",
    )(parts)


def body(
    mesh_feats,
    grid_embed,
    w_src,
    w_dst,
    w_out,
    truth,
    area_weight,
    var_weight,
    neighbour,
    edge_mask,
):
    own = mesh_feats[0]
    node_rows, width = own.shape
    grid_rows, slots = neighbour.shape
    half = width // 2
    space_count = lax.axis_size(SPACE)
    block_id = lax.axis_index(SPACE)
    members = lax.axis_size(ENS)
    swap = [(0, 1), (1, 0)]
    here = [lax.axis_index(name) for name in ("c", "x", "zh", "y")]
    place = jnp.stack(here).astype(jnp.int32)

    below = shifted(own, SPACE, 1)
    above = shifted(own, SPACE, -1)

    dst = jnp.dot(grid_embed, w_dst, preferred_element_type=f32).astype(bf16)
    local = jnp.mod(neighbour.T - (block_id - 1) * node_rows, node_rows * space_count)
    idx_t = jnp.where(edge_mask.T > 0, local, -1)
    wout_t = w_out.T
    truth_t = truth.T
    var = var_weight[:, None]
    area = area_weight[None, :]
    dst, idx_t, place, below = lax.optimization_barrier((dst, idx_t, place, below))
    feats = (below, own, above)
    chunks = lax.axis_size(FIRST)
    gp, agg, pred, sent, kept, *pieces = forward(
        place, *feats, w_src, dst, idx_t, wout_t, members
    )
    sums = [kept] + [shifted(piece, "x", d + 1) for d, piece in enumerate(pieces)]
    everyone = lax.all_to_all(sent, ENS, 0, 0, tiled=True)
    low = place[0] == 0
    edge = lax.ppermute(jnp.where(low, below, above), "c", swap)
    everyone, edge = lax.optimization_barrier((everyone, edge))
    lower, centre, upper, wide_own, wide_far, dst_own, dst_far = backward(
        place,
        everyone,
        pred,
        truth_t,
        area,
        var,
        wout_t,
        idx_t,
        sums,
        agg,
        grid_embed,
        gp,
        3 * node_rows,
    )
    dst_far = lax.ppermute(dst_far, "c", swap)
    wide_far = lax.ppermute(wide_far, "c", swap)
    from_above = shifted(lower, SPACE, -1)
    from_below = shifted(upper, SPACE, 1)

    total = pack(place, feats, edge, wide_own, wide_far, dst_own, dst_far, chunks)
    parts = lax.all_to_all(total, FIRST, 0, 0, tiled=True)
    rows_out = width // lax.axis_size(ENS + SPACE)

    total = join(parts, rows_out, half)
    total, from_above, from_below = lax.optimization_barrier((total, from_above, from_below))
    parts = lax.all_to_all(total, SECOND, 0, 0, tiled=True)
    dproj = (centre.astype(f32) + from_above.astype(f32) + from_below.astype(f32)).astype(bf16)
    grad_mesh = lax.dot_general(
        dproj, w_src, (((1,), (1,)), ((), ())), preferred_element_type=f32
    ).astype(bf16)
    total = jnp.sum(parts.reshape(-1, 2, rows_out, parts.shape[2]).astype(f32), axis=0)
    joined = lambda a, b: jnp.concatenate([total[0, :, a:b], total[1, :, a:b]], axis=1)
    return (
        grad_mesh[None],
        joined(0, half),
        joined(half, 2 * half),
        joined(2 * half, total.shape[-1]),
    )


def solution(mesh):
    fine = Mesh(mesh.devices.reshape(2, 4, 4, 4, 2), ("zh", "x", "y", "zl", "c"))
    everywhere = ENS + SPACE
    in_specs = (
        P(ENS, SPACE, None),
        P(SPACE, None),
        P(),
        P(),
        P(),
        P(SPACE, None),
        P(SPACE),
        P(),
        P(SPACE, None),
        P(SPACE, None),
    )
    out_specs = (
        P(ENS, SPACE, None),
        P(everywhere, None),
        P(everywhere, None),
        P(everywhere, None),
    )
    return jax.shard_map(body, mesh=fine, in_specs=in_specs, out_specs=out_specs, check_vma=False)
```

```python
import functools
import jax
import jax.numpy as jnp
from jax import lax
from jax.experimental import pallas as pl
from jax.experimental.pallas import tpu as pltpu
from jax.sharding import Mesh, PartitionSpec as P

loss_scale = 8.0
smooth_sq = 0.01
TILE = 64
NCOL = 256
ROWS = 32
GROUP = 4
VMEM_LIMIT = 56 * 1024 * 1024
BACK = 2
GROUPS = 2
QUARTERS = 4
f32 = jnp.float32
bf16 = jnp.bfloat16
SPACE = ("y", "zl", "c")
ENS = ("zh", "x")
FIRST = ("x", "y")
SECOND = ("zh", "zl", "c")


def shifted(block, axes, distance):
    count = lax.axis_size(axes)
    return lax.ppermute(block, axes, [(i, (i + distance) % count) for i in range(count)])


def smooth_grad(diff):
    return diff * lax.rsqrt(diff * diff + smooth_sq)


def gelu_parts(v):
    c0 = 0.7978845608
    c1 = c0 * 0.044715
    sq = v * v
    t = jnp.tanh(v * (c0 + c1 * sq))
    u = 1.0 + t
    slope = v * (c0 + (3.0 * c1) * sq)
    return v * u, u * (1.0 + (1.0 - t) * slope)


def whole(array):
    zeros = (0,) * len(array.shape)
    return pl.BlockSpec(array.shape, lambda *_: zeros)


def landed():
    return pl.BlockSpec(memory_space=pltpu.VMEM)


def kept_near(array):
    return pltpu.with_memory_space_constraint(array, pltpu.VMEM)


def params():
    return pltpu.CompilerParams(vmem_limit_bytes=VMEM_LIMIT)


def give(ref, columns, values):
    chunks, rows = ref.shape[0], ref.shape[1] // GROUPS
    for zh in range(GROUPS):
        some = values[zh * chunks * rows : (zh + 1) * chunks * rows, :].astype(ref.dtype)
        ref[:, zh * rows : (zh + 1) * rows, columns] = some.reshape(chunks, rows, some.shape[1])


def scale_column(idx_ref):
    used = jnp.sum(jnp.where(idx_ref[...] >= 0, 1.0, 0.0), axis=0, keepdims=True)
    return jnp.broadcast_to(0.5 / used, (8, used.shape[1])).T[:, :1]


def forward_kernel(
    slots,
    members,
    place_ref,
    below_ref,
    here_ref,
    above_ref,
    wsrc_ref,
    dst_ref,
    idxt_ref,
    wout_ref,
    gp_ref,
    agg_ref,
    pred_ref,
    sent_ref,
    *rest,
):
    piece_refs = rest[:QUARTERS]
    forward_steps(
        slots,
        members,
        place_ref[1],
        (below_ref, here_ref, above_ref),
        wsrc_ref,
        dst_ref,
        idxt_ref,
        wout_ref,
        gp_ref,
        agg_ref,
        pred_ref,
        sent_ref,
        piece_refs,
        *rest[QUARTERS:],
    )


def forward_steps(
    slots,
    members,
    along,
    feat_refs,
    wsrc_ref,
    dst_ref,
    idxt_ref,
    wout_ref,
    gp_ref,
    agg_ref,
    pred_ref,
    sent_ref,
    piece_refs,
    feats,
    rhs,
    hot,
    pre,
    idx_all,
    scale_all,
    sums,
):
    step = pl.program_id(0)
    nodes, width = feats.shape
    depth = rhs.shape[0]
    tile = depth - nodes
    block = feat_refs[0].shape[0]

    @pl.when(step == 0)
    def _():
        idx_all[...] = idxt_ref[...].astype(f32).T.astype(bf16)
        scale_all[...] = scale_column(idxt_ref)
        for i, ref in enumerate(feat_refs):
            feats[i * block : (i + 1) * block, :] = ref[...]
        for n in range(width // NCOL):
            cols = slice(n * NCOL, (n + 1) * NCOL)
            rhs[:nodes, cols] = jnp.dot(
                feats[...], wsrc_ref[:, cols], preferred_element_type=f32
            ).astype(bf16)

    base = pl.multiple_of(step * tile, tile)
    rhs[nodes:, :] = dst_ref[...]
    lane = lax.broadcasted_iota(jnp.int32, (tile, depth), 1)
    row = lax.broadcasted_iota(jnp.int32, (tile, depth), 0)
    eye = jnp.where(lane == row + nodes, 1.0, 0.0).astype(bf16)
    lane = lane.astype(f32).astype(bf16)
    idx = idx_all[pl.ds(base, tile), :]
    for k in range(slots):
        col = idx[:, k : k + 1]
        used = eye * jnp.where(col >= 0, 1.0, 0.0).astype(bf16)
        hot[k * tile : (k + 1) * tile, :] = jnp.where(lane == col, jnp.ones_like(used), used)
    for n in range(width // NCOL):
        cols = slice(n * NCOL, (n + 1) * NCOL)
        pre[n % 2] = jnp.dot(hot[...], rhs[:, cols], preferred_element_type=f32).astype(bf16)
        for r in range(0, tile, ROWS):
            acc_g = jnp.zeros((ROWS, NCOL), f32)
            acc_s = jnp.zeros((ROWS, NCOL), f32)
            for k in range(slots):
                rows = slice(k * tile + r, k * tile + r + ROWS)
                value, grad = gelu_parts(pre[n % 2, rows, :])
                gp_ref[rows, cols] = grad
                if k % GROUP == 0:
                    some_g, some_s = value, grad
                else:
                    some_g, some_s = some_g + value, some_s + grad
                if k % GROUP == GROUP - 1:
                    acc_g = acc_g + some_g.astype(f32)
                    acc_s = acc_s + some_s.astype(f32)
            scale = scale_all[pl.ds(pl.multiple_of(base + r, ROWS), ROWS), :]
            agg_ref[pl.ds(pl.multiple_of(base + r, ROWS), ROWS), cols] = (acc_g * scale).astype(bf16)
            part = (acc_s - (slots - 0.5 / scale)).astype(bf16)
            few = NCOL // 2
            for j in range(2):
                half, x = divmod(2 * n + j, QUARTERS)
                sums[x, r : r + ROWS, half * few : (half + 1) * few] = part[:, j * few : (j + 1) * few]

    for d, ref in enumerate(piece_refs):
        ref[...] = sums[(along + d) % QUARTERS]

    @pl.when(step == pl.num_programs(0) - 1)
    def _():
        pred = lax.dot_general(
            wout_ref[...], agg_ref[...], (((1,), (1,)), ((), ())), preferred_element_type=f32
        )
        pred_ref[...] = pred
        for e in range(members):
            sent_ref[e] = pred.astype(bf16)


def forward(place, below, here, above, w_src, dst, idx_t, wout_t, members):
    grid_rows, width = dst.shape
    nodes = 3 * here.shape[0]
    slots = idx_t.shape[0]
    outs = wout_t.shape[0]
    step = lambda t, place: (t, 0)
    out_shape = [
        jax.ShapeDtypeStruct((grid_rows * slots, width), bf16),
        jax.ShapeDtypeStruct((grid_rows, width), bf16),
        jax.ShapeDtypeStruct((outs, grid_rows), f32),
        jax.ShapeDtypeStruct((members, outs, grid_rows), bf16),
    ] + [jax.ShapeDtypeStruct((grid_rows, NCOL), bf16)] * QUARTERS
    return pl.pallas_call(
        functools.partial(forward_kernel, slots, members),
        grid_spec=prefetched(
            grid_rows // TILE,
            [landed(), whole(here), landed(), whole(w_src)]
            + [pl.BlockSpec((TILE, width), step), whole(idx_t), whole(wout_t)],
            [pl.BlockSpec((TILE * slots, width), step)]
            + [whole(x) for x in out_shape[1:4]]
            + [pl.BlockSpec((TILE, NCOL), step)] * QUARTERS,
            [
                pltpu.VMEM((nodes, width), bf16),
                pltpu.VMEM((nodes + TILE, width), bf16),
                pltpu.VMEM((TILE * slots, nodes + TILE), bf16),
                pltpu.VMEM((2, TILE * slots, NCOL), bf16),
                pltpu.VMEM((grid_rows, slots), bf16),
                pltpu.VMEM((grid_rows, 1), f32),
                pltpu.VMEM((QUARTERS, TILE, NCOL), bf16),
            ],
        ),
        out_shape=out_shape,
        compiler_params=params(),
        cost_estimate=pl.CostEstimate(
            flops=2 * grid_rows * slots * 256 * width,
            bytes_accessed=2 * grid_rows * slots * width,
            transcendentals=grid_rows * slots * width,
        ),
        name="forward",
    )(place, kept_near(below), here, kept_near(above), w_src, dst, idx_t, wout_t)


def middle_step(
    later,
    place_ref,
    every_ref,
    pred_ref,
    truth_ref,
    area_ref,
    var_ref,
    wout_ref,
    idxt_ref,
    sum_refs,
    agg_hbm,
    grid_hbm,
    lead_ref,
    own_ref,
    far_ref,
    agg_ref,
    grid_ref,
    ddst,
    part_ref,
    sems,
):
    loads = [
        pltpu.make_async_copy(agg_hbm, agg_ref, sems.at[0]),
        pltpu.make_async_copy(grid_hbm, grid_ref, sems.at[1]),
    ]
    for copy in loads + later:
        copy.start()
    width = wout_ref.shape[1]
    members = every_ref.shape[0]
    near, columns = QUARTERS, sum_refs[0].shape[1]
    core, x, zh = place_ref[0], place_ref[1], place_ref[2]
    weighting = loss_scale * area_ref[...] * var_ref[...]

    def dpred_of(pred):
        pair = -smooth_grad(pred - pred.astype(bf16).astype(f32))
        for e in range(members):
            pair = pair + smooth_grad(pred - every_ref[e].astype(f32))
        against = smooth_grad(pred - truth_ref[...]) / members
        return (weighting * (against - pair / (members * (members - 1)))).astype(bf16)

    scale = scale_column(idxt_ref)
    first = (((0,), (0,)), ((), ()))
    dpred = dpred_of(pred_ref[...])
    for n in range(width // NCOL):
        cols = slice(n * NCOL, (n + 1) * NCOL)
        dagg = lax.dot_general(dpred, wout_ref[:, cols], first, preferred_element_type=f32)
        lead_ref[:, cols] = (dagg * scale).astype(bf16)

    few = columns // 2
    quarter = jnp.concatenate(
        [
            wout_ref[:, pl.ds(pl.multiple_of(x * few + at, few), few)]
            for at in range(0, width, width // 2)
        ],
        axis=1,
    )
    total = jnp.zeros(sum_refs[0].shape, f32)
    for d, sum_ref in enumerate(sum_refs):
        other = dpred
        if d > 0:
            other = dpred_of(every_ref[zh * near + (x + near - d) % near].astype(f32))
        dagg = lax.dot_general(other, quarter, first, preferred_element_type=f32)
        total = total + dagg * sum_ref[...].astype(f32)
    ddst[...] = (total * scale).astype(bf16)

    for copy in loads:
        copy.wait()
    part_ref[...] = jnp.dot(dpred, agg_ref[...], preferred_element_type=f32)
    chunks, rows, few = own_ref.shape
    outs = part_ref.shape[0] // 2
    rows = rows - outs
    for ref, which in ((far_ref, 1 - core), (own_ref, core)):
        product = lax.dot_general(
            grid_ref[...],
            ddst[:, pl.ds(pl.multiple_of(which * few, few), few)],
            first,
            preferred_element_type=f32,
        )
        ref[:, :rows, :] = product.astype(bf16).reshape(chunks, rows, few)
        at = pl.ds(pl.multiple_of(which * outs, outs), outs)
        for chunk in range(chunks):
            ref[chunk, rows:, :] = part_ref[at, chunk * few : (chunk + 1) * few].astype(bf16)


def prefetched(count, ins, outs, scratch):
    return pltpu.PrefetchScalarGridSpec(
        num_scalar_prefetch=1, grid=(count,), in_specs=ins, out_specs=outs, scratch_shapes=scratch
    )


def backward_kernel(
    slots,
    place_ref,
    every_ref,
    pred_ref,
    truth_ref,
    area_ref,
    var_ref,
    wout_ref,
    idxt_ref,
    sum0_ref,
    sum1_ref,
    sum2_ref,
    sum3_ref,
    agg_hbm,
    grid_hbm,
    gp_hbm,
    lower_ref,
    centre_ref,
    upper_ref,
    own_ref,
    far_ref,
    dst_ref,
    dstfar_ref,
    lead,
    agg_ref,
    grid_ref,
    ddst,
    part_ref,
    sems,
    hot,
    prod,
    acc,
    blocks,
    arrived,
):
    step = pl.program_id(0)
    nodes, width = acc.shape
    count, size, _ = blocks.shape

    def block_copy(t):
        rows = pl.ds(pl.multiple_of(t * size, size), size)
        return pltpu.make_async_copy(gp_hbm.at[rows], blocks.at[t], arrived.at[t])

    @pl.when(step == 0)
    def _():
        middle_step(
            [block_copy(t) for t in range(count)],
            place_ref,
            every_ref,
            pred_ref,
            truth_ref,
            area_ref,
            var_ref,
            wout_ref,
            idxt_ref,
            (sum0_ref, sum1_ref, sum2_ref, sum3_ref),
            agg_hbm,
            grid_hbm,
            lead,
            dst_ref,
            dstfar_ref,
            agg_ref,
            grid_ref,
            ddst,
            part_ref,
            sems,
        )
        acc[...] = jnp.zeros_like(acc)

    block_copy(step).wait()
    wide = size // slots
    base = pl.multiple_of(step * wide, wide)
    node = lax.broadcasted_iota(jnp.int32, (nodes, wide), 0).astype(f32).astype(bf16)
    idx = idxt_ref[:, pl.ds(base, wide)].astype(f32).astype(bf16)
    one, zero = jnp.ones_like(node), jnp.zeros_like(node)
    for k in range(slots):
        hot[:, k * wide : (k + 1) * wide] = jnp.where(node == idx[k : k + 1, :], one, zero)
    for start in range(0, wide, TILE):
        some = lead[pl.ds(pl.multiple_of(base + start, TILE), TILE), :]
        for k in range(slots):
            at = start * slots + k * TILE
            to = k * wide + start
            prod[to : to + TILE, :] = blocks[step, at : at + TILE, :] * some
    for n in range(width // NCOL):
        here = slice(n * NCOL, (n + 1) * NCOL)
        acc[:, here] += jnp.dot(hot[...], prod[:, here], preferred_element_type=f32)

    @pl.when(step == pl.num_programs(0) - 1)
    def _():
        core = place_ref[0]
        half = own_ref.shape[1]
        block = lower_ref.shape[0]
        for i, ref in enumerate((lower_ref, centre_ref, upper_ref)):
            ref[...] = acc[i * block : (i + 1) * block, :].astype(bf16)
        own_ref[...] = acc[:, pl.ds(pl.multiple_of(core * half, half), half)].astype(bf16)
        far_ref[...] = acc[:, pl.ds(pl.multiple_of((1 - core) * half, half), half)].astype(bf16)


def backward(
    place, everyone, pred, truth_t, area, var, wout_t, idx_t, sums, agg, grid_embed, gp, nodes
):
    grid_rows, width = agg.shape
    slots = idx_t.shape[0]
    rows = BACK * TILE
    columns = sums[0].shape[1]
    chunks = GROUPS * QUARTERS
    product = (chunks, width // chunks + wout_t.shape[0] // 2, columns // 2)
    anywhere = pl.BlockSpec(memory_space=pl.ANY)
    out_shape = (
        [jax.ShapeDtypeStruct((nodes // 3, width), bf16)] * 3
        + [pltpu.VMEM((nodes, width // 2), bf16)] * 2
        + [pltpu.VMEM(product, bf16)] * 2
    )
    small = (pred, truth_t, area, var, wout_t, idx_t, sums[0])
    return pl.pallas_call(
        functools.partial(backward_kernel, slots),
        grid_spec=prefetched(
            grid_rows // rows,
            [landed()]
            + [whole(x) for x in small]
            + [landed()] * (len(sums) - 1)
            + [anywhere] * 3,
            [whole(x) for x in out_shape[:3]] + [landed()] * 4,
            [
                pltpu.VMEM((grid_rows, width), bf16),
                pltpu.VMEM((grid_rows, width), bf16),
                pltpu.VMEM((grid_rows, width), bf16),
                pltpu.VMEM((grid_rows, columns), bf16),
                pltpu.VMEM(wout_t.shape, f32),
                pltpu.SemaphoreType.DMA((2,)),
                pltpu.VMEM((nodes, rows * slots), bf16),
                pltpu.VMEM((rows * slots, width), bf16),
                pltpu.VMEM((nodes, width), f32),
                pltpu.VMEM((grid_rows // rows, rows * slots, width), bf16),
                pltpu.SemaphoreType.DMA((grid_rows // rows,)),
            ],
        ),
        out_shape=out_shape,
        compiler_params=params(),
        cost_estimate=pl.CostEstimate(flops=gp.size * 512, bytes_accessed=2 * gp.size, transcendentals=0),
        name="backward",
    )(place, kept_near(everyone), *small, *map(kept_near, sums[1:]), agg, grid_embed, gp)


def pack_kernel(
    place_ref, below_ref, here_ref, above_ref, edge_ref, own_ref, far_ref, dst_ref, dstfar_ref, total_ref
):
    low = place_ref[0] == 0
    below, here, above, edge = below_ref[...], here_ref[...], above_ref[...], edge_ref[...]
    first = (((0,), (0,)), ((), ()))
    half = own_ref.shape[1]
    mine = jnp.concatenate([below, here, above], axis=0)
    other = jnp.concatenate(
        [jnp.where(low, here, edge), jnp.where(low, above, below), jnp.where(low, edge, here)], axis=0
    )
    product = lax.dot_general(mine, own_ref[...], first, preferred_element_type=f32)
    product = product + lax.dot_general(other, far_ref[...], first, preferred_element_type=f32)
    chunks, rows, columns = total_ref.shape
    total_ref[:, :, :half] = product.astype(bf16).reshape(chunks, rows, half)
    per_zh = dst_ref.shape[0] // GROUPS
    at = pl.ds(pl.program_id(0) * per_zh, per_zh)
    both = dst_ref[at].astype(f32) + dstfar_ref[at].astype(f32)
    few = both.shape[2]
    outs = columns - half - few
    some = both[:, : both.shape[1] - outs].astype(bf16)
    total_ref[:, :, half : half + few] = some.reshape(chunks, rows, few)
    some = jnp.concatenate([both[i, both.shape[1] - outs :] for i in range(both.shape[0])], axis=1)
    total_ref[:, :, half + few :] = some.T.astype(bf16).reshape(chunks, rows, outs)


def pack(place, feats, edge, own, far, dst_own, dst_far, chunks):
    nodes, width = feats[0].shape
    outs = dst_own.shape[1] - width // dst_own.shape[0]
    columns = width // 2 + dst_own.shape[2] + outs
    rows = width // chunks
    feat = pl.BlockSpec((nodes, width // GROUPS), lambda t, place: (0, t))
    return pl.pallas_call(
        pack_kernel,
        grid_spec=prefetched(
            GROUPS,
            [feat] * 4 + [landed()] * 4,
            pl.BlockSpec((chunks, rows // GROUPS, columns), lambda t, place: (0, t, 0)),
            [],
        ),
        out_shape=jax.ShapeDtypeStruct((chunks, rows, columns), bf16),
        compiler_params=params(),
        cost_estimate=pl.CostEstimate(
            flops=4 * width * own.size, bytes_accessed=4 * width * width, transcendentals=0
        ),
        name="pack",
    )(place, *feats, edge, kept_near(own), kept_near(far), kept_near(dst_own), kept_near(dst_far))


def join_kernel(parts_ref, total_ref):
    half = total_ref.shape[2] - parts_ref.shape[2]
    half = half * QUARTERS // (QUARTERS - 1)
    few = half // QUARTERS
    each = parts_ref.shape[0] // QUARTERS
    pieces = []
    ends = 0.0
    for x in range(QUARTERS):
        some = parts_ref[x * each].astype(f32)
        for y in range(1, each):
            some = some + parts_ref[x * each + y].astype(f32)
        pieces.append(some[:, half : half + few])
        ends = ends + some
    total = jnp.concatenate([ends[:, :half]] + pieces + [ends[:, half + few :]], axis=1).astype(bf16)
    for i in range(total_ref.shape[0]):
        rows = total_ref.shape[1]
        total_ref[i] = total[i * rows : (i + 1) * rows, :]


def join(parts, rows_out, half):
    sources, rows, columns = parts.shape
    wide = columns - half // QUARTERS + half
    count = rows // rows_out
    return pl.pallas_call(
        join_kernel,
        grid=(GROUPS,),
        in_specs=[pl.BlockSpec((sources, rows // GROUPS, columns), lambda t: (0, t, 0))],
        out_specs=pl.BlockSpec((count // GROUPS, rows_out, wide), lambda t: (t, 0, 0)),
        out_shape=jax.ShapeDtypeStruct((count, rows_out, wide), bf16),
        compiler_params=params(),
        cost_estimate=pl.CostEstimate(flops=parts.size, bytes_accessed=2 * parts.size, transcendentals=0),
        name="join",
    )(parts)


def body(
    mesh_feats,
    grid_embed,
    w_src,
    w_dst,
    w_out,
    truth,
    area_weight,
    var_weight,
    neighbour,
    edge_mask,
):
    own = mesh_feats[0]
    node_rows, width = own.shape
    grid_rows, slots = neighbour.shape
    half = width // 2
    space_count = lax.axis_size(SPACE)
    block_id = lax.axis_index(SPACE)
    members = lax.axis_size(ENS)
    swap = [(0, 1), (1, 0)]
    here = [lax.axis_index(name) for name in ("c", "x", "zh", "y")]
    place = jnp.stack(here).astype(jnp.int32)

    below = shifted(own, SPACE, 1)
    above = shifted(own, SPACE, -1)

    dst = jnp.dot(grid_embed, w_dst, preferred_element_type=f32).astype(bf16)
    local = jnp.mod(neighbour.T - (block_id - 1) * node_rows, node_rows * space_count)
    idx_t = jnp.where(edge_mask.T > 0, local, -1)
    wout_t = w_out.T
    truth_t = truth.T
    var = var_weight[:, None]
    area = area_weight[None, :]
    dst, idx_t, place, below = lax.optimization_barrier((dst, idx_t, place, below))
    feats = (below, own, above)
    chunks = lax.axis_size(FIRST)
    gp, agg, pred, sent, kept, *pieces = forward(
        place, *feats, w_src, dst, idx_t, wout_t, members
    )
    two = shifted(pieces[1], "x", 2)
    sums = [kept, shifted(pieces[0], "x", 1), two, shifted(pieces[2], "x", 3)]
    everyone = lax.all_to_all(sent, ENS, 0, 0, tiled=True)
    low = place[0] == 0
    edge = lax.ppermute(jnp.where(low, below, above), "c", swap)
    everyone, edge = lax.optimization_barrier((everyone, edge))
    lower, centre, upper, wide_own, wide_far, dst_own, dst_far = backward(
        place,
        everyone,
        pred,
        truth_t,
        area,
        var,
        wout_t,
        idx_t,
        sums,
        agg,
        grid_embed,
        gp,
        3 * node_rows,
    )
    dst_far = lax.ppermute(dst_far, "c", swap)
    wide_far = lax.ppermute(wide_far, "c", swap)
    from_above = shifted(lower, SPACE, -1)
    from_below = shifted(upper, SPACE, 1)

    total = pack(place, feats, edge, wide_own, wide_far, dst_own, dst_far, chunks)
    parts = lax.all_to_all(total, FIRST, 0, 0, tiled=True)
    rows_out = width // lax.axis_size(ENS + SPACE)

    total = join(parts, rows_out, half)
    total, from_above, from_below = lax.optimization_barrier((total, from_above, from_below))
    parts = lax.all_to_all(total, SECOND, 0, 0, tiled=True)
    dproj = (centre.astype(f32) + from_above.astype(f32) + from_below.astype(f32)).astype(bf16)
    grad_mesh = lax.dot_general(
        dproj, w_src, (((1,), (1,)), ((), ())), preferred_element_type=f32
    ).astype(bf16)
    total = jnp.sum(parts.reshape(-1, 2, rows_out, parts.shape[2]).astype(f32), axis=0)
    joined = lambda a, b: jnp.concatenate([total[0, :, a:b], total[1, :, a:b]], axis=1)
    return (
        grad_mesh[None],
        joined(0, half),
        joined(half, 2 * half),
        joined(2 * half, total.shape[-1]),
    )


def solution(mesh):
    fine = Mesh(mesh.devices.reshape(2, 4, 4, 4, 2), ("zh", "x", "y", "zl", "c"))
    everywhere = ENS + SPACE
    in_specs = (
        P(ENS, SPACE, None),
        P(SPACE, None),
        P(),
        P(),
        P(),
        P(SPACE, None),
        P(SPACE),
        P(),
        P(SPACE, None),
        P(SPACE, None),
    )
    out_specs = (
        P(ENS, SPACE, None),
        P(everywhere, None),
        P(everywhere, None),
        P(everywhere, None),
    )
    return jax.shard_map(body, mesh=fine, in_specs=in_specs, out_specs=out_specs, check_vma=False)
```

```python
import functools
import jax
import jax.numpy as jnp
from jax import lax
from jax.experimental import pallas as pl
from jax.experimental.pallas import tpu as pltpu
from jax.sharding import Mesh, PartitionSpec as P

loss_scale = 8.0
smooth_sq = 0.01
TILE = 64
NCOL = 256
ROWS = 32
GROUP = 4
VMEM_LIMIT = 56 * 1024 * 1024
BACK = 2
GROUPS = 2
QUARTERS = 4
JOINS = 4
f32 = jnp.float32
bf16 = jnp.bfloat16
SPACE = ("y", "zl", "c")
ENS = ("zh", "x")
FIRST = ("x", "y")
SECOND = ("zh", "zl", "c")


def shifted(block, axes, distance):
    count = lax.axis_size(axes)
    return lax.ppermute(block, axes, [(i, (i + distance) % count) for i in range(count)])


def smooth_grad(diff):
    return diff * lax.rsqrt(diff * diff + smooth_sq)


def gelu_parts(v):
    c0 = 0.7978845608
    c1 = c0 * 0.044715
    sq = v * v
    t = jnp.tanh(v * (c0 + c1 * sq))
    u = 1.0 + t
    slope = v * (c0 + (3.0 * c1) * sq)
    return v * u, u * (1.0 + (1.0 - t) * slope)


def whole(array):
    zeros = (0,) * len(array.shape)
    return pl.BlockSpec(array.shape, lambda *_: zeros)


def landed():
    return pl.BlockSpec(memory_space=pltpu.VMEM)


def kept_near(array):
    return pltpu.with_memory_space_constraint(array, pltpu.VMEM)


def params():
    return pltpu.CompilerParams(vmem_limit_bytes=VMEM_LIMIT)


def give(ref, columns, values):
    chunks, rows = ref.shape[0], ref.shape[1] // GROUPS
    for zh in range(GROUPS):
        some = values[zh * chunks * rows : (zh + 1) * chunks * rows, :].astype(ref.dtype)
        ref[:, zh * rows : (zh + 1) * rows, columns] = some.reshape(chunks, rows, some.shape[1])


def scale_column(idx_ref):
    used = jnp.sum(jnp.where(idx_ref[...] >= 0, 1.0, 0.0), axis=0, keepdims=True)
    return jnp.broadcast_to(0.5 / used, (8, used.shape[1])).T[:, :1]


def forward_kernel(
    slots,
    members,
    place_ref,
    below_ref,
    here_ref,
    above_ref,
    wsrc_ref,
    dst_ref,
    idxt_ref,
    wout_ref,
    gp_ref,
    agg_ref,
    pred_ref,
    sent_ref,
    *rest,
):
    piece_refs = rest[:QUARTERS]
    forward_steps(
        slots,
        members,
        place_ref[1],
        (below_ref, here_ref, above_ref),
        wsrc_ref,
        dst_ref,
        idxt_ref,
        wout_ref,
        gp_ref,
        agg_ref,
        pred_ref,
        sent_ref,
        piece_refs,
        *rest[QUARTERS:],
    )


def forward_steps(
    slots,
    members,
    along,
    feat_refs,
    wsrc_ref,
    dst_ref,
    idxt_ref,
    wout_ref,
    gp_ref,
    agg_ref,
    pred_ref,
    sent_ref,
    piece_refs,
    feats,
    rhs,
    hot,
    pre,
    idx_all,
    scale_all,
    sums,
):
    step = pl.program_id(0)
    nodes, width = feats.shape
    depth = rhs.shape[0]
    tile = depth - nodes
    block = feat_refs[0].shape[0]

    @pl.when(step == 0)
    def _():
        idx_all[...] = idxt_ref[...].astype(f32).T.astype(bf16)
        scale_all[...] = scale_column(idxt_ref)
        for i, ref in enumerate(feat_refs):
            feats[i * block : (i + 1) * block, :] = ref[...]
        for n in range(width // NCOL):
            cols = slice(n * NCOL, (n + 1) * NCOL)
            rhs[:nodes, cols] = jnp.dot(
                feats[...], wsrc_ref[:, cols], preferred_element_type=f32
            ).astype(bf16)

    base = pl.multiple_of(step * tile, tile)
    rhs[nodes:, :] = dst_ref[...]
    lane = lax.broadcasted_iota(jnp.int32, (tile, depth), 1)
    row = lax.broadcasted_iota(jnp.int32, (tile, depth), 0)
    eye = jnp.where(lane == row + nodes, 1.0, 0.0).astype(bf16)
    lane = lane.astype(f32).astype(bf16)
    idx = idx_all[pl.ds(base, tile), :]
    for k in range(slots):
        col = idx[:, k : k + 1]
        used = eye * jnp.where(col >= 0, 1.0, 0.0).astype(bf16)
        hot[k * tile : (k + 1) * tile, :] = jnp.where(lane == col, jnp.ones_like(used), used)
    for n in range(width // NCOL):
        cols = slice(n * NCOL, (n + 1) * NCOL)
        pre[n % 2] = jnp.dot(hot[...], rhs[:, cols], preferred_element_type=f32).astype(bf16)
        for r in range(0, tile, ROWS):
            acc_g = jnp.zeros((ROWS, NCOL), f32)
            acc_s = jnp.zeros((ROWS, NCOL), f32)
            for k in range(slots):
                rows = slice(k * tile + r, k * tile + r + ROWS)
                value, grad = gelu_parts(pre[n % 2, rows, :])
                gp_ref[rows, cols] = grad
                if k % GROUP == 0:
                    some_g, some_s = value, grad
                else:
                    some_g, some_s = some_g + value, some_s + grad
                if k % GROUP == GROUP - 1:
                    acc_g = acc_g + some_g.astype(f32)
                    acc_s = acc_s + some_s.astype(f32)
            scale = scale_all[pl.ds(pl.multiple_of(base + r, ROWS), ROWS), :]
            agg_ref[pl.ds(pl.multiple_of(base + r, ROWS), ROWS), cols] = (acc_g * scale).astype(bf16)
            part = (acc_s - (slots - 0.5 / scale)).astype(bf16)
            few = NCOL // 2
            for j in range(2):
                half, x = divmod(2 * n + j, QUARTERS)
                sums[x, r : r + ROWS, half * few : (half + 1) * few] = part[:, j * few : (j + 1) * few]

    for d, ref in enumerate(piece_refs):
        ref[...] = sums[(along + d) % QUARTERS]

    @pl.when(step == pl.num_programs(0) - 1)
    def _():
        pred = lax.dot_general(
            wout_ref[...], agg_ref[...], (((1,), (1,)), ((), ())), preferred_element_type=f32
        )
        pred_ref[...] = pred
        for e in range(members):
            sent_ref[e] = pred.astype(bf16)


def forward(place, below, here, above, w_src, dst, idx_t, wout_t, members):
    grid_rows, width = dst.shape
    nodes = 3 * here.shape[0]
    slots = idx_t.shape[0]
    outs = wout_t.shape[0]
    step = lambda t, place: (t, 0)
    out_shape = [
        jax.ShapeDtypeStruct((grid_rows * slots, width), bf16),
        jax.ShapeDtypeStruct((grid_rows, width), bf16),
        jax.ShapeDtypeStruct((outs, grid_rows), f32),
        jax.ShapeDtypeStruct((members, outs, grid_rows), bf16),
    ] + [jax.ShapeDtypeStruct((grid_rows, NCOL), bf16)] * QUARTERS
    return pl.pallas_call(
        functools.partial(forward_kernel, slots, members),
        grid_spec=prefetched(
            grid_rows // TILE,
            [landed(), whole(here), landed(), whole(w_src)]
            + [pl.BlockSpec((TILE, width), step), whole(idx_t), whole(wout_t)],
            [pl.BlockSpec((TILE * slots, width), step)]
            + [whole(x) for x in out_shape[1:4]]
            + [pl.BlockSpec((TILE, NCOL), step)] * QUARTERS,
            [
                pltpu.VMEM((nodes, width), bf16),
                pltpu.VMEM((nodes + TILE, width), bf16),
                pltpu.VMEM((TILE * slots, nodes + TILE), bf16),
                pltpu.VMEM((2, TILE * slots, NCOL), bf16),
                pltpu.VMEM((grid_rows, slots), bf16),
                pltpu.VMEM((grid_rows, 1), f32),
                pltpu.VMEM((QUARTERS, TILE, NCOL), bf16),
            ],
        ),
        out_shape=out_shape,
        compiler_params=params(),
        cost_estimate=pl.CostEstimate(
            flops=2 * grid_rows * slots * 256 * width,
            bytes_accessed=2 * grid_rows * slots * width,
            transcendentals=grid_rows * slots * width,
        ),
        name="forward",
    )(place, kept_near(below), here, kept_near(above), w_src, dst, idx_t, wout_t)


def middle_step(
    later,
    place_ref,
    every_ref,
    pred_ref,
    truth_ref,
    area_ref,
    var_ref,
    wout_ref,
    idxt_ref,
    sum_refs,
    agg_hbm,
    grid_hbm,
    lead_ref,
    own_ref,
    far_ref,
    agg_ref,
    grid_ref,
    ddst,
    part_ref,
    sems,
):
    loads = [
        pltpu.make_async_copy(agg_hbm, agg_ref, sems.at[0]),
        pltpu.make_async_copy(grid_hbm, grid_ref, sems.at[1]),
    ]
    for copy in loads + later:
        copy.start()
    width = wout_ref.shape[1]
    members = every_ref.shape[0]
    near, columns = QUARTERS, sum_refs[0].shape[1]
    core, x, zh = place_ref[0], place_ref[1], place_ref[2]
    weighting = loss_scale * area_ref[...] * var_ref[...]

    def dpred_of(pred):
        pair = -smooth_grad(pred - pred.astype(bf16).astype(f32))
        for e in range(members):
            pair = pair + smooth_grad(pred - every_ref[e].astype(f32))
        against = smooth_grad(pred - truth_ref[...]) / members
        return (weighting * (against - pair / (members * (members - 1)))).astype(bf16)

    scale = scale_column(idxt_ref)
    first = (((0,), (0,)), ((), ()))
    dpred = dpred_of(pred_ref[...])
    for n in range(width // NCOL):
        cols = slice(n * NCOL, (n + 1) * NCOL)
        dagg = lax.dot_general(dpred, wout_ref[:, cols], first, preferred_element_type=f32)
        lead_ref[:, cols] = (dagg * scale).astype(bf16)

    few = columns // 2
    quarter = jnp.concatenate(
        [
            wout_ref[:, pl.ds(pl.multiple_of(x * few + at, few), few)]
            for at in range(0, width, width // 2)
        ],
        axis=1,
    )
    total = jnp.zeros(sum_refs[0].shape, f32)
    for d, sum_ref in enumerate(sum_refs):
        other = dpred
        if d > 0:
            other = dpred_of(every_ref[zh * near + (x + near - d) % near].astype(f32))
        dagg = lax.dot_general(other, quarter, first, preferred_element_type=f32)
        total = total + dagg * sum_ref[...].astype(f32)
    ddst[...] = (total * scale).astype(bf16)

    for copy in loads:
        copy.wait()
    part_ref[...] = jnp.dot(dpred, agg_ref[...], preferred_element_type=f32)
    chunks, rows, few = own_ref.shape
    outs = part_ref.shape[0] // 2
    rows = rows - outs
    for ref, which in ((far_ref, 1 - core), (own_ref, core)):
        product = lax.dot_general(
            grid_ref[...],
            ddst[:, pl.ds(pl.multiple_of(which * few, few), few)],
            first,
            preferred_element_type=f32,
        )
        ref[:, :rows, :] = product.astype(bf16).reshape(chunks, rows, few)
        at = pl.ds(pl.multiple_of(which * outs, outs), outs)
        for chunk in range(chunks):
            ref[chunk, rows:, :] = part_ref[at, chunk * few : (chunk + 1) * few].astype(bf16)


def prefetched(count, ins, outs, scratch):
    return pltpu.PrefetchScalarGridSpec(
        num_scalar_prefetch=1, grid=(count,), in_specs=ins, out_specs=outs, scratch_shapes=scratch
    )


def backward_kernel(
    slots,
    place_ref,
    every_ref,
    pred_ref,
    truth_ref,
    area_ref,
    var_ref,
    wout_ref,
    idxt_ref,
    sum0_ref,
    sum1_ref,
    sum2_ref,
    sum3_ref,
    agg_hbm,
    grid_hbm,
    gp_hbm,
    lower_ref,
    centre_ref,
    upper_ref,
    own_ref,
    far_ref,
    dst_ref,
    dstfar_ref,
    lead,
    agg_ref,
    grid_ref,
    ddst,
    part_ref,
    sems,
    hot,
    prod,
    acc,
    blocks,
    arrived,
):
    step = pl.program_id(0)
    nodes, width = acc.shape
    count, size, _ = blocks.shape

    def block_copy(t):
        rows = pl.ds(pl.multiple_of(t * size, size), size)
        return pltpu.make_async_copy(gp_hbm.at[rows], blocks.at[t], arrived.at[t])

    @pl.when(step == 0)
    def _():
        middle_step(
            [block_copy(t) for t in range(count)],
            place_ref,
            every_ref,
            pred_ref,
            truth_ref,
            area_ref,
            var_ref,
            wout_ref,
            idxt_ref,
            (sum0_ref, sum1_ref, sum2_ref, sum3_ref),
            agg_hbm,
            grid_hbm,
            lead,
            dst_ref,
            dstfar_ref,
            agg_ref,
            grid_ref,
            ddst,
            part_ref,
            sems,
        )
        acc[...] = jnp.zeros_like(acc)

    block_copy(step).wait()
    wide = size // slots
    base = pl.multiple_of(step * wide, wide)
    node = lax.broadcasted_iota(jnp.int32, (nodes, wide), 0)
    idx = idxt_ref[:, pl.ds(base, wide)]
    for k in range(slots):
        hot[:, k * wide : (k + 1) * wide] = jnp.where(node == idx[k : k + 1, :], 1.0, 0.0).astype(bf16)
    for start in range(0, wide, TILE):
        some = lead[pl.ds(pl.multiple_of(base + start, TILE), TILE), :]
        for k in range(slots):
            at = start * slots + k * TILE
            to = k * wide + start
            prod[to : to + TILE, :] = blocks[step, at : at + TILE, :] * some
    for n in range(width // NCOL):
        here = slice(n * NCOL, (n + 1) * NCOL)
        acc[:, here] += jnp.dot(hot[...], prod[:, here], preferred_element_type=f32)

    @pl.when(step == pl.num_programs(0) - 1)
    def _():
        core = place_ref[0]
        half = own_ref.shape[1]
        block = lower_ref.shape[0]
        for i, ref in enumerate((lower_ref, centre_ref, upper_ref)):
            ref[...] = acc[i * block : (i + 1) * block, :].astype(bf16)
        own_ref[...] = acc[:, pl.ds(pl.multiple_of(core * half, half), half)].astype(bf16)
        far_ref[...] = acc[:, pl.ds(pl.multiple_of((1 - core) * half, half), half)].astype(bf16)


def backward(
    place, everyone, pred, truth_t, area, var, wout_t, idx_t, sums, agg, grid_embed, gp, nodes
):
    grid_rows, width = agg.shape
    slots = idx_t.shape[0]
    rows = BACK * TILE
    columns = sums[0].shape[1]
    chunks = GROUPS * QUARTERS
    product = (chunks, width // chunks + wout_t.shape[0] // 2, columns // 2)
    anywhere = pl.BlockSpec(memory_space=pl.ANY)
    out_shape = (
        [jax.ShapeDtypeStruct((nodes // 3, width), bf16)] * 3
        + [pltpu.VMEM((nodes, width // 2), bf16)] * 2
        + [pltpu.VMEM(product, bf16)] * 2
    )
    small = (pred, truth_t, area, var, wout_t, idx_t, sums[0])
    return pl.pallas_call(
        functools.partial(backward_kernel, slots),
        grid_spec=prefetched(
            grid_rows // rows,
            [landed()]
            + [whole(x) for x in small]
            + [landed()] * (len(sums) - 1)
            + [anywhere] * 3,
            [whole(x) for x in out_shape[:3]] + [landed()] * 4,
            [
                pltpu.VMEM((grid_rows, width), bf16),
                pltpu.VMEM((grid_rows, width), bf16),
                pltpu.VMEM((grid_rows, width), bf16),
                pltpu.VMEM((grid_rows, columns), bf16),
                pltpu.VMEM(wout_t.shape, f32),
                pltpu.SemaphoreType.DMA((2,)),
                pltpu.VMEM((nodes, rows * slots), bf16),
                pltpu.VMEM((rows * slots, width), bf16),
                pltpu.VMEM((nodes, width), f32),
                pltpu.VMEM((grid_rows // rows, rows * slots, width), bf16),
                pltpu.SemaphoreType.DMA((grid_rows // rows,)),
            ],
        ),
        out_shape=out_shape,
        compiler_params=params(),
        cost_estimate=pl.CostEstimate(flops=gp.size * 512, bytes_accessed=2 * gp.size, transcendentals=0),
        name="backward",
    )(place, kept_near(everyone), *small, *map(kept_near, sums[1:]), agg, grid_embed, gp)


def pack_kernel(
    place_ref, below_ref, here_ref, above_ref, edge_ref, own_ref, far_ref, dst_ref, dstfar_ref, total_ref
):
    low = place_ref[0] == 0
    below, here, above, edge = below_ref[...], here_ref[...], above_ref[...], edge_ref[...]
    first = (((0,), (0,)), ((), ()))
    half = own_ref.shape[1]
    mine = jnp.concatenate([below, here, above], axis=0)
    other = jnp.concatenate(
        [jnp.where(low, here, edge), jnp.where(low, above, below), jnp.where(low, edge, here)], axis=0
    )
    product = lax.dot_general(mine, own_ref[...], first, preferred_element_type=f32)
    product = product + lax.dot_general(other, far_ref[...], first, preferred_element_type=f32)
    chunks, rows, columns = total_ref.shape
    total_ref[:, :, :half] = product.astype(bf16).reshape(chunks, rows, half)
    per_zh = dst_ref.shape[0] // GROUPS
    at = pl.ds(pl.program_id(0) * per_zh, per_zh)
    both = dst_ref[at].astype(f32) + dstfar_ref[at].astype(f32)
    few = both.shape[2]
    outs = columns - half - few
    some = both[:, : both.shape[1] - outs].astype(bf16)
    total_ref[:, :, half : half + few] = some.reshape(chunks, rows, few)
    some = jnp.concatenate([both[i, both.shape[1] - outs :] for i in range(both.shape[0])], axis=1)
    total_ref[:, :, half + few :] = some.T.astype(bf16).reshape(chunks, rows, outs)


def pack(place, feats, edge, own, far, dst_own, dst_far, chunks):
    nodes, width = feats[0].shape
    outs = dst_own.shape[1] - width // dst_own.shape[0]
    columns = width // 2 + dst_own.shape[2] + outs
    rows = width // chunks
    feat = pl.BlockSpec((nodes, width // GROUPS), lambda t, place: (0, t))
    return pl.pallas_call(
        pack_kernel,
        grid_spec=prefetched(
            GROUPS,
            [feat] * 4 + [landed()] * 4,
            pl.BlockSpec((chunks, rows // GROUPS, columns), lambda t, place: (0, t, 0)),
            [],
        ),
        out_shape=jax.ShapeDtypeStruct((chunks, rows, columns), bf16),
        compiler_params=params(),
        cost_estimate=pl.CostEstimate(
            flops=4 * width * own.size, bytes_accessed=4 * width * width, transcendentals=0
        ),
        name="pack",
    )(place, *feats, edge, kept_near(own), kept_near(far), kept_near(dst_own), kept_near(dst_far))


def join_kernel(parts_ref, total_ref):
    half = total_ref.shape[2] - parts_ref.shape[2]
    half = half * QUARTERS // (QUARTERS - 1)
    few = half // QUARTERS
    each = parts_ref.shape[0] // QUARTERS
    pieces = []
    ends = 0.0
    for x in range(QUARTERS):
        some = parts_ref[x * each].astype(f32)
        for y in range(1, each):
            some = some + parts_ref[x * each + y].astype(f32)
        pieces.append(some[:, half : half + few])
        ends = ends + some
    total = jnp.concatenate([ends[:, :half]] + pieces + [ends[:, half + few :]], axis=1).astype(bf16)
    for i in range(total_ref.shape[0]):
        rows = total_ref.shape[1]
        total_ref[i] = total[i * rows : (i + 1) * rows, :]


def join(parts, rows_out, half):
    sources, rows, columns = parts.shape
    wide = columns - half // QUARTERS + half
    count = rows // rows_out
    return pl.pallas_call(
        join_kernel,
        grid=(JOINS,),
        in_specs=[pl.BlockSpec((sources, rows // JOINS, columns), lambda t: (0, t, 0))],
        out_specs=pl.BlockSpec((count // JOINS, rows_out, wide), lambda t: (t, 0, 0)),
        out_shape=jax.ShapeDtypeStruct((count, rows_out, wide), bf16),
        compiler_params=params(),
        cost_estimate=pl.CostEstimate(flops=parts.size, bytes_accessed=2 * parts.size, transcendentals=0),
        name="join",
    )(parts)


def body(
    mesh_feats,
    grid_embed,
    w_src,
    w_dst,
    w_out,
    truth,
    area_weight,
    var_weight,
    neighbour,
    edge_mask,
):
    own = mesh_feats[0]
    node_rows, width = own.shape
    grid_rows, slots = neighbour.shape
    half = width // 2
    space_count = lax.axis_size(SPACE)
    block_id = lax.axis_index(SPACE)
    members = lax.axis_size(ENS)
    swap = [(0, 1), (1, 0)]
    here = [lax.axis_index(name) for name in ("c", "x", "zh", "y")]
    place = jnp.stack(here).astype(jnp.int32)

    below = shifted(own, SPACE, 1)
    above = shifted(own, SPACE, -1)

    dst = jnp.dot(grid_embed, w_dst, preferred_element_type=f32).astype(bf16)
    local = jnp.mod(neighbour.T - (block_id - 1) * node_rows, node_rows * space_count)
    idx_t = jnp.where(edge_mask.T > 0, local, -1)
    wout_t = w_out.T
    truth_t = truth.T
    var = var_weight[:, None]
    area = area_weight[None, :]
    dst, idx_t, place, below = lax.optimization_barrier((dst, idx_t, place, below))
    feats = (below, own, above)
    chunks = lax.axis_size(FIRST)
    gp, agg, pred, sent, kept, *pieces = forward(
        place, *feats, w_src, dst, idx_t, wout_t, members
    )
    sums = [kept] + [shifted(piece, "x", d + 1) for d, piece in enumerate(pieces)]
    everyone = lax.all_to_all(sent, ENS, 0, 0, tiled=True)
    low = place[0] == 0
    edge = lax.ppermute(jnp.where(low, below, above), "c", swap)
    everyone, edge = lax.optimization_barrier((everyone, edge))
    lower, centre, upper, wide_own, wide_far, dst_own, dst_far = backward(
        place,
        everyone,
        pred,
        truth_t,
        area,
        var,
        wout_t,
        idx_t,
        sums,
        agg,
        grid_embed,
        gp,
        3 * node_rows,
    )
    dst_far = lax.ppermute(dst_far, "c", swap)
    wide_far = lax.ppermute(wide_far, "c", swap)
    from_above = shifted(lower, SPACE, -1)
    from_below = shifted(upper, SPACE, 1)

    total = pack(place, feats, edge, wide_own, wide_far, dst_own, dst_far, chunks)
    parts = lax.all_to_all(total, FIRST, 0, 0, tiled=True)
    rows_out = width // lax.axis_size(ENS + SPACE)

    total = join(parts, rows_out, half)
    total, from_above, from_below = lax.optimization_barrier((total, from_above, from_below))
    parts = lax.all_to_all(total, SECOND, 0, 0, tiled=True)
    dproj = (centre.astype(f32) + from_above.astype(f32) + from_below.astype(f32)).astype(bf16)
    grad_mesh = lax.dot_general(
        dproj, w_src, (((1,), (1,)), ((), ())), preferred_element_type=f32
    ).astype(bf16)
    total = jnp.sum(parts.reshape(-1, 2, rows_out, parts.shape[2]).astype(f32), axis=0)
    joined = lambda a, b: jnp.concatenate([total[0, :, a:b], total[1, :, a:b]], axis=1)
    return (
        grad_mesh[None],
        joined(0, half),
        joined(half, 2 * half),
        joined(2 * half, total.shape[-1]),
    )


def solution(mesh):
    fine = Mesh(mesh.devices.reshape(2, 4, 4, 4, 2), ("zh", "x", "y", "zl", "c"))
    everywhere = ENS + SPACE
    in_specs = (
        P(ENS, SPACE, None),
        P(SPACE, None),
        P(),
        P(),
        P(),
        P(SPACE, None),
        P(SPACE),
        P(),
        P(SPACE, None),
        P(SPACE, None),
    )
    out_specs = (
        P(ENS, SPACE, None),
        P(everywhere, None),
        P(everywhere, None),
        P(everywhere, None),
    )
    return jax.shard_map(body, mesh=fine, in_specs=in_specs, out_specs=out_specs, check_vma=False)
```
